32 devices in a mesh: gx: 8 (over y, x, core), gy: 4 (over z).
Axes of the slice: x: 2, y: 2, z: 4, core: 2. Of those that a mesh axis runs over, the one named last changes fastest.
Arguments:
- field: float32 [256, 256, 128], P('gx', 'gy'), may hold values from -8 to 8
- spacing_x: float32 [256], replicated, may hold values from 0.5 to 2
- spacing_y: float32 [256], replicated, may hold values from 0.5 to 2
Outputs:
- decomposed: float32 [256, 256, 128], P('gx', 'gy')
The draws below stay inside these ranges and needn't reach their ends.
All inputs are finite; a program needn't handle non-finite values.
Results may differ from the reference program's by a relative error of at most 0.00002.
Values sent between devices are 32-bit elements; how exact they have to be, the bound alone decides.
No kernel may reach another device: no remote copies, remote signals or barrier semaphores. Data moves between devices by JAX's collectives and lax.ppermute only.
A program may use at most 64 MiB of HBM per device.

```python
import math
import jax
import jax.numpy as jnp
from jax import lax

Z = 128
SMOOTH_X = 48
SMOOTH_Y = 96
NX = 256
NY = 256


def draw_field(key, part):
    noise = jnp.clip(jax.random.normal(key, (NX, NY, Z), jnp.float32), -5.0, 5.0)
    return noise


def setup_inputs(seed: int = 0) -> dict:
    splits = jax.random.split(jax.random.key(seed), 4)
    field = draw_field(jax.random.fold_in(splits[3], 71), 0)
    spacing_x = jnp.clip(jnp.exp(jax.random.uniform(splits[1], (NX,), jnp.float32, math.log(0.5), math.log(2.0))), 0.5, 2.0)
    spacing_y = jnp.clip(jnp.exp(jax.random.uniform(splits[2], (NY,), jnp.float32, math.log(0.5), math.log(2.0))), 0.5, 2.0)
    return dict(field=field, spacing_x=spacing_x, spacing_y=spacing_y)


def decompose_line(values, spacing, axis_dim, stiffness):
    moved = jnp.moveaxis(values, axis_dim, 0)
    nodes = moved.shape[0]
    rest_shape = moved.shape[1:]
    flat = moved.reshape(nodes, -1)
    even_nodes = flat[0::2]
    odd_nodes = flat[1::2]
    right_nodes = jnp.concatenate([even_nodes[1:], flat[nodes - 2:nodes - 1]], axis=0)
    left_space = spacing[0::2][:, None]
    right_space = spacing[1::2][:, None]
    detail = odd_nodes - (right_space * even_nodes + left_space * right_nodes) / (left_space + right_space)
    zero_row = jnp.zeros_like(detail[:1])
    shifted = jnp.concatenate([zero_row, detail[:-1]], axis=0)
    zero_one = jnp.zeros_like(spacing[:1])
    shifted_space = jnp.concatenate([zero_one, spacing[1::2][:-1]])[:, None]
    load = (shifted_space * shifted + left_space * detail) * 0.5
    coarse = spacing[0::2] + spacing[1::2]
    inverse = 1.0 / coarse
    before = jnp.concatenate([zero_one, coarse[:-1]])
    before_inv = jnp.concatenate([zero_one, inverse[:-1]])
    diagonal = (before + coarse) / 3.0 + stiffness * (before_inv + inverse)
    offdiag = coarse / 6.0 - stiffness * inverse
    upper = jnp.concatenate([offdiag[:-1], zero_one])
    lower = jnp.concatenate([zero_one, offdiag[:-1]])
    correction = lax.linalg.tridiagonal_solve(lower, diagonal, upper, load)
    result = jnp.stack([even_nodes + correction, detail], axis=1).reshape((nodes,) + rest_shape)
    return jnp.moveaxis(result, 0, axis_dim)

def reference(field, spacing_x, spacing_y):
    stiff_x = float(SMOOTH_X) ** 2
    stiff_y = float(SMOOTH_Y) ** 2
    first = decompose_line(field, spacing_x, 0, stiff_x)
    first = first.at[0::2].set(decompose_line(first[0::2], spacing_y, 1, stiff_y))
    coarse_x = spacing_x[0::2] + spacing_x[1::2]
    coarse_y = spacing_y[0::2] + spacing_y[1::2]
    grid = decompose_line(first[0::2, 0::2], coarse_x, 0, stiff_x)
    grid = grid.at[0::2].set(decompose_line(grid[0::2], coarse_y, 1, stiff_y))
    return first.at[0::2, 0::2].set(grid)
```

```python
import functools

import jax
import jax.numpy as jnp
from jax import lax
from jax.experimental import pallas as pl
from jax.experimental.pallas import tpu as pltpu
from jax.sharding import PartitionSpec as P

SMOOTH_X = 48
SMOOTH_Y = 96
F32 = jnp.float32
LANES = 128

GA, GB, GA2, GB2, HW1, HW2, CA0, CA1, KAP, LAM, CB0, CB1, VN, UN, HG = range(15)
SINGLES = 16


def offsets(n):
    n1, n2 = n // 2, n // 4
    names = ["wl", "wr", "al", "be", "u", "v"]
    where, row = {}, SINGLES
    for name in names:
        where[name] = row
        row += n1
    for name in names:
        where[name + "2"] = row
        row += n2
    return where, row


def pick(row, stride, start, width):
    source = lax.broadcasted_iota(jnp.int32, (row.shape[1], width), 0)
    target = lax.broadcasted_iota(jnp.int32, (row.shape[1], width), 1)
    select = jnp.where(source == stride * target + start, 1.0, 0.0).astype(F32)
    return jnp.dot(row, select, precision=lax.Precision.HIGHEST, preferred_element_type=F32)


def combine(left, right):
    a, b, c, d = left
    p, q, r, s = right
    return (a * p + b * r, a * q + b * s, c * p + d * r, c * q + d * s)


def build_table(h, index, n, stiffness, tab):
    nodes = h.shape[1]
    m, m2 = nodes // 2, nodes // 4
    n1, n2 = n // 2, n // 4
    lane = lax.broadcasted_iota(jnp.int32, (1, m), 1)
    even1 = pick(h, 2, 0, m)
    odd1 = pick(h, 2, 1, m)
    coarse = even1 + odd1
    inside = lane < m2
    even2 = jnp.where(inside, pick(coarse, 2, 0, m), 1.0)
    odd2 = jnp.where(inside, pick(coarse, 2, 1, m), 1.0)
    even = jnp.concatenate([even1, even2], axis=0)
    odd = jnp.concatenate([odd1, odd2], axis=0)
    lanes = lax.broadcasted_iota(jnp.int32, (2, m), 1)
    level = lax.broadcasted_iota(jnp.int32, (2, m), 0)
    count = jnp.where(level == 0, m, m2)
    real = lanes < count
    last = lanes == count - 1
    width = even + odd
    inverse = 1.0 / width
    stiff = stiffness * inverse
    across = 1.0 / (stiff - width * (1.0 / 6.0))
    same = jnp.where(real, (width * (1.0 / 3.0) + stiff) * across, 1.0)
    into = jnp.where(real, across, 0.0)
    back = jnp.where(real, (stiffness + width * width * (1.0 / 12.0)) * across, 0.0)
    prefix = (same, into, back, same)
    suffix = (same, into, back, same)
    step = 1
    while step < m:
        def shift(x, by, gone, fill):
            return jnp.where(gone, fill, pltpu.roll(x, by, 1))
        head, tail = lanes < step, lanes >= m - step
        fills = (1.0, 0.0, 0.0, 1.0)
        prefix = combine(prefix, [shift(x, step, head, f) for x, f in zip(prefix, fills)])
        suffix = combine(suffix, [shift(x, m - step, tail, f) for x, f in zip(suffix, fills)])
        step *= 2
    u_next = prefix[0]
    u = jnp.where(lanes == 0, 1.0, pltpu.roll(u_next, 1, 1))
    v = suffix[1]
    v_next = jnp.where(lanes == m - 1, 0.0, pltpu.roll(v, m - 1, 1))
    scale = 0.5 / u_next[:, m - 1 : m]
    alpha = (u * even + u_next * odd) * scale
    beta = (v * even + v_next * odd) * scale
    wl = jnp.where(last, 1.0, odd * inverse)
    wr = jnp.where(last, 0.0, even * inverse)
    both = jnp.concatenate([u[0:1], v[0:1]], axis=0)
    node = pick(both, 2, 0, m)
    between = pick(both, 2, 1, m)
    right = jnp.where(lanes >= m2 - 1, 0.0, pltpu.roll(node, m - 1, 1))
    halo = -wr[1:2] * right
    detail = jnp.where(lanes < m2, between - wl[1:2] * node + halo, 0.0)

    def total(x):
        return jnp.sum(x, axis=1, keepdims=True)

    def below(device, weight, which):
        x, y = weight * detail[which : which + 1], weight * halo[which : which + 1]
        return total(
            jnp.where(lane < device * n2, x, 0.0) - jnp.where(lane == device * n2 - 1, y, 0.0)
        )

    def above(device, weight, which):
        x, y = weight * detail[which : which + 1], weight * halo[which : which + 1]
        first = (device + 1) * n2
        return total(jnp.where(lane >= first, x, 0.0) + jnp.where(lane == first - 1, y, 0.0))

    def at(place, x):
        return total(jnp.where(lane == place, x, 0.0))

    al1, be1, al2, be2 = alpha[0:1], beta[0:1], alpha[1:2], beta[1:2]
    wr1, wr2 = wr[0:1], wr[1:2]
    first1, first2 = index * n1, index * n2
    vn, un = at(first1 + n1, v[0:1]), at(first1 + n1, u[0:1])
    singles = {
        GA: at(first1 - 1, -wr1 * al1),
        GB: at(first1 - 1, -wr1 * be1),
        GA2: at(first2 - 1, -wr2 * al2),
        GB2: at(first2 - 1, -wr2 * be2),
        HW1: at(first1 + n1 - 1, wr1),
        HW2: at(first2 + n2 - 1, wr2),
        CA0: below(index, al2, 1),
        CA1: below(index + 1, al2, 1),
        KAP: below(index, al2, 0),
        LAM: above(index, be2, 1),
        CB0: below(index, be2, 0),
        CB1: below(index + 1, be2, 0),
        VN: vn,
        UN: un,
        HG: 1.0
        - vn * at(first1 + n1 - 1, wr1 * al1)
        + un * at(first1 + n1 - 1, wr1 * be1),
    }
    for row, value in singles.items():
        tab[row : row + 1, :] = jnp.broadcast_to(value, (1, LANES))
    where, _ = offsets(n)
    for lv, rows, suffix_name in ((0, n1, ""), (1, n2, "2")):
        col = lax.broadcasted_iota(jnp.int32, (rows, m), 1)
        sub = lax.broadcasted_iota(jnp.int32, (rows, m), 0)
        mine = col == index * rows + sub
        mine_inner = mine & (sub < rows - 1)
        for name, x, mask in (
            ("wl", wl, mine),
            ("wr", wr, mine_inner),
            ("al", alpha, mine),
            ("be", beta, mine),
            ("u", u, mine),
            ("v", v, mine),
        ):
            values = total(jnp.where(mask, x[lv : lv + 1], 0.0))
            start = where[name + suffix_name]
            tab[start : start + rows, :] = jnp.broadcast_to(values, (rows, LANES))


def one_level(even, odd, tab, where, suffix, ga, gb, from_left, from_right):
    def c(name, i):
        row = where[name + suffix] + i
        return tab[row : row + 1, :]

    count = len(even)
    details = []
    for i in range(count):
        e = odd[i] - c("wl", i) * even[i]
        if i + 1 < count:
            e = e - c("wr", i) * even[i + 1]
        details.append(e)
    first = tab[ga : ga + 1, :] * even[0]
    acc = first if from_left is None else from_left + first
    lefts = []
    for i in range(count):
        lefts.append(acc)
        acc = acc + c("al", i) * details[i]
    left_end = acc
    acc = from_right
    rights = [None] * count
    for i in reversed(range(count)):
        term = c("be", i) * details[i]
        acc = term if acc is None else acc + term
        rights[i] = acc
    nodes = [even[i] + c("v", i) * lefts[i] + c("u", i) * rights[i] for i in range(count)]
    right_end = rights[0] + tab[gb : gb + 1, :] * even[0]
    return details, nodes, left_end, right_end


def single(tab, row):
    return tab[row : row + 1, :]


def summaries(tab, p1, q1, p2, q2):
    to_right = p2 + single(tab, KAP) * q1 - single(tab, CA1) * p1
    to_left = q2 + single(tab, LAM) * p1 + single(tab, CB0) * q1
    return to_right, to_left


def second_sums(tab, left, right, left2, right2, p1, q1):
    left_second = left2 + single(tab, CA0) * left + single(tab, KAP) * (q1 + right)
    right_second = right2 - single(tab, CB1) * right + single(tab, LAM) * (left + p1)
    return left_second, right_second


class Exchange:
    def __init__(self, axis, count):
        self.axis, self.count = axis, count
        self.xor = count & (count - 1) == 0
        self.steps = list(range(1, count))

    def target(self, i, step):
        return i ^ step if self.xor else (i + step) % self.count

    def source(self, i, step):
        return i ^ step if self.xor else (i + self.count - step) % self.count

    def near(self, step):
        return any(self.target(i, step) == i - 1 for i in range(1, self.count))

    def send(self, step, x):
        pairs = [(i, self.target(i, step)) for i in range(self.count)]
        return lax.ppermute(x, self.axis, pairs)


def x_tile(tab, where, field, n, cols, sums):
    even = [field[2 * i, cols, :] for i in range(n // 2)]
    odd = [field[2 * i + 1, cols, :] for i in range(n // 2)]
    left, right = sums if sums else (None, None)
    return one_level(even, odd, tab, where, "", GA, GB, left, right)


def first_kernel(ex, n, ny, stiffness, ct, h_ref, field, tab, *messages):
    index = lax.axis_index(ex.axis)
    build_table(h_ref[...], index, n, stiffness, tab)
    where, _ = offsets(n)

    def body(t, carry):
        begin = pl.multiple_of(t * ct, ct)
        cols = pl.ds(begin, ct)
        _, nodes, p1, q1 = x_tile(tab, where, field, n, cols, None)
        _, _, p2, q2 = one_level(nodes[0::2], nodes[1::2], tab, where, "2", GA2, GB2, None, None)
        p2, q2 = summaries(tab, p1, q1, p2, q2)
        for step, message in zip(ex.steps, messages):
            upward = ex.target(index, step) > index
            message[cols, :] = jnp.where(upward, p1, q1)
            message[pl.ds(begin + ny, ct), :] = jnp.where(upward, p2, q2)
            if ex.near(step):
                message[pl.ds(begin + 2 * ny, ct), :] = field[0, cols, :]
        return carry

    lax.fori_loop(0, ny // ct, body, 0)


def second_kernel(exx, exy, n, ny, ct, *refs):
    field, xtab, ytab = refs[:3]
    incoming = refs[3 : 3 + len(exx.steps)]
    rest = refs[3 + len(exx.steps) :]
    out, own = rest[0], rest[1]
    messages = rest[2 : 2 + len(exy.steps)]
    full, mixed = rest[2 + len(exy.steps) :]
    index = lax.axis_index(exx.axis)
    n1, n2 = n // 2, n // 4
    where, _ = offsets(n)

    def body(t, carry):
        begin = pl.multiple_of(t * ct, ct)
        cols = pl.ds(begin, ct)
        zero = jnp.zeros((ct, LANES), F32)
        left = right = left2 = right2 = halo = zero
        for step, message in zip(exx.steps, incoming):
            source = exx.source(index, step)
            lower = source < index
            one = message[cols, :]
            two = message[pl.ds(begin + ny, ct), :]
            left = left + jnp.where(lower, one, 0.0)
            right = right + jnp.where(lower, 0.0, one)
            left2 = left2 + jnp.where(lower, two, 0.0)
            right2 = right2 + jnp.where(lower, 0.0, two)
            if exx.near(step):
                halo = jnp.where(source == index + 1, message[pl.ds(begin + 2 * ny, ct), :], halo)
        details, nodes, left_end, right_end = x_tile(xtab, where, field, n, cols, (left, right))
        details[-1] = details[-1] - single(xtab, HW1) * halo
        for i in range(n1):
            out[pl.ds((2 * i + 1) * ny + begin, ct), :] = details[i]
            full[pl.ds(i * ny + begin, ct), :] = nodes[i]
        ghost = single(xtab, HG) * halo + single(xtab, VN) * left_end + single(xtab, UN) * right
        left2 = left2 + single(xtab, CA0) * left + single(xtab, KAP) * right_end
        right2 = right2 - single(xtab, CB1) * right + single(xtab, LAM) * left_end
        details, nodes, _, _ = one_level(
            nodes[0::2], nodes[1::2], xtab, where, "2", GA2, GB2, left2, right2
        )
        details[-1] = details[-1] - single(xtab, HW2) * ghost
        for i in range(n2):
            mixed[pl.ds(i * ny + begin, ct), :] = nodes[i]
            mixed[pl.ds((n2 + i) * ny + begin, ct), :] = details[i]
        return carry

    lax.fori_loop(0, ny // ct, body, 0)

    m1, m2 = ny // 2, ny // 4
    ywhere, _ = offsets(ny)

    def column(ref, j):
        return ref[pl.ds(j, n1, stride=ny), :]

    for j in range(m1):
        e = column(full, 2 * j + 1) - single(ytab, ywhere["wl"] + j) * column(full, 2 * j)
        if j + 1 < m1:
            e = e - single(ytab, ywhere["wr"] + j) * column(full, 2 * j + 2)
        out[pl.ds(2 * j + 1, n1, stride=2 * ny), :] = e
    even = [column(mixed, 2 * j) for j in range(m1)]
    odd = [column(mixed, 2 * j + 1) for j in range(m1)]
    _, nodes, p1, q1 = one_level(even, odd, ytab, ywhere, "", GA, GB, None, None)
    for j in range(m1):
        out[pl.ds(2 * ny + 2 * j, n2, stride=4 * ny), :] = nodes[j][n2:]
    thin = [x[:n2] for x in nodes]
    details, nodes, p2, q2 = one_level(
        thin[0::2], thin[1::2], ytab, ywhere, "2", GA2, GB2, None, None
    )
    for j in range(m2):
        out[pl.ds(4 * j, n2, stride=4 * ny), :] = nodes[j]
        out[pl.ds(4 * j + 2, n2, stride=4 * ny), :] = details[j]
    p2, q2 = summaries(ytab, p1[:n2], q1[:n2], p2, q2)
    own[:n2, :] = p1[:n2]
    own[n2:, :] = q1[:n2]
    yindex = lax.axis_index(exy.axis)
    for step, message in zip(exy.steps, messages):
        upward = exy.target(yindex, step) > yindex
        message[:n1, :] = jnp.where(upward, p1, q1)
        message[n1 : n1 + n2, :] = jnp.where(upward, p2, q2)
        if exy.near(step):
            message[n1 + n2 : 2 * n1 + n2, :] = column(full, 0)
            message[2 * n1 + n2 :, :] = mixed[pl.ds(0, n2, stride=ny), :]


def y_table_kernel(ex, ny, stiffness, h_ref, tab, ranks):
    index = lax.axis_index(ex.axis)
    build_table(h_ref[...], index, ny, stiffness, tab)
    where, _ = offsets(ny)
    m1, m2 = ny // 2, ny // 4
    ranks[...] = jnp.zeros_like(ranks)

    def put(rank, j, value):
        ranks[rank, j : j + 1, :] = value

    for rank, name, end in ((0, "v", VN), (1, "u", UN)):
        nodes = [single(tab, where[name] + i) for i in range(m1)]
        for i in range(m1):
            put(rank, 2 * i, nodes[i])
        details, nodes2, _, _ = one_level(
            nodes[0::2], nodes[1::2], tab, where, "2", GA2, GB2, None, None
        )
        details[-1] = details[-1] - single(tab, HW2) * single(tab, end)
        for i in range(m2):
            put(2 + rank, 4 * i, nodes2[i])
            put(2 + rank, 4 * i + 2, details[i])
            put(4 + rank, 4 * i, single(tab, where[name + "2"] + i))
    put(6, ny - 1, -single(tab, HW1))
    put(7, ny - 2, -single(tab, HW2))


def third_kernel(ex, n, ny, *refs):
    partial, tab, ranks, own = refs[:4]
    incoming = refs[4 : 4 + len(ex.steps)]
    out, sums = refs[4 + len(ex.steps) :]
    n1, n2 = n // 2, n // 4
    index = lax.axis_index(ex.axis)
    zero, zero2 = jnp.zeros((n1, LANES), F32), jnp.zeros((n2, LANES), F32)
    left, right, left2, right2, halo, halo2 = zero, zero, zero2, zero2, zero, zero2
    for step, message in zip(ex.steps, incoming):
        source = ex.source(index, step)
        lower = source < index
        one, two = message[:n1, :], message[n1 : n1 + n2, :]
        left = left + jnp.where(lower, one, 0.0)
        right = right + jnp.where(lower, 0.0, one)
        left2 = left2 + jnp.where(lower, two, 0.0)
        right2 = right2 + jnp.where(lower, 0.0, two)
        if ex.near(step):
            mine = source == index + 1
            halo = jnp.where(mine, message[n1 + n2 : 2 * n1 + n2, :], halo)
            halo2 = jnp.where(mine, message[2 * n1 + n2 :, :], halo2)
    p1, q1 = own[:n2, :], own[n2:, :]
    left2, right2 = second_sums(tab, left[:n2], right[:n2], left2, right2, p1, q1)
    ghost = single(tab, HG) * halo2 + single(tab, VN) * p1
    sums[0:n1, :] = left
    sums[n1 : 2 * n1, :] = right
    sums[2 * n1 : 3 * n1, :] = halo
    sums[3 * n1 : 3 * n1 + n2, :] = left2
    sums[3 * n1 + n2 : 3 * n1 + 2 * n2, :] = right2
    sums[3 * n1 + 2 * n2 : 3 * n1 + 3 * n2, :] = ghost

    def row(i):
        return sums[i : i + 1, :]

    def body(t, carry):
        cols = pl.ds(pl.multiple_of(t * 8, 8), 8)
        tables = [ranks[r, cols, :] for r in range(8)]
        for k in range(n1):
            x = partial[2 * k, cols, :] + tables[6] * row(2 * n1 + k)
            if k % 2:
                i = n2 + k // 2
                x = x + tables[0] * row(i) + tables[1] * row(n1 + i)
            else:
                i = k // 2
                x = x + tables[2] * row(i) + tables[3] * row(n1 + i)
                x = x + tables[4] * row(3 * n1 + i) + tables[5] * row(3 * n1 + n2 + i)
                x = x + tables[7] * row(3 * n1 + 2 * n2 + i)
            out[2 * k, cols, :] = x
            out[2 * k + 1, cols, :] = partial[2 * k + 1, cols, :]
        return carry

    lax.fori_loop(0, ny // 8, body, 0)


def shape(*dims):
    return jax.ShapeDtypeStruct(dims, F32)


def on_device(exx, exy, field, spacing_x, spacing_y):
    n, ny, _ = field.shape
    n1, n2 = n // 2, n // 4
    ct = 16
    xrows = offsets(n)[1]
    yrows = offsets(ny)[1]
    params = pltpu.CompilerParams(vmem_limit_bytes=40 * 1024 * 1024)
    xtab, *outgoing = pl.pallas_call(
        functools.partial(first_kernel, exx, n, ny, float(SMOOTH_X) ** 2, ct),
        out_shape=[shape(xrows, LANES)]
        + [shape((3 if exx.near(s) else 2) * ny, LANES) for s in exx.steps],
        compiler_params=params,
        name="x_summary",
    )(spacing_x[None], field)
    ytab, ranks = pl.pallas_call(
        functools.partial(y_table_kernel, exy, ny, float(SMOOTH_Y) ** 2),
        out_shape=[shape(yrows, LANES), shape(8, ny, LANES)],
        compiler_params=params,
        name="y_table",
    )(spacing_y[None])
    incoming = [exx.send(s, x) for s, x in zip(exx.steps, outgoing)]
    partial, own, *outgoing = pl.pallas_call(
        functools.partial(second_kernel, exx, exy, n, ny, ct),
        out_shape=[shape(n * ny, LANES), shape(2 * n2, LANES)]
        + [shape((2 * (n1 + n2)) if exy.near(s) else n1 + n2, LANES) for s in exy.steps],
        scratch_shapes=[pltpu.VMEM((n1 * ny, LANES), F32), pltpu.VMEM((n1 * ny, LANES), F32)],
        compiler_params=params,
        name="x_transform",
    )(field, xtab, ytab, *incoming)
    incoming = [exy.send(s, x) for s, x in zip(exy.steps, outgoing)]
    return pl.pallas_call(
        functools.partial(third_kernel, exy, n, ny),
        out_shape=shape(n, ny, LANES),
        scratch_shapes=[pltpu.VMEM((3 * n1 + 3 * n2, LANES), F32)],
        compiler_params=params,
        name="y_update",
    )(partial.reshape(n, ny, LANES), ytab, ranks, own, *incoming)


def solution(mesh):
    exx = Exchange("gx", mesh.shape["gx"])
    exy = Exchange("gy", mesh.shape["gy"])
    placed = (P("gx", "gy", None), P(), P())
    return jax.shard_map(
        functools.partial(on_device, exx, exy),
        mesh=mesh,
        in_specs=placed,
        out_specs=P("gx", "gy", None),
        check_vma=False,
    )
```

```python
import functools

import jax
import jax.numpy as jnp
from jax import lax
from jax.experimental import pallas as pl
from jax.experimental.pallas import tpu as pltpu
from jax.sharding import PartitionSpec as P

SMOOTH_X = 48
SMOOTH_Y = 96
F32 = jnp.float32
LANES = 128

GA, GB, GA2, GB2, HW1, HW2, CA0, CA1, KAP, LAM, CB0, CB1, VN, UN, HG = range(15)
SINGLES = 16


def offsets(n):
    n1, n2 = n // 2, n // 4
    names = ["wl", "wr", "al", "be", "u", "v"]
    where, row = {}, SINGLES
    for name in names:
        where[name] = row
        row += n1
    for name in names:
        where[name + "2"] = row
        row += n2
    return where, row


def pick(row, stride, start, width):
    source = lax.broadcasted_iota(jnp.int32, (row.shape[1], width), 0)
    target = lax.broadcasted_iota(jnp.int32, (row.shape[1], width), 1)
    select = jnp.where(source == stride * target + start, 1.0, 0.0).astype(F32)
    return jnp.dot(row, select, precision=lax.Precision.HIGHEST, preferred_element_type=F32)


def combine(left, right):
    a, b, c, d = left
    p, q, r, s = right
    return (a * p + b * r, a * q + b * s, c * p + d * r, c * q + d * s)


def build_table(h, index, n, stiffness, tab):
    nodes = h.shape[1]
    m, m2 = nodes // 2, nodes // 4
    n1, n2 = n // 2, n // 4
    lane = lax.broadcasted_iota(jnp.int32, (1, m), 1)
    even1 = pick(h, 2, 0, m)
    odd1 = pick(h, 2, 1, m)
    coarse = even1 + odd1
    inside = lane < m2
    even2 = jnp.where(inside, pick(coarse, 2, 0, m), 1.0)
    odd2 = jnp.where(inside, pick(coarse, 2, 1, m), 1.0)
    even = jnp.concatenate([even1, even2], axis=0)
    odd = jnp.concatenate([odd1, odd2], axis=0)
    lanes = lax.broadcasted_iota(jnp.int32, (2, m), 1)
    level = lax.broadcasted_iota(jnp.int32, (2, m), 0)
    count = jnp.where(level == 0, m, m2)
    real = lanes < count
    last = lanes == count - 1
    width = even + odd
    inverse = 1.0 / width
    stiff = stiffness * inverse
    across = 1.0 / (stiff - width * (1.0 / 6.0))
    same = jnp.where(real, (width * (1.0 / 3.0) + stiff) * across, 1.0)
    into = jnp.where(real, across, 0.0)
    back = jnp.where(real, (stiffness + width * width * (1.0 / 12.0)) * across, 0.0)
    prefix = (same, into, back, same)
    suffix = (same, into, back, same)
    step = 1
    while step < m:
        def shift(x, by, gone, fill):
            return jnp.where(gone, fill, pltpu.roll(x, by, 1))
        head, tail = lanes < step, lanes >= m - step
        fills = (1.0, 0.0, 0.0, 1.0)
        prefix = combine(prefix, [shift(x, step, head, f) for x, f in zip(prefix, fills)])
        suffix = combine(suffix, [shift(x, m - step, tail, f) for x, f in zip(suffix, fills)])
        step *= 2
    u_next = prefix[0]
    u = jnp.where(lanes == 0, 1.0, pltpu.roll(u_next, 1, 1))
    v = suffix[1]
    v_next = jnp.where(lanes == m - 1, 0.0, pltpu.roll(v, m - 1, 1))
    scale = 0.5 / u_next[:, m - 1 : m]
    alpha = (u * even + u_next * odd) * scale
    beta = (v * even + v_next * odd) * scale
    wl = jnp.where(last, 1.0, odd * inverse)
    wr = jnp.where(last, 0.0, even * inverse)
    both = jnp.concatenate([u[0:1], v[0:1]], axis=0)
    node = pick(both, 2, 0, m)
    between = pick(both, 2, 1, m)
    right = jnp.where(lanes >= m2 - 1, 0.0, pltpu.roll(node, m - 1, 1))
    halo = -wr[1:2] * right
    detail = jnp.where(lanes < m2, between - wl[1:2] * node + halo, 0.0)

    def total(x):
        return jnp.sum(x, axis=1, keepdims=True)

    def below(device, weight, which):
        x, y = weight * detail[which : which + 1], weight * halo[which : which + 1]
        return total(
            jnp.where(lane < device * n2, x, 0.0) - jnp.where(lane == device * n2 - 1, y, 0.0)
        )

    def above(device, weight, which):
        x, y = weight * detail[which : which + 1], weight * halo[which : which + 1]
        first = (device + 1) * n2
        return total(jnp.where(lane >= first, x, 0.0) + jnp.where(lane == first - 1, y, 0.0))

    def at(place, x):
        return total(jnp.where(lane == place, x, 0.0))

    al1, be1, al2, be2 = alpha[0:1], beta[0:1], alpha[1:2], beta[1:2]
    wr1, wr2 = wr[0:1], wr[1:2]
    first1, first2 = index * n1, index * n2
    vn, un = at(first1 + n1, v[0:1]), at(first1 + n1, u[0:1])
    singles = {
        GA: at(first1 - 1, -wr1 * al1),
        GB: at(first1 - 1, -wr1 * be1),
        GA2: at(first2 - 1, -wr2 * al2),
        GB2: at(first2 - 1, -wr2 * be2),
        HW1: at(first1 + n1 - 1, wr1),
        HW2: at(first2 + n2 - 1, wr2),
        CA0: below(index, al2, 1),
        CA1: below(index + 1, al2, 1),
        KAP: below(index, al2, 0),
        LAM: above(index, be2, 1),
        CB0: below(index, be2, 0),
        CB1: below(index + 1, be2, 0),
        VN: vn,
        UN: un,
        HG: 1.0
        - vn * at(first1 + n1 - 1, wr1 * al1)
        + un * at(first1 + n1 - 1, wr1 * be1),
    }
    for row, value in singles.items():
        tab[row : row + 1, :] = jnp.broadcast_to(value, (1, LANES))
    where, _ = offsets(n)
    for lv, rows, suffix_name in ((0, n1, ""), (1, n2, "2")):
        col = lax.broadcasted_iota(jnp.int32, (rows, m), 1)
        sub = lax.broadcasted_iota(jnp.int32, (rows, m), 0)
        mine = col == index * rows + sub
        mine_inner = mine & (sub < rows - 1)
        for name, x, mask in (
            ("wl", wl, mine),
            ("wr", wr, mine_inner),
            ("al", alpha, mine),
            ("be", beta, mine),
            ("u", u, mine),
            ("v", v, mine),
        ):
            values = total(jnp.where(mask, x[lv : lv + 1], 0.0))
            start = where[name + suffix_name]
            tab[start : start + rows, :] = jnp.broadcast_to(values, (rows, LANES))


def one_level(even, odd, tab, where, suffix, ga, gb, from_left, from_right):
    def c(name, i):
        row = where[name + suffix] + i
        return tab[row : row + 1, :]

    count = len(even)
    details = []
    for i in range(count):
        e = odd[i] - c("wl", i) * even[i]
        if i + 1 < count:
            e = e - c("wr", i) * even[i + 1]
        details.append(e)
    first = tab[ga : ga + 1, :] * even[0]
    acc = first if from_left is None else from_left + first
    lefts = []
    for i in range(count):
        lefts.append(acc)
        acc = acc + c("al", i) * details[i]
    left_end = acc
    acc = from_right
    rights = [None] * count
    for i in reversed(range(count)):
        term = c("be", i) * details[i]
        acc = term if acc is None else acc + term
        rights[i] = acc
    nodes = [even[i] + c("v", i) * lefts[i] + c("u", i) * rights[i] for i in range(count)]
    right_end = rights[0] + tab[gb : gb + 1, :] * even[0]
    return details, nodes, left_end, right_end


def single(tab, row):
    return tab[row : row + 1, :]


def summaries(tab, p1, q1, p2, q2):
    to_right = p2 + single(tab, KAP) * q1 - single(tab, CA1) * p1
    to_left = q2 + single(tab, LAM) * p1 + single(tab, CB0) * q1
    return to_right, to_left


def second_sums(tab, left, right, left2, right2, p1, q1):
    left_second = left2 + single(tab, CA0) * left + single(tab, KAP) * (q1 + right)
    right_second = right2 - single(tab, CB1) * right + single(tab, LAM) * (left + p1)
    return left_second, right_second


class Exchange:
    def __init__(self, axis, count, paired):
        self.axis, self.count, self.paired = axis, count, paired
        self.xor = count & (count - 1) == 0
        self.steps = list(range(1, count))

    def target(self, i, step):
        return i ^ step if self.xor else (i + step) % self.count

    def source(self, i, step):
        return i ^ step if self.xor else (i + self.count - step) % self.count

    def near(self, step):
        return any(self.target(i, step) == i - 1 for i in range(1, self.count))

    def send(self, step, x):
        pairs = [(i, self.target(i, step)) for i in range(self.count)]
        return lax.ppermute(x, self.axis, pairs)

    def direct(self):
        if not (self.xor and self.paired):
            return self.steps
        return [s for s in self.steps if s == 1 or s % 2 == 0]

    def carries(self, step):
        return self.near(step) or (step not in (1,) and self.passed(step) and self.near(step ^ 1))

    def passed(self, step):
        return step not in self.direct() or (step ^ 1) not in self.direct()

    def all(self, messages):
        direct = dict(zip(self.direct(), messages))
        got = {s: self.send(s, x) for s, x in direct.items()}
        for s in self.steps:
            if s not in got:
                got[s] = self.send(1, got[s ^ 1])
        return [got[s] for s in self.steps]


def x_tile(tab, where, field, n, cols, sums):
    even = [field[2 * i, cols, :] for i in range(n // 2)]
    odd = [field[2 * i + 1, cols, :] for i in range(n // 2)]
    left, right = sums if sums else (None, None)
    return one_level(even, odd, tab, where, "", GA, GB, left, right)


def first_kernel(ex, n, ny, stiffness, ct, h_ref, source, tab, *refs):
    messages = refs[: len(ex.direct())]
    field, spacing, sems, sem = refs[len(ex.direct()) :]
    index = lax.axis_index(ex.axis)
    tiles = ny // ct

    def fetch(t):
        cols = pl.ds(pl.multiple_of(t * ct, ct), ct)
        return pltpu.make_async_copy(source.at[:, cols, :], field.at[:, cols, :], sems.at[t])

    spacing_copy = pltpu.make_async_copy(h_ref, spacing, sem)
    spacing_copy.start()
    for t in range(tiles):
        fetch(t).start()
    spacing_copy.wait()
    build_table(spacing[...], index, n, stiffness, tab)
    where, _ = offsets(n)

    def body(t, carry):
        begin = pl.multiple_of(t * ct, ct)
        cols = pl.ds(begin, ct)
        fetch(t).wait()
        _, nodes, p1, q1 = x_tile(tab, where, field, n, cols, None)
        _, _, p2, q2 = one_level(nodes[0::2], nodes[1::2], tab, where, "2", GA2, GB2, None, None)
        p2, q2 = summaries(tab, p1, q1, p2, q2)
        for step, message in zip(ex.direct(), messages):
            upward = ex.target(index, step) > index
            message[cols, :] = jnp.where(upward, p1, q1)
            message[pl.ds(begin + ny, ct), :] = jnp.where(upward, p2, q2)
            if ex.carries(step):
                message[pl.ds(begin + 2 * ny, ct), :] = field[0, cols, :]
        return carry

    lax.fori_loop(0, tiles, body, 0)


def second_kernel(exx, exy, n, ny, ct, *refs):
    field, xtab, ytab = refs[:3]
    incoming = refs[3 : 3 + len(exx.steps)]
    rest = refs[3 + len(exx.steps) :]
    result, out, own = rest[:3]
    messages = rest[3 : 3 + len(exy.steps)]
    full, mixed, fine, sems = rest[3 + len(exy.steps) :]
    index = lax.axis_index(exx.axis)
    n1, n2 = n // 2, n // 4
    where, _ = offsets(n)

    def put(t):
        cols = pl.ds(pl.multiple_of(t * ct, ct), ct)
        return pltpu.make_async_copy(
            fine.at[:, cols, :], result.at[:, 1, cols, :], sems.at[t]
        )

    def body(t, carry):
        begin = pl.multiple_of(t * ct, ct)
        cols = pl.ds(begin, ct)
        zero = jnp.zeros((ct, LANES), F32)
        left = right = left2 = right2 = halo = zero
        for step, message in zip(exx.steps, incoming):
            source = exx.source(index, step)
            lower = source < index
            one = message[cols, :]
            two = message[pl.ds(begin + ny, ct), :]
            left = left + jnp.where(lower, one, 0.0)
            right = right + jnp.where(lower, 0.0, one)
            left2 = left2 + jnp.where(lower, two, 0.0)
            right2 = right2 + jnp.where(lower, 0.0, two)
            if exx.near(step):
                halo = jnp.where(source == index + 1, message[pl.ds(begin + 2 * ny, ct), :], halo)
        details, nodes, left_end, right_end = x_tile(xtab, where, field, n, cols, (left, right))
        details[-1] = details[-1] - single(xtab, HW1) * halo
        for i in range(n1):
            fine[i, cols, :] = details[i]
            full[pl.ds(i * ny + begin, ct), :] = nodes[i]
        put(t).start()
        ghost = single(xtab, HG) * halo + single(xtab, VN) * left_end + single(xtab, UN) * right
        left2 = left2 + single(xtab, CA0) * left + single(xtab, KAP) * right_end
        right2 = right2 - single(xtab, CB1) * right + single(xtab, LAM) * left_end
        details, nodes, _, _ = one_level(
            nodes[0::2], nodes[1::2], xtab, where, "2", GA2, GB2, left2, right2
        )
        details[-1] = details[-1] - single(xtab, HW2) * ghost
        for i in range(n2):
            mixed[pl.ds(i * ny + begin, ct), :] = nodes[i]
            mixed[pl.ds((n2 + i) * ny + begin, ct), :] = details[i]
        return carry

    lax.fori_loop(0, ny // ct, body, 0)

    m1, m2 = ny // 2, ny // 4
    ywhere, _ = offsets(ny)

    def column(ref, j):
        return ref[pl.ds(j, n1, stride=ny), :]

    for j in range(m1):
        e = column(full, 2 * j + 1) - single(ytab, ywhere["wl"] + j) * column(full, 2 * j)
        if j + 1 < m1:
            e = e - single(ytab, ywhere["wr"] + j) * column(full, 2 * j + 2)
        out[pl.ds(2 * j + 1, n1, stride=ny), :] = e
    even = [column(mixed, 2 * j) for j in range(m1)]
    odd = [column(mixed, 2 * j + 1) for j in range(m1)]
    _, nodes, p1, q1 = one_level(even, odd, ytab, ywhere, "", GA, GB, None, None)
    for j in range(m1):
        out[pl.ds(ny + 2 * j, n2, stride=2 * ny), :] = nodes[j][n2:]
    thin = [x[:n2] for x in nodes]
    details, nodes, p2, q2 = one_level(
        thin[0::2], thin[1::2], ytab, ywhere, "2", GA2, GB2, None, None
    )
    for j in range(m2):
        out[pl.ds(4 * j, n2, stride=2 * ny), :] = nodes[j]
        out[pl.ds(4 * j + 2, n2, stride=2 * ny), :] = details[j]
    p2, q2 = summaries(ytab, p1[:n2], q1[:n2], p2, q2)
    own[:n2, :] = p1[:n2]
    own[n2:, :] = q1[:n2]
    yindex = lax.axis_index(exy.axis)
    for step, message in zip(exy.steps, messages):
        upward = exy.target(yindex, step) > yindex
        message[:n1, :] = jnp.where(upward, p1, q1)
        message[n1 : n1 + n2, :] = jnp.where(upward, p2, q2)
        if exy.near(step):
            message[n1 + n2 : 2 * n1 + n2, :] = column(full, 0)
            message[2 * n1 + n2 :, :] = mixed[pl.ds(0, n2, stride=ny), :]
    for t in range(ny // ct):
        put(t).wait()


def y_table_kernel(ex, ny, stiffness, h_ref, tab, ranks):
    index = lax.axis_index(ex.axis)
    build_table(h_ref[...], index, ny, stiffness, tab)
    where, _ = offsets(ny)
    m1, m2 = ny // 2, ny // 4
    ranks[...] = jnp.zeros_like(ranks)

    def put(rank, j, value):
        ranks[rank, j : j + 1, :] = value

    for rank, name, end in ((0, "v", VN), (1, "u", UN)):
        nodes = [single(tab, where[name] + i) for i in range(m1)]
        for i in range(m1):
            put(rank, 2 * i, nodes[i])
        details, nodes2, _, _ = one_level(
            nodes[0::2], nodes[1::2], tab, where, "2", GA2, GB2, None, None
        )
        details[-1] = details[-1] - single(tab, HW2) * single(tab, end)
        for i in range(m2):
            put(2 + rank, 4 * i, nodes2[i])
            put(2 + rank, 4 * i + 2, details[i])
            put(4 + rank, 4 * i, single(tab, where[name + "2"] + i))
    put(6, ny - 1, -single(tab, HW1))
    put(7, ny - 2, -single(tab, HW2))


def third_kernel(ex, n, ny, *refs):
    partial, tab, ranks, own = refs[1:5]
    incoming = refs[5 : 5 + len(ex.steps)]
    result, sums, done, sems = refs[5 + len(ex.steps) :]
    n1, n2 = n // 2, n // 4
    index = lax.axis_index(ex.axis)
    zero, zero2 = jnp.zeros((n1, LANES), F32), jnp.zeros((n2, LANES), F32)
    left, right, left2, right2, halo, halo2 = zero, zero, zero2, zero2, zero, zero2
    for step, message in zip(ex.steps, incoming):
        source = ex.source(index, step)
        lower = source < index
        one, two = message[:n1, :], message[n1 : n1 + n2, :]
        left = left + jnp.where(lower, one, 0.0)
        right = right + jnp.where(lower, 0.0, one)
        left2 = left2 + jnp.where(lower, two, 0.0)
        right2 = right2 + jnp.where(lower, 0.0, two)
        if ex.near(step):
            mine = source == index + 1
            halo = jnp.where(mine, message[n1 + n2 : 2 * n1 + n2, :], halo)
            halo2 = jnp.where(mine, message[2 * n1 + n2 :, :], halo2)
    p1, q1 = own[:n2, :], own[n2:, :]
    left2, right2 = second_sums(tab, left[:n2], right[:n2], left2, right2, p1, q1)
    ghost = single(tab, HG) * halo2 + single(tab, VN) * p1
    sums[0:n1, :] = left
    sums[n1 : 2 * n1, :] = right
    sums[2 * n1 : 3 * n1, :] = halo
    sums[3 * n1 : 3 * n1 + n2, :] = left2
    sums[3 * n1 + n2 : 3 * n1 + 2 * n2, :] = right2
    sums[3 * n1 + 2 * n2 : 3 * n1 + 3 * n2, :] = ghost

    def row(i):
        return sums[i : i + 1, :]

    def put(t):
        cols = pl.ds(pl.multiple_of(t * 8, 8), 8)
        return pltpu.make_async_copy(
            done.at[:, cols, :], result.at[:, 0, cols, :], sems.at[t]
        )

    def body(t, carry):
        cols = pl.ds(pl.multiple_of(t * 8, 8), 8)
        tables = [ranks[r, cols, :] for r in range(8)]
        for k in range(n1):
            x = partial[k, cols, :] + tables[6] * row(2 * n1 + k)
            if k % 2:
                i = n2 + k // 2
                x = x + tables[0] * row(i) + tables[1] * row(n1 + i)
            else:
                i = k // 2
                x = x + tables[2] * row(i) + tables[3] * row(n1 + i)
                x = x + tables[4] * row(3 * n1 + i) + tables[5] * row(3 * n1 + n2 + i)
                x = x + tables[7] * row(3 * n1 + 2 * n2 + i)
            done[k, cols, :] = x
        put(t).start()
        return carry

    lax.fori_loop(0, ny // 8, body, 0)
    for t in range(ny // 8):
        put(t).wait()


def shape(*dims):
    return jax.ShapeDtypeStruct(dims, F32)


def on_device(exx, exy, field, spacing_x, spacing_y):
    n, ny, _ = field.shape
    n1, n2 = n // 2, n // 4
    ct = 16
    xrows = offsets(n)[1]
    yrows = offsets(ny)[1]
    params = pltpu.CompilerParams(vmem_limit_bytes=40 * 1024 * 1024)
    anywhere = pl.BlockSpec(memory_space=pl.ANY)
    inside = pl.BlockSpec(memory_space=pltpu.VMEM)
    dma = pltpu.SemaphoreType.DMA
    xtab, *outgoing = pl.pallas_call(
        functools.partial(first_kernel, exx, n, ny, float(SMOOTH_X) ** 2, ct),
        out_shape=[shape(xrows, LANES)]
        + [shape((3 if exx.carries(s) else 2) * ny, LANES) for s in exx.direct()],
        in_specs=[anywhere, anywhere],
        scratch_shapes=[
            pltpu.VMEM((n, ny, LANES), F32),
            pltpu.VMEM((1, spacing_x.shape[0]), F32),
            dma((ny // ct,)),
            dma(()),
        ],
        compiler_params=params,
        name="x_summary",
    )(spacing_x[None], field)
    ytab, ranks = pl.pallas_call(
        functools.partial(y_table_kernel, exy, ny, float(SMOOTH_Y) ** 2),
        out_shape=[shape(yrows, LANES), shape(8, ny, LANES)],
        compiler_params=params,
        name="y_table",
    )(spacing_y[None])
    incoming = exx.all(outgoing)
    result, partial, own, *outgoing = pl.pallas_call(
        functools.partial(second_kernel, exx, exy, n, ny, ct),
        out_shape=[shape(n1, 2, ny, LANES), shape(n1 * ny, LANES), shape(2 * n2, LANES)]
        + [shape((2 * (n1 + n2)) if exy.near(s) else n1 + n2, LANES) for s in exy.steps],
        out_specs=[anywhere] + [inside] * (2 + len(exy.steps)),
        scratch_shapes=[
            pltpu.VMEM((n1 * ny, LANES), F32),
            pltpu.VMEM((n1 * ny, LANES), F32),
            pltpu.VMEM((n1, ny, LANES), F32),
            dma((ny // ct,)),
        ],
        compiler_params=params,
        name="x_transform",
    )(field, xtab, ytab, *incoming)
    incoming = exy.all(outgoing)
    result = pl.pallas_call(
        functools.partial(third_kernel, exy, n, ny),
        out_shape=shape(n1, 2, ny, LANES),
        in_specs=[anywhere] + [inside] * (4 + len(incoming)),
        out_specs=anywhere,
        input_output_aliases={0: 0},
        scratch_shapes=[
            pltpu.VMEM((3 * n1 + 3 * n2, LANES), F32),
            pltpu.VMEM((n1, ny, LANES), F32),
            dma((ny // 8,)),
        ],
        compiler_params=params,
        name="y_update",
    )(result, partial.reshape(n1, ny, LANES), ytab, ranks, own, *incoming)
    return result.reshape(n, ny, LANES)


def solution(mesh):
    exx = Exchange("gx", mesh.shape["gx"], True)
    exy = Exchange("gy", mesh.shape["gy"], False)
    placed = (P("gx", "gy", None), P(), P())
    return jax.shard_map(
        functools.partial(on_device, exx, exy),
        mesh=mesh,
        in_specs=placed,
        out_specs=P("gx", "gy", None),
        check_vma=False,
    )
```

```python
import functools

import jax
import jax.numpy as jnp
from jax import lax
from jax.experimental import pallas as pl
from jax.experimental.pallas import tpu as pltpu
from jax.sharding import PartitionSpec as P

SMOOTH_X = 48
SMOOTH_Y = 96
F32 = jnp.float32
LANES = 128

GA, GB, GA2, GB2, HW1, HW2, CA0, CA1, KAP, LAM, CB0, CB1, VN, UN, HG = range(15)
SINGLES = 16


def offsets(n):
    n1, n2 = n // 2, n // 4
    names = ["wl", "wr", "al", "be", "u", "v"]
    where, row = {}, SINGLES
    for name in names:
        where[name] = row
        row += n1
    for name in names:
        where[name + "2"] = row
        row += n2
    return where, row


def pick(row, stride, start, width):
    source = lax.broadcasted_iota(jnp.int32, (row.shape[1], width), 0)
    target = lax.broadcasted_iota(jnp.int32, (row.shape[1], width), 1)
    select = jnp.where(source == stride * target + start, 1.0, 0.0).astype(F32)
    return jnp.dot(row, select, precision=lax.Precision.HIGHEST, preferred_element_type=F32)


def combine(left, right):
    a, b, c, d = left
    p, q, r, s = right
    return (a * p + b * r, a * q + b * s, c * p + d * r, c * q + d * s)


def build_table(h, index, n, stiffness, tab):
    nodes = h.shape[1]
    m, m2 = nodes // 2, nodes // 4
    n1, n2 = n // 2, n // 4
    lane = lax.broadcasted_iota(jnp.int32, (1, m), 1)
    even1 = pick(h, 2, 0, m)
    odd1 = pick(h, 2, 1, m)
    coarse = even1 + odd1
    inside = lane < m2
    even2 = jnp.where(inside, pick(coarse, 2, 0, m), 1.0)
    odd2 = jnp.where(inside, pick(coarse, 2, 1, m), 1.0)
    even = jnp.concatenate([even1, even2], axis=0)
    odd = jnp.concatenate([odd1, odd2], axis=0)
    lanes = lax.broadcasted_iota(jnp.int32, (2, m), 1)
    level = lax.broadcasted_iota(jnp.int32, (2, m), 0)
    count = jnp.where(level == 0, m, m2)
    real = lanes < count
    last = lanes == count - 1
    width = even + odd
    inverse = 1.0 / width
    stiff = stiffness * inverse
    across = 1.0 / (stiff - width * (1.0 / 6.0))
    same = jnp.where(real, (width * (1.0 / 3.0) + stiff) * across, 1.0)
    into = jnp.where(real, across, 0.0)
    back = jnp.where(real, (stiffness + width * width * (1.0 / 12.0)) * across, 0.0)
    prefix = (same, into, back, same)
    suffix = (same, into, back, same)
    step = 1
    while step < m:
        def shift(x, by, gone, fill):
            return jnp.where(gone, fill, pltpu.roll(x, by, 1))
        head, tail = lanes < step, lanes >= m - step
        fills = (1.0, 0.0, 0.0, 1.0)
        prefix = combine(prefix, [shift(x, step, head, f) for x, f in zip(prefix, fills)])
        suffix = combine(suffix, [shift(x, m - step, tail, f) for x, f in zip(suffix, fills)])
        step *= 2
    u_next = prefix[0]
    u = jnp.where(lanes == 0, 1.0, pltpu.roll(u_next, 1, 1))
    v = suffix[1]
    v_next = jnp.where(lanes == m - 1, 0.0, pltpu.roll(v, m - 1, 1))
    scale = 0.5 / u_next[:, m - 1 : m]
    alpha = (u * even + u_next * odd) * scale
    beta = (v * even + v_next * odd) * scale
    wl = jnp.where(last, 1.0, odd * inverse)
    wr = jnp.where(last, 0.0, even * inverse)
    both = jnp.concatenate([u[0:1], v[0:1]], axis=0)
    node = pick(both, 2, 0, m)
    between = pick(both, 2, 1, m)
    right = jnp.where(lanes >= m2 - 1, 0.0, pltpu.roll(node, m - 1, 1))
    halo = -wr[1:2] * right
    detail = jnp.where(lanes < m2, between - wl[1:2] * node + halo, 0.0)

    def total(x):
        return jnp.sum(x, axis=1, keepdims=True)

    def below(device, weight, which):
        x, y = weight * detail[which : which + 1], weight * halo[which : which + 1]
        return total(
            jnp.where(lane < device * n2, x, 0.0) - jnp.where(lane == device * n2 - 1, y, 0.0)
        )

    def above(device, weight, which):
        x, y = weight * detail[which : which + 1], weight * halo[which : which + 1]
        first = (device + 1) * n2
        return total(jnp.where(lane >= first, x, 0.0) + jnp.where(lane == first - 1, y, 0.0))

    def at(place, x):
        return total(jnp.where(lane == place, x, 0.0))

    al1, be1, al2, be2 = alpha[0:1], beta[0:1], alpha[1:2], beta[1:2]
    wr1, wr2 = wr[0:1], wr[1:2]
    first1, first2 = index * n1, index * n2
    vn, un = at(first1 + n1, v[0:1]), at(first1 + n1, u[0:1])
    singles = {
        GA: at(first1 - 1, -wr1 * al1),
        GB: at(first1 - 1, -wr1 * be1),
        GA2: at(first2 - 1, -wr2 * al2),
        GB2: at(first2 - 1, -wr2 * be2),
        HW1: at(first1 + n1 - 1, wr1),
        HW2: at(first2 + n2 - 1, wr2),
        CA0: below(index, al2, 1),
        CA1: below(index + 1, al2, 1),
        KAP: below(index, al2, 0),
        LAM: above(index, be2, 1),
        CB0: below(index, be2, 0),
        CB1: below(index + 1, be2, 0),
        VN: vn,
        UN: un,
        HG: 1.0
        - vn * at(first1 + n1 - 1, wr1 * al1)
        + un * at(first1 + n1 - 1, wr1 * be1),
    }
    for row, value in singles.items():
        tab[row : row + 1, :] = jnp.broadcast_to(value, (1, LANES))
    where, _ = offsets(n)
    for lv, rows, suffix_name in ((0, n1, ""), (1, n2, "2")):
        col = lax.broadcasted_iota(jnp.int32, (rows, m), 1)
        sub = lax.broadcasted_iota(jnp.int32, (rows, m), 0)
        mine = col == index * rows + sub
        mine_inner = mine & (sub < rows - 1)
        for name, x, mask in (
            ("wl", wl, mine),
            ("wr", wr, mine_inner),
            ("al", alpha, mine),
            ("be", beta, mine),
            ("u", u, mine),
            ("v", v, mine),
        ):
            values = total(jnp.where(mask, x[lv : lv + 1], 0.0))
            start = where[name + suffix_name]
            tab[start : start + rows, :] = jnp.broadcast_to(values, (rows, LANES))


def one_level(even, odd, tab, where, suffix, ga, gb, from_left, from_right):
    def c(name, i):
        row = where[name + suffix] + i
        return tab[row : row + 1, :]

    count = len(even)
    details = []
    for i in range(count):
        e = odd[i] - c("wl", i) * even[i]
        if i + 1 < count:
            e = e - c("wr", i) * even[i + 1]
        details.append(e)
    first = tab[ga : ga + 1, :] * even[0]
    acc = first if from_left is None else from_left + first
    lefts = []
    for i in range(count):
        lefts.append(acc)
        acc = acc + c("al", i) * details[i]
    left_end = acc
    acc = from_right
    rights = [None] * count
    for i in reversed(range(count)):
        term = c("be", i) * details[i]
        acc = term if acc is None else acc + term
        rights[i] = acc
    nodes = [even[i] + c("v", i) * lefts[i] + c("u", i) * rights[i] for i in range(count)]
    right_end = rights[0] + tab[gb : gb + 1, :] * even[0]
    return details, nodes, left_end, right_end


def single(tab, row):
    return tab[row : row + 1, :]


def summaries(tab, p1, q1, p2, q2):
    to_right = p2 + single(tab, KAP) * q1 - single(tab, CA1) * p1
    to_left = q2 + single(tab, LAM) * p1 + single(tab, CB0) * q1
    return to_right, to_left


def second_sums(tab, left, right, left2, right2, p1, q1):
    left_second = left2 + single(tab, CA0) * left + single(tab, KAP) * (q1 + right)
    right_second = right2 - single(tab, CB1) * right + single(tab, LAM) * (left + p1)
    return left_second, right_second


class Exchange:
    def __init__(self, axis, count, paired):
        self.axis, self.count, self.paired = axis, count, paired
        self.xor = count & (count - 1) == 0
        self.steps = list(range(1, count))

    def target(self, i, step):
        return i ^ step if self.xor else (i + step) % self.count

    def source(self, i, step):
        return i ^ step if self.xor else (i + self.count - step) % self.count

    def near(self, step):
        return any(self.target(i, step) == i - 1 for i in range(1, self.count))

    def send(self, step, x):
        pairs = [(i, self.target(i, step)) for i in range(self.count)]
        return lax.ppermute(x, self.axis, pairs)

    def direct(self):
        if not (self.xor and self.paired):
            return self.steps
        return [s for s in self.steps if s == 1 or s % 2 == 0]

    def carries(self, step):
        return self.near(step) or (step not in (1,) and self.passed(step) and self.near(step ^ 1))

    def passed(self, step):
        return step not in self.direct() or (step ^ 1) not in self.direct()

    def all(self, messages):
        direct = dict(zip(self.direct(), messages))
        got = {s: self.send(s, x) for s, x in direct.items()}
        for s in self.steps:
            if s not in got:
                got[s] = self.send(1, got[s ^ 1])
        return [got[s] for s in self.steps]


def x_tile(tab, where, field, n, cols, sums):
    even = [field[2 * i, cols, :] for i in range(n // 2)]
    odd = [field[2 * i + 1, cols, :] for i in range(n // 2)]
    left, right = sums if sums else (None, None)
    return one_level(even, odd, tab, where, "", GA, GB, left, right)


def first_kernel(ex, n, ny, stiffness, ct, h_ref, hy_ref, source, field, spacing_y, tab, *refs):
    messages = refs[: len(ex.direct())]
    spacing, sems, sem, sem_y = refs[len(ex.direct()) :]
    index = lax.axis_index(ex.axis)
    tiles = ny // ct

    def fetch(t):
        cols = pl.ds(pl.multiple_of(t * ct, ct), ct)
        return pltpu.make_async_copy(source.at[:, cols, :], field.at[:, cols, :], sems.at[t])

    spacing_copy = pltpu.make_async_copy(h_ref, spacing, sem)
    spacing_copy.start()
    for t in range(tiles):
        fetch(t).start()
    other_copy = pltpu.make_async_copy(hy_ref, spacing_y, sem_y)
    other_copy.start()
    spacing_copy.wait()
    build_table(spacing[...], index, n, stiffness, tab)
    where, _ = offsets(n)

    def body(t, carry):
        begin = pl.multiple_of(t * ct, ct)
        cols = pl.ds(begin, ct)
        fetch(t).wait()
        _, nodes, p1, q1 = x_tile(tab, where, field, n, cols, None)
        _, _, p2, q2 = one_level(nodes[0::2], nodes[1::2], tab, where, "2", GA2, GB2, None, None)
        p2, q2 = summaries(tab, p1, q1, p2, q2)
        for step, message in zip(ex.direct(), messages):
            upward = ex.target(index, step) > index
            message[cols, :] = jnp.where(upward, p1, q1)
            message[pl.ds(begin + ny, ct), :] = jnp.where(upward, p2, q2)
            if ex.carries(step):
                message[pl.ds(begin + 2 * ny, ct), :] = field[0, cols, :]
        return carry

    lax.fori_loop(0, tiles, body, 0)
    other_copy.wait()


def second_kernel(exx, exy, n, ny, ct, *refs):
    field, xtab, ytab = refs[:3]
    incoming = refs[3 : 3 + len(exx.steps)]
    rest = refs[3 + len(exx.steps) :]
    result, out, own = rest[:3]
    messages = rest[3 : 3 + len(exy.steps)]
    full, mixed, fine, sems = rest[3 + len(exy.steps) :]
    index = lax.axis_index(exx.axis)
    n1, n2 = n // 2, n // 4
    where, _ = offsets(n)

    def put(t):
        cols = pl.ds(pl.multiple_of(t * ct, ct), ct)
        return pltpu.make_async_copy(
            fine.at[:, cols, :], result.at[:, 1, cols, :], sems.at[t]
        )

    def body(t, carry):
        begin = pl.multiple_of(t * ct, ct)
        cols = pl.ds(begin, ct)
        zero = jnp.zeros((ct, LANES), F32)
        left = right = left2 = right2 = halo = zero
        for step, message in zip(exx.steps, incoming):
            source = exx.source(index, step)
            lower = source < index
            one = message[cols, :]
            two = message[pl.ds(begin + ny, ct), :]
            left = left + jnp.where(lower, one, 0.0)
            right = right + jnp.where(lower, 0.0, one)
            left2 = left2 + jnp.where(lower, two, 0.0)
            right2 = right2 + jnp.where(lower, 0.0, two)
            if exx.near(step):
                halo = jnp.where(source == index + 1, message[pl.ds(begin + 2 * ny, ct), :], halo)
        details, nodes, left_end, right_end = x_tile(xtab, where, field, n, cols, (left, right))
        details[-1] = details[-1] - single(xtab, HW1) * halo
        for i in range(n1):
            fine[i, cols, :] = details[i]
            full[pl.ds(i * ny + begin, ct), :] = nodes[i]
        put(t).start()
        ghost = single(xtab, HG) * halo + single(xtab, VN) * left_end + single(xtab, UN) * right
        left2 = left2 + single(xtab, CA0) * left + single(xtab, KAP) * right_end
        right2 = right2 - single(xtab, CB1) * right + single(xtab, LAM) * left_end
        details, nodes, _, _ = one_level(
            nodes[0::2], nodes[1::2], xtab, where, "2", GA2, GB2, left2, right2
        )
        details[-1] = details[-1] - single(xtab, HW2) * ghost
        for i in range(n2):
            mixed[pl.ds(i * ny + begin, ct), :] = nodes[i]
            mixed[pl.ds((n2 + i) * ny + begin, ct), :] = details[i]
        return carry

    lax.fori_loop(0, ny // ct, body, 0)

    m1, m2 = ny // 2, ny // 4
    ywhere, _ = offsets(ny)

    def column(ref, j):
        return ref[pl.ds(j, n1, stride=ny), :]

    for j in range(m1):
        e = column(full, 2 * j + 1) - single(ytab, ywhere["wl"] + j) * column(full, 2 * j)
        if j + 1 < m1:
            e = e - single(ytab, ywhere["wr"] + j) * column(full, 2 * j + 2)
        out[pl.ds(2 * j + 1, n1, stride=ny), :] = e
    even = [column(mixed, 2 * j) for j in range(m1)]
    odd = [column(mixed, 2 * j + 1) for j in range(m1)]
    _, nodes, p1, q1 = one_level(even, odd, ytab, ywhere, "", GA, GB, None, None)
    for j in range(m1):
        out[pl.ds(ny + 2 * j, n2, stride=2 * ny), :] = nodes[j][n2:]
    thin = [x[:n2] for x in nodes]
    details, nodes, p2, q2 = one_level(
        thin[0::2], thin[1::2], ytab, ywhere, "2", GA2, GB2, None, None
    )
    for j in range(m2):
        out[pl.ds(4 * j, n2, stride=2 * ny), :] = nodes[j]
        out[pl.ds(4 * j + 2, n2, stride=2 * ny), :] = details[j]
    p2, q2 = summaries(ytab, p1[:n2], q1[:n2], p2, q2)
    own[:n2, :] = p1[:n2]
    own[n2:, :] = q1[:n2]
    yindex = lax.axis_index(exy.axis)
    for step, message in zip(exy.steps, messages):
        upward = exy.target(yindex, step) > yindex
        message[:n1, :] = jnp.where(upward, p1, q1)
        message[n1 : n1 + n2, :] = jnp.where(upward, p2, q2)
        if exy.near(step):
            message[n1 + n2 : 2 * n1 + n2, :] = column(full, 0)
            message[2 * n1 + n2 :, :] = mixed[pl.ds(0, n2, stride=ny), :]
    for t in range(ny // ct):
        put(t).wait()


def y_table_kernel(ex, ny, stiffness, h_ref, passing, tab, passed):
    index = lax.axis_index(ex.axis)
    build_table(h_ref[...], index, ny, stiffness, tab)


def rank_kernel(ny, tab, ranks):
    where, _ = offsets(ny)
    m1, m2 = ny // 2, ny // 4
    ranks[...] = jnp.zeros_like(ranks)

    def put(rank, j, value):
        ranks[rank, j : j + 1, :] = value

    for rank, name, end in ((0, "v", VN), (1, "u", UN)):
        nodes = [single(tab, where[name] + i) for i in range(m1)]
        for i in range(m1):
            put(rank, 2 * i, nodes[i])
        details, nodes2, _, _ = one_level(
            nodes[0::2], nodes[1::2], tab, where, "2", GA2, GB2, None, None
        )
        details[-1] = details[-1] - single(tab, HW2) * single(tab, end)
        for i in range(m2):
            put(2 + rank, 4 * i, nodes2[i])
            put(2 + rank, 4 * i + 2, details[i])
            put(4 + rank, 4 * i, single(tab, where[name + "2"] + i))
    put(6, ny - 1, -single(tab, HW1))
    put(7, ny - 2, -single(tab, HW2))


def third_kernel(ex, n, ny, *refs):
    partial, tab, ranks, own = refs[1:5]
    incoming = refs[5 : 5 + len(ex.steps)]
    result, sums, done, sems = refs[5 + len(ex.steps) :]
    n1, n2 = n // 2, n // 4
    index = lax.axis_index(ex.axis)
    zero, zero2 = jnp.zeros((n1, LANES), F32), jnp.zeros((n2, LANES), F32)
    left, right, left2, right2, halo, halo2 = zero, zero, zero2, zero2, zero, zero2
    for step, message in zip(ex.steps, incoming):
        source = ex.source(index, step)
        lower = source < index
        one, two = message[:n1, :], message[n1 : n1 + n2, :]
        left = left + jnp.where(lower, one, 0.0)
        right = right + jnp.where(lower, 0.0, one)
        left2 = left2 + jnp.where(lower, two, 0.0)
        right2 = right2 + jnp.where(lower, 0.0, two)
        if ex.near(step):
            mine = source == index + 1
            halo = jnp.where(mine, message[n1 + n2 : 2 * n1 + n2, :], halo)
            halo2 = jnp.where(mine, message[2 * n1 + n2 :, :], halo2)
    p1, q1 = own[:n2, :], own[n2:, :]
    left2, right2 = second_sums(tab, left[:n2], right[:n2], left2, right2, p1, q1)
    ghost = single(tab, HG) * halo2 + single(tab, VN) * p1
    sums[0:n1, :] = left
    sums[n1 : 2 * n1, :] = right
    sums[2 * n1 : 3 * n1, :] = halo
    sums[3 * n1 : 3 * n1 + n2, :] = left2
    sums[3 * n1 + n2 : 3 * n1 + 2 * n2, :] = right2
    sums[3 * n1 + 2 * n2 : 3 * n1 + 3 * n2, :] = ghost

    def row(i):
        return sums[i : i + 1, :]

    def put(t):
        cols = pl.ds(pl.multiple_of(t * 8, 8), 8)
        return pltpu.make_async_copy(
            done.at[:, cols, :], result.at[:, 0, cols, :], sems.at[t]
        )

    def body(t, carry):
        cols = pl.ds(pl.multiple_of(t * 8, 8), 8)
        tables = [ranks[r, cols, :] for r in range(8)]
        for k in range(n1):
            x = partial[k, cols, :] + tables[6] * row(2 * n1 + k)
            if k % 2:
                i = n2 + k // 2
                x = x + tables[0] * row(i) + tables[1] * row(n1 + i)
            else:
                i = k // 2
                x = x + tables[2] * row(i) + tables[3] * row(n1 + i)
                x = x + tables[4] * row(3 * n1 + i) + tables[5] * row(3 * n1 + n2 + i)
                x = x + tables[7] * row(3 * n1 + 2 * n2 + i)
            done[k, cols, :] = x
        put(t).start()
        return carry

    lax.fori_loop(0, ny // 8, body, 0)
    for t in range(ny // 8):
        put(t).wait()


def shape(*dims):
    return jax.ShapeDtypeStruct(dims, F32)


def on_device(exx, exy, field, spacing_x, spacing_y):
    n, ny, _ = field.shape
    n1, n2 = n // 2, n // 4
    ct = 16
    xrows = offsets(n)[1]
    yrows = offsets(ny)[1]
    params = pltpu.CompilerParams(vmem_limit_bytes=40 * 1024 * 1024)
    anywhere = pl.BlockSpec(memory_space=pl.ANY)
    inside = pl.BlockSpec(memory_space=pltpu.VMEM)
    dma = pltpu.SemaphoreType.DMA
    operands = (spacing_x[None], spacing_y[None], field)
    field, heights, xtab, *outgoing = pl.pallas_call(
        functools.partial(first_kernel, exx, n, ny, float(SMOOTH_X) ** 2, ct),
        out_shape=[shape(n, ny, LANES), shape(*operands[1].shape), shape(xrows, LANES)]
        + [shape((3 if exx.carries(s) else 2) * ny, LANES) for s in exx.direct()],
        in_specs=[anywhere] * 3,
        scratch_shapes=[
            pltpu.VMEM((1, spacing_x.shape[0]), F32),
            dma((ny // ct,)),
            dma(()),
            dma(()),
        ],
        compiler_params=params,
        name="x_summary",
    )(*[pltpu.with_memory_space_constraint(a, pltpu.HBM) for a in operands])
    ytab, outgoing[0] = pl.pallas_call(
        functools.partial(y_table_kernel, exy, ny, float(SMOOTH_Y) ** 2),
        out_shape=[shape(yrows, LANES), shape(*outgoing[0].shape)],
        in_specs=[inside, anywhere],
        out_specs=[inside, anywhere],
        input_output_aliases={1: 1},
        compiler_params=params,
        name="y_table",
    )(heights, outgoing[0])
    incoming = exx.all(outgoing)
    result, partial, own, *outgoing = pl.pallas_call(
        functools.partial(second_kernel, exx, exy, n, ny, ct),
        out_shape=[shape(n1, 2, ny, LANES), shape(n1 * ny, LANES), shape(2 * n2, LANES)]
        + [shape((2 * (n1 + n2)) if exy.near(s) else n1 + n2, LANES) for s in exy.steps],
        out_specs=[anywhere] + [inside] * (2 + len(exy.steps)),
        scratch_shapes=[
            pltpu.VMEM((n1 * ny, LANES), F32),
            pltpu.VMEM((n1 * ny, LANES), F32),
            pltpu.VMEM((n1, ny, LANES), F32),
            dma((ny // ct,)),
        ],
        compiler_params=params,
        name="x_transform",
    )(field, xtab, ytab, *incoming)
    ranks = pl.pallas_call(
        functools.partial(rank_kernel, ny),
        out_shape=shape(8, ny, LANES),
        compiler_params=params,
        name="y_ranks",
    )(ytab)
    incoming = exy.all(outgoing)
    result = pl.pallas_call(
        functools.partial(third_kernel, exy, n, ny),
        out_shape=shape(n1, 2, ny, LANES),
        in_specs=[anywhere] + [inside] * (4 + len(incoming)),
        out_specs=anywhere,
        input_output_aliases={0: 0},
        scratch_shapes=[
            pltpu.VMEM((3 * n1 + 3 * n2, LANES), F32),
            pltpu.VMEM((n1, ny, LANES), F32),
            dma((ny // 8,)),
        ],
        compiler_params=params,
        name="y_update",
    )(result, partial.reshape(n1, ny, LANES), ytab, ranks, own, *incoming)
    return result.reshape(n, ny, LANES)


def solution(mesh):
    exx = Exchange("gx", mesh.shape["gx"], True)
    exy = Exchange("gy", mesh.shape["gy"], False)
    placed = (P("gx", "gy", None), P(), P())
    return jax.shard_map(
        functools.partial(on_device, exx, exy),
        mesh=mesh,
        in_specs=placed,
        out_specs=P("gx", "gy", None),
        check_vma=False,
    )
```

```python
import functools

import jax
import jax.numpy as jnp
from jax import lax
from jax.experimental import pallas as pl
from jax.experimental.pallas import tpu as pltpu
from jax.sharding import PartitionSpec as P

SMOOTH_X = 48
SMOOTH_Y = 96
F32 = jnp.float32
LANES = 128

GA, GB, GA2, GB2, HW1, HW2, CA0, CA1, KAP, LAM, CB0, CB1, VN, UN, HG = range(15)
SINGLES = 16


def offsets(n):
    n1, n2 = n // 2, n // 4
    names = ["wl", "wr", "al", "be", "u", "v"]
    where, row = {}, SINGLES
    for name in names:
        where[name] = row
        row += n1
    for name in names:
        where[name + "2"] = row
        row += n2
    return where, row


def combine(left, right):
    a, b, c, d = left
    p, q, r, s = right
    return (a * p + b * r, a * q + b * s, c * p + d * r, c * q + d * s)


def gather(x, position):
    out = []
    for t in range(position.shape[1] // LANES):
        place = position[:, t * LANES : (t + 1) * LANES]
        inner, block = place & (LANES - 1), place // LANES
        picked = None
        for b in range(x.shape[1] // LANES):
            part = jnp.take_along_axis(
                x[:, b * LANES : (b + 1) * LANES], inner, axis=1, mode="promise_in_bounds"
            )
            picked = part if picked is None else jnp.where(block == b, part, picked)
        out.append(picked)
    return out[0] if len(out) == 1 else jnp.concatenate(out, axis=1)


def down(x, by):
    return pltpu.roll(x, by, 0)


def build_pack(h, counts, places, locals_, stiffness, pack, sums):
    m = h.shape[1] // 2
    lanes = lax.broadcasted_iota(jnp.int32, (8, m), 1)
    rows = lax.broadcasted_iota(jnp.int32, (8, m), 0)
    lower = rows >= 4
    is_y = (rows & 2) == 2
    second = (rows & 1) == 1

    def by_axis(pair):
        return jnp.where(is_y, pair[1], pair[0])

    count = jnp.where(second, by_axis(counts) // 4, by_axis(counts) // 2)
    real = lanes < count
    last = lanes == count - 1
    k = jnp.where(lower, count - 1 - lanes, lanes)
    k = jnp.where(real, k, 0)
    first = jnp.where(second, 4 * k, 2 * k)
    even = gather(h, first) + jnp.where(second, gather(h, first + 1), 0.0)
    odd = gather(h, jnp.where(second, first + 2, first + 1))
    odd = odd + jnp.where(second, gather(h, jnp.where(second, first + 3, first)), 0.0)
    width = even + odd
    inverse = 1.0 / width
    s = by_axis(stiffness)
    stiff = s * inverse
    across = 1.0 / (stiff - width * (1.0 / 6.0))
    same = jnp.where(real, (width * (1.0 / 3.0) + stiff) * across, 1.0)
    into = jnp.where(real, across, 0.0)
    back = jnp.where(real, (s + width * width * (1.0 / 12.0)) * across, 0.0)
    product = (same, into, back, same)
    step = 1
    while step < m:
        head = lanes < step
        shifted = [
            jnp.where(head, fill, pltpu.roll(x, step, 1))
            for x, fill in zip(product, (1.0, 0.0, 0.0, 1.0))
        ]
        product = combine(product, shifted)
        step *= 2
    w = jnp.where(lower, product[1], product[0])
    total = jnp.where(lower, product[3], product[0])[:, m - 1 : m]
    here = jnp.where(lower, count - 1 - lanes, lanes - 1)
    there = jnp.where(lower, count - 2 - lanes, lanes)
    uv = gather(w, jnp.maximum(here, 0))
    uv = jnp.where(lower, jnp.where(real, uv, 0.0), jnp.where(lanes == 0, 1.0, uv))
    uv_next = gather(w, jnp.maximum(there, 0))
    uv_next = jnp.where(lower & (lanes >= count - 1), 0.0, uv_next)
    even = jnp.where(lower, down(even, 4), even)
    odd = jnp.where(lower, down(odd, 4), odd)
    inverse = jnp.where(lower, down(inverse, 4), inverse)
    ab = jnp.where(real, (uv * even + uv_next * odd) * (0.5 / total), 0.0)
    weight = jnp.where(lower, even, odd) * inverse
    weight = jnp.where(last, jnp.where(lower, 0.0, 1.0), weight)
    weight = jnp.where(real, weight, 0.0)
    pack[0:8, :] = uv
    pack[8:16, :] = ab
    pack[16:24, :] = weight
    other = down(weight, 4)
    wl = jnp.where(lower, other, weight)
    wr = jnp.where(lower, weight, other)
    fine = down(uv, 1)
    twice = jnp.where(real & second, 2 * lanes, 0)
    halo = -wr * gather(fine, jnp.minimum(twice + 2, m - 1))
    detail = gather(fine, twice + 1) - wl * gather(fine, twice) + halo
    valid = real & second
    halo = jnp.where(valid, halo, 0.0)
    detail = jnp.where(valid, detail, 0.0)
    place = by_axis(places)
    local = jnp.where(second, by_axis(locals_) // 4, by_axis(locals_) // 2)
    begin, end = place * local, (place + 1) * local

    def lane_sum(row, x):
        value = jnp.sum(x, axis=1, keepdims=True)
        sums[8 * row : 8 * row + 8, :] = jnp.broadcast_to(value, (8, LANES))
        return value

    def below(edge, x, y):
        return jnp.where(lanes < edge, x, 0.0) - jnp.where(lanes == edge - 1, y, 0.0)

    def above(edge, x, y):
        return jnp.where(lanes >= edge, x, 0.0) + jnp.where(lanes == edge - 1, y, 0.0)

    cross, cross_halo = ab * down(detail, 4), ab * down(halo, 4)
    alike, alike_halo = ab * detail, ab * halo
    lane_sum(0, below(begin, cross, cross_halo))
    lane_sum(1, below(end, cross, cross_halo))
    lane_sum(
        2, jnp.where(lower, above(end, alike, alike_halo), below(begin, alike, alike_halo))
    )
    edge = -ab * wr
    lane_sum(3, jnp.where(lanes == begin - 1, edge, 0.0))
    edge_last = lane_sum(4, jnp.where(lanes == end - 1, edge, 0.0))
    lane_sum(5, jnp.where(lanes == end - 1, wr, 0.0))
    ghost = lane_sum(6, jnp.where(lanes == end, uv, 0.0))
    ghost, edge_last = jnp.broadcast_to(ghost, (8, LANES)), jnp.broadcast_to(edge_last, (8, LANES))
    part = down(ghost, 4) * edge_last
    sums[56:64, :] = 1.0 + part - down(part, 4)


def build_table(pack, sums, axis, index, n, tab):
    m = pack.shape[1]
    n1, n2 = n // 2, n // 4
    a = 2 * axis
    for row, (block, r) in {
        GA: (3, a),
        GB: (3, a + 4),
        GA2: (3, a + 1),
        GB2: (3, a + 5),
        HW1: (5, a),
        HW2: (5, a + 1),
        CA0: (0, a + 1),
        CA1: (1, a + 1),
        KAP: (2, a + 1),
        LAM: (2, a + 5),
        CB0: (0, a + 5),
        CB1: (1, a + 5),
        VN: (6, a + 4),
        UN: (6, a),
        HG: (7, a),
    }.items():
        source = 8 * block + r
        tab[row : row + 1, :] = sums[source : source + 1, :]
    where, _ = offsets(n)
    for lv, rows, suffix_name in ((0, n1, ""), (1, n2, "2")):
        col = lax.broadcasted_iota(jnp.int32, (rows, m), 1)
        sub = lax.broadcasted_iota(jnp.int32, (rows, m), 0)
        mine = col == index * rows + sub
        mine_inner = mine & (sub < rows - 1)
        for name, block, below, mask in (
            ("wl", 2, 0, mine),
            ("wr", 2, 4, mine_inner),
            ("al", 1, 0, mine),
            ("be", 1, 4, mine),
            ("u", 0, 0, mine),
            ("v", 0, 4, mine),
        ):
            r = 8 * block + below + a + lv
            values = jnp.sum(jnp.where(mask, pack[r : r + 1, :], 0.0), axis=1, keepdims=True)
            start = where[name + suffix_name]
            tab[start : start + rows, :] = jnp.broadcast_to(values, (rows, LANES))


def one_level(even, odd, tab, where, suffix, ga, gb, from_left, from_right):
    def c(name, i):
        row = where[name + suffix] + i
        return tab[row : row + 1, :]

    count = len(even)
    details = []
    for i in range(count):
        e = odd[i] - c("wl", i) * even[i]
        if i + 1 < count:
            e = e - c("wr", i) * even[i + 1]
        details.append(e)
    first = tab[ga : ga + 1, :] * even[0]
    acc = first if from_left is None else from_left + first
    lefts = []
    for i in range(count):
        lefts.append(acc)
        acc = acc + c("al", i) * details[i]
    left_end = acc
    acc = from_right
    rights = [None] * count
    for i in reversed(range(count)):
        term = c("be", i) * details[i]
        acc = term if acc is None else acc + term
        rights[i] = acc
    nodes = [even[i] + c("v", i) * lefts[i] + c("u", i) * rights[i] for i in range(count)]
    right_end = rights[0] + tab[gb : gb + 1, :] * even[0]
    return details, nodes, left_end, right_end


def single(tab, row):
    return tab[row : row + 1, :]


def summaries(tab, p1, q1, p2, q2):
    to_right = p2 + single(tab, KAP) * q1 - single(tab, CA1) * p1
    to_left = q2 + single(tab, LAM) * p1 + single(tab, CB0) * q1
    return to_right, to_left


def second_sums(tab, left, right, left2, right2, p1, q1):
    left_second = left2 + single(tab, CA0) * left + single(tab, KAP) * (q1 + right)
    right_second = right2 - single(tab, CB1) * right + single(tab, LAM) * (left + p1)
    return left_second, right_second


class Exchange:
    def __init__(self, axis, count, paired):
        self.axis, self.count, self.paired = axis, count, paired
        self.xor = count & (count - 1) == 0
        self.steps = list(range(1, count))

    def target(self, i, step):
        return i ^ step if self.xor else (i + step) % self.count

    def source(self, i, step):
        return i ^ step if self.xor else (i + self.count - step) % self.count

    def near(self, step):
        return any(self.target(i, step) == i - 1 for i in range(1, self.count))

    def send(self, step, x):
        pairs = [(i, self.target(i, step)) for i in range(self.count)]
        return lax.ppermute(x, self.axis, pairs)

    def direct(self):
        if not (self.xor and self.paired):
            return self.steps
        return [s for s in self.steps if s == 1 or s % 2 == 0]

    def carries(self, step):
        return self.near(step) or (step not in (1,) and self.passed(step) and self.near(step ^ 1))

    def passed(self, step):
        return step not in self.direct() or (step ^ 1) not in self.direct()

    def all(self, messages):
        direct = dict(zip(self.direct(), messages))
        got = {s: self.send(s, x) for s, x in direct.items()}
        for s in self.steps:
            if s not in got:
                got[s] = self.send(1, got[s ^ 1])
        return [got[s] for s in self.steps]


def x_tile(tab, where, field, n, cols, sums):
    even = [field[2 * i, cols, :] for i in range(n // 2)]
    odd = [field[2 * i + 1, cols, :] for i in range(n // 2)]
    left, right = sums if sums else (None, None)
    return one_level(even, odd, tab, where, "", GA, GB, left, right)


def first_kernel(exx, exy, n, ny, stiffness, ct, hx_ref, hy_ref, source, *refs):
    field, pack, sums, tab = refs[:4]
    messages = refs[4 : 4 + len(exx.direct())]
    hx, hy, sems, spacing_sems = refs[4 + len(exx.direct()) :]
    ex = exx
    index = lax.axis_index(exx.axis)
    tiles = ny // ct

    def fetch(t):
        cols = pl.ds(pl.multiple_of(t * ct, ct), ct)
        return pltpu.make_async_copy(source.at[:, cols, :], field.at[:, cols, :], sems.at[t])

    spacings = [
        pltpu.make_async_copy(a, b, spacing_sems.at[i])
        for i, (a, b) in enumerate(((hx_ref, hx), (hy_ref, hy)))
    ]
    for copy in spacings:
        copy.start()
    for t in range(tiles):
        fetch(t).start()
    for copy in spacings:
        copy.wait()
    lanes = 2 * pack.shape[1]
    counts = (hx.shape[1], hy.shape[1])

    def row(ref):
        x = ref[...]
        if x.shape[1] < lanes:
            x = jnp.concatenate([x, jnp.ones((1, lanes - x.shape[1]), F32)], axis=1)
        return jnp.broadcast_to(x, (8, lanes))

    is_y = (lax.broadcasted_iota(jnp.int32, (8, lanes), 0) & 2) == 2
    build_pack(
        jnp.where(is_y, row(hy), row(hx)),
        counts,
        (index, lax.axis_index(exy.axis)),
        (n, ny),
        stiffness,
        pack,
        sums,
    )
    build_table(pack, sums, 0, index, n, tab)
    where, _ = offsets(n)

    def body(t, carry):
        begin = pl.multiple_of(t * ct, ct)
        cols = pl.ds(begin, ct)
        fetch(t).wait()
        _, nodes, p1, q1 = x_tile(tab, where, field, n, cols, None)
        _, _, p2, q2 = one_level(nodes[0::2], nodes[1::2], tab, where, "2", GA2, GB2, None, None)
        p2, q2 = summaries(tab, p1, q1, p2, q2)
        for step, message in zip(ex.direct(), messages):
            upward = ex.target(index, step) > index
            message[cols, :] = jnp.where(upward, p1, q1)
            message[pl.ds(begin + ny, ct), :] = jnp.where(upward, p2, q2)
            if ex.carries(step):
                message[pl.ds(begin + 2 * ny, ct), :] = field[0, cols, :]
        return carry

    lax.fori_loop(0, tiles, body, 0)


def second_kernel(exx, exy, n, ny, ct, *refs):
    field, xtab, ytab = refs[:3]
    incoming = refs[3 : 3 + len(exx.steps)]
    rest = refs[3 + len(exx.steps) :]
    result, out, own = rest[:3]
    messages = rest[3 : 3 + len(exy.steps)]
    full, mixed, fine, sems = rest[3 + len(exy.steps) :]
    index = lax.axis_index(exx.axis)
    n1, n2 = n // 2, n // 4
    where, _ = offsets(n)

    def put(t):
        cols = pl.ds(pl.multiple_of(t * ct, ct), ct)
        return pltpu.make_async_copy(
            fine.at[:, cols, :], result.at[:, 1, cols, :], sems.at[t]
        )

    def body(t, carry):
        begin = pl.multiple_of(t * ct, ct)
        cols = pl.ds(begin, ct)
        zero = jnp.zeros((ct, LANES), F32)
        left = right = left2 = right2 = halo = zero
        for step, message in zip(exx.steps, incoming):
            source = exx.source(index, step)
            lower = source < index
            one = message[cols, :]
            two = message[pl.ds(begin + ny, ct), :]
            left = left + jnp.where(lower, one, 0.0)
            right = right + jnp.where(lower, 0.0, one)
            left2 = left2 + jnp.where(lower, two, 0.0)
            right2 = right2 + jnp.where(lower, 0.0, two)
            if exx.near(step):
                halo = jnp.where(source == index + 1, message[pl.ds(begin + 2 * ny, ct), :], halo)
        details, nodes, left_end, right_end = x_tile(xtab, where, field, n, cols, (left, right))
        details[-1] = details[-1] - single(xtab, HW1) * halo
        for i in range(n1):
            fine[i, cols, :] = details[i]
            full[pl.ds(i * ny + begin, ct), :] = nodes[i]
        put(t).start()
        ghost = single(xtab, HG) * halo + single(xtab, VN) * left_end + single(xtab, UN) * right
        left2 = left2 + single(xtab, CA0) * left + single(xtab, KAP) * right_end
        right2 = right2 - single(xtab, CB1) * right + single(xtab, LAM) * left_end
        details, nodes, _, _ = one_level(
            nodes[0::2], nodes[1::2], xtab, where, "2", GA2, GB2, left2, right2
        )
        details[-1] = details[-1] - single(xtab, HW2) * ghost
        for i in range(n2):
            mixed[pl.ds(i * ny + begin, ct), :] = nodes[i]
            mixed[pl.ds((n2 + i) * ny + begin, ct), :] = details[i]
        return carry

    lax.fori_loop(0, ny // ct, body, 0)

    m1, m2 = ny // 2, ny // 4
    ywhere, _ = offsets(ny)

    def column(ref, j):
        return ref[pl.ds(j, n1, stride=ny), :]

    for j in range(m1):
        e = column(full, 2 * j + 1) - single(ytab, ywhere["wl"] + j) * column(full, 2 * j)
        if j + 1 < m1:
            e = e - single(ytab, ywhere["wr"] + j) * column(full, 2 * j + 2)
        out[pl.ds(2 * j + 1, n1, stride=ny), :] = e
    even = [column(mixed, 2 * j) for j in range(m1)]
    odd = [column(mixed, 2 * j + 1) for j in range(m1)]
    _, nodes, p1, q1 = one_level(even, odd, ytab, ywhere, "", GA, GB, None, None)
    for j in range(m1):
        out[pl.ds(ny + 2 * j, n2, stride=2 * ny), :] = nodes[j][n2:]
    thin = [x[:n2] for x in nodes]
    details, nodes, p2, q2 = one_level(
        thin[0::2], thin[1::2], ytab, ywhere, "2", GA2, GB2, None, None
    )
    for j in range(m2):
        out[pl.ds(4 * j, n2, stride=2 * ny), :] = nodes[j]
        out[pl.ds(4 * j + 2, n2, stride=2 * ny), :] = details[j]
    p2, q2 = summaries(ytab, p1[:n2], q1[:n2], p2, q2)
    own[:n2, :] = p1[:n2]
    own[n2:, :] = q1[:n2]
    yindex = lax.axis_index(exy.axis)
    for step, message in zip(exy.steps, messages):
        upward = exy.target(yindex, step) > yindex
        message[:n1, :] = jnp.where(upward, p1, q1)
        message[n1 : n1 + n2, :] = jnp.where(upward, p2, q2)
        if exy.near(step):
            message[n1 + n2 : 2 * n1 + n2, :] = column(full, 0)
            message[2 * n1 + n2 : 2 * (n1 + n2), :] = mixed[pl.ds(0, n2, stride=ny), :]
    for t in range(ny // ct):
        put(t).wait()


def y_table_kernel(ex, ny, pack, sums, passing, tab, passed):
    build_table(pack, sums, 1, lax.axis_index(ex.axis), ny, tab)


def rank_kernel(ny, tab, ranks):
    where, _ = offsets(ny)
    m1, m2 = ny // 2, ny // 4
    ranks[...] = jnp.zeros_like(ranks)

    def put(rank, j, value):
        ranks[rank, j : j + 1, :] = value

    for rank, name, end in ((0, "v", VN), (1, "u", UN)):
        nodes = [single(tab, where[name] + i) for i in range(m1)]
        for i in range(m1):
            put(rank, 2 * i, nodes[i])
        details, nodes2, _, _ = one_level(
            nodes[0::2], nodes[1::2], tab, where, "2", GA2, GB2, None, None
        )
        details[-1] = details[-1] - single(tab, HW2) * single(tab, end)
        for i in range(m2):
            put(2 + rank, 4 * i, nodes2[i])
            put(2 + rank, 4 * i + 2, details[i])
            put(4 + rank, 4 * i, single(tab, where[name + "2"] + i))
    put(6, ny - 1, -single(tab, HW1))
    put(7, ny - 2, -single(tab, HW2))


def third_kernel(ex, n, ny, *refs):
    partial, tab, ranks, own = refs[1:5]
    incoming = refs[5 : 5 + len(ex.steps)]
    result, sums, done, sems = refs[5 + len(ex.steps) :]
    n1, n2 = n // 2, n // 4
    index = lax.axis_index(ex.axis)
    zero, zero2 = jnp.zeros((n1, LANES), F32), jnp.zeros((n2, LANES), F32)
    left, right, left2, right2, halo, halo2 = zero, zero, zero2, zero2, zero, zero2
    for step, message in zip(ex.steps, incoming):
        source = ex.source(index, step)
        lower = source < index
        one, two = message[:n1, :], message[n1 : n1 + n2, :]
        left = left + jnp.where(lower, one, 0.0)
        right = right + jnp.where(lower, 0.0, one)
        left2 = left2 + jnp.where(lower, two, 0.0)
        right2 = right2 + jnp.where(lower, 0.0, two)
        if ex.near(step):
            mine = source == index + 1
            halo = jnp.where(mine, message[n1 + n2 : 2 * n1 + n2, :], halo)
            halo2 = jnp.where(mine, message[2 * n1 + n2 : 2 * (n1 + n2), :], halo2)
    p1, q1 = own[:n2, :], own[n2:, :]
    left2, right2 = second_sums(tab, left[:n2], right[:n2], left2, right2, p1, q1)
    ghost = single(tab, HG) * halo2 + single(tab, VN) * p1
    sums[0:n1, :] = left
    sums[n1 : 2 * n1, :] = right
    sums[2 * n1 : 3 * n1, :] = halo
    sums[3 * n1 : 3 * n1 + n2, :] = left2
    sums[3 * n1 + n2 : 3 * n1 + 2 * n2, :] = right2
    sums[3 * n1 + 2 * n2 : 3 * n1 + 3 * n2, :] = ghost

    def row(i):
        return sums[i : i + 1, :]

    def put(t):
        cols = pl.ds(pl.multiple_of(t * 8, 8), 8)
        return pltpu.make_async_copy(
            done.at[:, cols, :], result.at[:, 0, cols, :], sems.at[t]
        )

    def body(t, carry):
        cols = pl.ds(pl.multiple_of(t * 8, 8), 8)
        tables = [ranks[r, cols, :] for r in range(8)]
        for k in range(n1):
            x = partial[k, cols, :] + tables[6] * row(2 * n1 + k)
            if k % 2:
                i = n2 + k // 2
                x = x + tables[0] * row(i) + tables[1] * row(n1 + i)
            else:
                i = k // 2
                x = x + tables[2] * row(i) + tables[3] * row(n1 + i)
                x = x + tables[4] * row(3 * n1 + i) + tables[5] * row(3 * n1 + n2 + i)
                x = x + tables[7] * row(3 * n1 + 2 * n2 + i)
            done[k, cols, :] = x
        put(t).start()
        return carry

    lax.fori_loop(0, ny // 8, body, 0)
    for t in range(ny // 8):
        put(t).wait()


def y_rows(ex, n, step):
    if not ex.near(step):
        return 3 * n // 4
    return 3 * n // 2 + (8 if step > 1 else 0)


def shape(*dims):
    return jax.ShapeDtypeStruct(dims, F32)


def on_device(exx, exy, field, spacing_x, spacing_y):
    n, ny, _ = field.shape
    n1, n2 = n // 2, n // 4
    ct = 16
    xrows = offsets(n)[1]
    yrows = offsets(ny)[1]
    params = pltpu.CompilerParams(vmem_limit_bytes=40 * 1024 * 1024)
    anywhere = pl.BlockSpec(memory_space=pl.ANY)
    inside = pl.BlockSpec(memory_space=pltpu.VMEM)
    dma = pltpu.SemaphoreType.DMA
    operands = (spacing_x[None], spacing_y[None], field)
    lanes = max(spacing_x.shape[0], spacing_y.shape[0])
    lanes = (lanes + 2 * LANES - 1) // (2 * LANES) * LANES
    stiffness = (float(SMOOTH_X) ** 2, float(SMOOTH_Y) ** 2)
    field, pack, sums, xtab, *outgoing = pl.pallas_call(
        functools.partial(first_kernel, exx, exy, n, ny, stiffness, ct),
        out_shape=[shape(n, ny, LANES), shape(24, lanes), shape(64, LANES), shape(xrows, LANES)]
        + [shape((3 if exx.carries(s) else 2) * ny, LANES) for s in exx.direct()],
        in_specs=[anywhere] * 3,
        scratch_shapes=[
            pltpu.VMEM((1, spacing_x.shape[0]), F32),
            pltpu.VMEM((1, spacing_y.shape[0]), F32),
            dma((ny // ct,)),
            dma((2,)),
        ],
        compiler_params=params,
        name="x_summary",
    )(*[pltpu.with_memory_space_constraint(a, pltpu.HBM) for a in operands])
    ytab, outgoing[0] = pl.pallas_call(
        functools.partial(y_table_kernel, exy, ny),
        out_shape=[shape(yrows, LANES), shape(*outgoing[0].shape)],
        in_specs=[inside, inside, anywhere],
        out_specs=[inside, anywhere],
        input_output_aliases={2: 1},
        compiler_params=params,
        name="y_table",
    )(pack, sums, outgoing[0])
    incoming = exx.all(outgoing)
    result, partial, own, *outgoing = pl.pallas_call(
        functools.partial(second_kernel, exx, exy, n, ny, ct),
        out_shape=[shape(n1, 2, ny, LANES), shape(n1 * ny, LANES), shape(2 * n2, LANES)]
        + [shape(y_rows(exy, n, s), LANES) for s in exy.steps],
        out_specs=[anywhere] + [inside] * (2 + len(exy.steps)),
        scratch_shapes=[
            pltpu.VMEM((n1 * ny, LANES), F32),
            pltpu.VMEM((n1 * ny, LANES), F32),
            pltpu.VMEM((n1, ny, LANES), F32),
            dma((ny // ct,)),
        ],
        compiler_params=params,
        name="x_transform",
    )(field, xtab, ytab, *incoming)
    ranks = pl.pallas_call(
        functools.partial(rank_kernel, ny),
        out_shape=shape(8, ny, LANES),
        compiler_params=params,
        name="y_ranks",
    )(ytab)
    incoming = exy.all(outgoing)
    result = pl.pallas_call(
        functools.partial(third_kernel, exy, n, ny),
        out_shape=shape(n1, 2, ny, LANES),
        in_specs=[anywhere] + [inside] * (4 + len(incoming)),
        out_specs=anywhere,
        input_output_aliases={0: 0},
        scratch_shapes=[
            pltpu.VMEM((3 * n1 + 3 * n2, LANES), F32),
            pltpu.VMEM((n1, ny, LANES), F32),
            dma((ny // 8,)),
        ],
        compiler_params=params,
        name="y_update",
    )(result, partial.reshape(n1, ny, LANES), ytab, ranks, own, *incoming)
    return result.reshape(n, ny, LANES)


def solution(mesh):
    exx = Exchange("gx", mesh.shape["gx"], True)
    exy = Exchange("gy", mesh.shape["gy"], False)
    placed = (P("gx", "gy", None), P(), P())
    return jax.shard_map(
        functools.partial(on_device, exx, exy),
        mesh=mesh,
        in_specs=placed,
        out_specs=P("gx", "gy", None),
        check_vma=False,
    )
```

```python
import functools

import jax
import jax.numpy as jnp
from jax import lax
from jax.experimental import pallas as pl
from jax.experimental.pallas import tpu as pltpu
from jax.sharding import PartitionSpec as P

SMOOTH_X = 48
SMOOTH_Y = 96
F32 = jnp.float32
LANES = 128

GA, GB, GA2, GB2, HW1, HW2, CA0, CA1, KAP, LAM, CB0, CB1, VN, UN, HG = range(15)
SINGLES = 16


def offsets(n):
    n1, n2 = n // 2, n // 4
    names = ["wl", "wr", "al", "be", "u", "v"]
    where, row = {}, SINGLES
    for name in names:
        where[name] = row
        row += n1
    for name in names:
        where[name + "2"] = row
        row += n2
    return where, row


def combine(left, right):
    a, b, c, d = left
    p, q, r, s = right
    return (a * p + b * r, a * q + b * s, c * p + d * r, c * q + d * s)


def gather(x, position):
    out = []
    for t in range(position.shape[1] // LANES):
        place = position[:, t * LANES : (t + 1) * LANES]
        inner, block = place & (LANES - 1), place // LANES
        picked = None
        for b in range(x.shape[1] // LANES):
            part = jnp.take_along_axis(
                x[:, b * LANES : (b + 1) * LANES], inner, axis=1, mode="promise_in_bounds"
            )
            picked = part if picked is None else jnp.where(block == b, part, picked)
        out.append(picked)
    return out[0] if len(out) == 1 else jnp.concatenate(out, axis=1)


def down(x, by):
    return pltpu.roll(x, by, 0)


def build_pack(h, counts, places, locals_, stiffness, pack, sums):
    m = h.shape[1] // 2
    lanes = lax.broadcasted_iota(jnp.int32, (8, m), 1)
    rows = lax.broadcasted_iota(jnp.int32, (8, m), 0)
    lower = rows >= 4
    is_y = (rows & 2) == 2
    second = (rows & 1) == 1

    def by_axis(pair):
        return jnp.where(is_y, pair[1], pair[0])

    count = jnp.where(second, by_axis(counts) // 4, by_axis(counts) // 2)
    real = lanes < count
    last = lanes == count - 1
    k = jnp.where(lower, count - 1 - lanes, lanes)
    k = jnp.where(real, k, 0)
    first = jnp.where(second, 4 * k, 2 * k)
    even = gather(h, first) + jnp.where(second, gather(h, first + 1), 0.0)
    odd = gather(h, jnp.where(second, first + 2, first + 1))
    odd = odd + jnp.where(second, gather(h, jnp.where(second, first + 3, first)), 0.0)
    width = even + odd
    inverse = 1.0 / width
    s = by_axis(stiffness)
    stiff = s * inverse
    across = 1.0 / (stiff - width * (1.0 / 6.0))
    same = jnp.where(real, (width * (1.0 / 3.0) + stiff) * across, 1.0)
    into = jnp.where(real, across, 0.0)
    back = jnp.where(real, (s + width * width * (1.0 / 12.0)) * across, 0.0)
    product = (same, into, back, same)
    step = 1
    while step < m:
        head = lanes < step
        shifted = [
            jnp.where(head, fill, pltpu.roll(x, step, 1))
            for x, fill in zip(product, (1.0, 0.0, 0.0, 1.0))
        ]
        product = combine(product, shifted)
        step *= 2
    w = jnp.where(lower, product[1], product[0])
    total = jnp.where(lower, product[3], product[0])[:, m - 1 : m]
    here = jnp.where(lower, count - 1 - lanes, lanes - 1)
    there = jnp.where(lower, count - 2 - lanes, lanes)
    uv = gather(w, jnp.maximum(here, 0))
    uv = jnp.where(lower, jnp.where(real, uv, 0.0), jnp.where(lanes == 0, 1.0, uv))
    uv_next = gather(w, jnp.maximum(there, 0))
    uv_next = jnp.where(lower & (lanes >= count - 1), 0.0, uv_next)
    even = jnp.where(lower, down(even, 4), even)
    odd = jnp.where(lower, down(odd, 4), odd)
    inverse = jnp.where(lower, down(inverse, 4), inverse)
    ab = jnp.where(real, (uv * even + uv_next * odd) * (0.5 / total), 0.0)
    weight = jnp.where(lower, even, odd) * inverse
    weight = jnp.where(last, jnp.where(lower, 0.0, 1.0), weight)
    weight = jnp.where(real, weight, 0.0)
    pack[0:8, :] = uv
    pack[8:16, :] = ab
    pack[16:24, :] = weight
    other = down(weight, 4)
    wl = jnp.where(lower, other, weight)
    wr = jnp.where(lower, weight, other)
    fine = down(uv, 1)
    twice = jnp.where(real & second, 2 * lanes, 0)
    halo = -wr * gather(fine, jnp.minimum(twice + 2, m - 1))
    detail = gather(fine, twice + 1) - wl * gather(fine, twice) + halo
    valid = real & second
    halo = jnp.where(valid, halo, 0.0)
    detail = jnp.where(valid, detail, 0.0)
    place = by_axis(places)
    local = jnp.where(second, by_axis(locals_) // 4, by_axis(locals_) // 2)
    begin, end = place * local, (place + 1) * local

    def lane_sum(row, x):
        value = jnp.sum(x, axis=1, keepdims=True)
        sums[8 * row : 8 * row + 8, :] = jnp.broadcast_to(value, (8, LANES))
        return value

    def below(edge, x, y):
        return jnp.where(lanes < edge, x, 0.0) - jnp.where(lanes == edge - 1, y, 0.0)

    def above(edge, x, y):
        return jnp.where(lanes >= edge, x, 0.0) + jnp.where(lanes == edge - 1, y, 0.0)

    cross, cross_halo = ab * down(detail, 4), ab * down(halo, 4)
    alike, alike_halo = ab * detail, ab * halo
    lane_sum(0, below(begin, cross, cross_halo))
    lane_sum(1, below(end, cross, cross_halo))
    lane_sum(
        2, jnp.where(lower, above(end, alike, alike_halo), below(begin, alike, alike_halo))
    )
    edge = -ab * wr
    lane_sum(3, jnp.where(lanes == begin - 1, edge, 0.0))
    edge_last = lane_sum(4, jnp.where(lanes == end - 1, edge, 0.0))
    lane_sum(5, jnp.where(lanes == end - 1, wr, 0.0))
    ghost = lane_sum(6, jnp.where(lanes == end, uv, 0.0))
    ghost, edge_last = jnp.broadcast_to(ghost, (8, LANES)), jnp.broadcast_to(edge_last, (8, LANES))
    part = down(ghost, 4) * edge_last
    sums[56:64, :] = 1.0 + part - down(part, 4)


def build_table(pack, sums, axis, index, n, tab):
    m = pack.shape[1]
    n1, n2 = n // 2, n // 4
    a = 2 * axis
    for row, (block, r) in {
        GA: (3, a),
        GB: (3, a + 4),
        GA2: (3, a + 1),
        GB2: (3, a + 5),
        HW1: (5, a),
        HW2: (5, a + 1),
        CA0: (0, a + 1),
        CA1: (1, a + 1),
        KAP: (2, a + 1),
        LAM: (2, a + 5),
        CB0: (0, a + 5),
        CB1: (1, a + 5),
        VN: (6, a + 4),
        UN: (6, a),
        HG: (7, a),
    }.items():
        source = 8 * block + r
        tab[row : row + 1, :] = sums[source : source + 1, :]
    where, _ = offsets(n)
    for lv, rows, suffix_name in ((0, n1, ""), (1, n2, "2")):
        col = lax.broadcasted_iota(jnp.int32, (rows, m), 1)
        sub = lax.broadcasted_iota(jnp.int32, (rows, m), 0)
        mine = col == index * rows + sub
        mine_inner = mine & (sub < rows - 1)
        for name, block, below, mask in (
            ("wl", 2, 0, mine),
            ("wr", 2, 4, mine_inner),
            ("al", 1, 0, mine),
            ("be", 1, 4, mine),
            ("u", 0, 0, mine),
            ("v", 0, 4, mine),
        ):
            r = 8 * block + below + a + lv
            values = jnp.sum(jnp.where(mask, pack[r : r + 1, :], 0.0), axis=1, keepdims=True)
            start = where[name + suffix_name]
            tab[start : start + rows, :] = jnp.broadcast_to(values, (rows, LANES))


def one_level(even, odd, tab, where, suffix, ga, gb, from_left, from_right):
    def c(name, i):
        row = where[name + suffix] + i
        return tab[row : row + 1, :]

    count = len(even)
    details = []
    for i in range(count):
        e = odd[i] - c("wl", i) * even[i]
        if i + 1 < count:
            e = e - c("wr", i) * even[i + 1]
        details.append(e)
    first = tab[ga : ga + 1, :] * even[0]
    acc = first if from_left is None else from_left + first
    lefts = []
    for i in range(count):
        lefts.append(acc)
        acc = acc + c("al", i) * details[i]
    left_end = acc
    acc = from_right
    rights = [None] * count
    for i in reversed(range(count)):
        term = c("be", i) * details[i]
        acc = term if acc is None else acc + term
        rights[i] = acc
    nodes = [even[i] + c("v", i) * lefts[i] + c("u", i) * rights[i] for i in range(count)]
    right_end = rights[0] + tab[gb : gb + 1, :] * even[0]
    return details, nodes, left_end, right_end


def single(tab, row):
    return tab[row : row + 1, :]


def summaries(tab, p1, q1, p2, q2):
    to_right = p2 + single(tab, KAP) * q1 - single(tab, CA1) * p1
    to_left = q2 + single(tab, LAM) * p1 + single(tab, CB0) * q1
    return to_right, to_left


def second_sums(tab, left, right, left2, right2, p1, q1):
    left_second = left2 + single(tab, CA0) * left + single(tab, KAP) * (q1 + right)
    right_second = right2 - single(tab, CB1) * right + single(tab, LAM) * (left + p1)
    return left_second, right_second


class Exchange:
    def __init__(self, axis, count, paired):
        self.axis, self.count, self.paired = axis, count, paired
        self.xor = count & (count - 1) == 0
        self.steps = list(range(1, count))

    def target(self, i, step):
        return i ^ step if self.xor else (i + step) % self.count

    def source(self, i, step):
        return i ^ step if self.xor else (i + self.count - step) % self.count

    def near(self, step):
        return any(self.target(i, step) == i - 1 for i in range(1, self.count))

    def send(self, step, x):
        pairs = [(i, self.target(i, step)) for i in range(self.count)]
        return lax.ppermute(x, self.axis, pairs)

    def direct(self):
        if not (self.xor and self.paired):
            return self.steps
        return [s for s in self.steps if s == 1 or s % 2 == 0]

    def carries(self, step):
        return self.near(step) or (step not in (1,) and self.passed(step) and self.near(step ^ 1))

    def passed(self, step):
        return step not in self.direct() or (step ^ 1) not in self.direct()

    def all(self, messages):
        direct = dict(zip(self.direct(), messages))
        got = {s: self.send(s, x) for s, x in direct.items()}
        for s in self.steps:
            if s not in got:
                got[s] = self.send(1, got[s ^ 1])
        return [got[s] for s in self.steps]


def x_tile(tab, where, field, n, cols, sums):
    even = [field[2 * i, cols, :] for i in range(n // 2)]
    odd = [field[2 * i + 1, cols, :] for i in range(n // 2)]
    left, right = sums if sums else (None, None)
    return one_level(even, odd, tab, where, "", GA, GB, left, right)


def first_kernel(exx, exy, n, ny, stiffness, ct, hx_ref, hy_ref, source, *refs):
    field, pack, sums, tab, own = refs[:5]
    messages = refs[5 : 5 + len(exx.direct())]
    hx, hy, sems, spacing_sems = refs[5 + len(exx.direct()) :]
    ex = exx
    index = lax.axis_index(exx.axis)
    tiles = ny // ct

    def fetch(t):
        cols = pl.ds(pl.multiple_of(t * ct, ct), ct)
        return pltpu.make_async_copy(source.at[:, cols, :], field.at[:, cols, :], sems.at[t])

    spacings = [
        pltpu.make_async_copy(a, b, spacing_sems.at[i])
        for i, (a, b) in enumerate(((hx_ref, hx), (hy_ref, hy)))
    ]
    for copy in spacings:
        copy.start()
    for t in range(tiles):
        fetch(t).start()
    for copy in spacings:
        copy.wait()
    lanes = 2 * pack.shape[1]
    counts = (hx.shape[1], hy.shape[1])

    def row(ref):
        x = ref[...]
        if x.shape[1] < lanes:
            x = jnp.concatenate([x, jnp.ones((1, lanes - x.shape[1]), F32)], axis=1)
        return jnp.broadcast_to(x, (8, lanes))

    is_y = (lax.broadcasted_iota(jnp.int32, (8, lanes), 0) & 2) == 2
    build_pack(
        jnp.where(is_y, row(hy), row(hx)),
        counts,
        (index, lax.axis_index(exy.axis)),
        (n, ny),
        stiffness,
        pack,
        sums,
    )
    build_table(pack, sums, 0, index, n, tab)
    where, _ = offsets(n)

    def body(t, carry):
        begin = pl.multiple_of(t * ct, ct)
        cols = pl.ds(begin, ct)
        fetch(t).wait()
        _, nodes, p1, q1 = x_tile(tab, where, field, n, cols, None)
        _, _, p2, q2 = one_level(nodes[0::2], nodes[1::2], tab, where, "2", GA2, GB2, None, None)
        p2, q2 = summaries(tab, p1, q1, p2, q2)
        own[cols, :] = p1
        own[pl.ds(begin + ny, ct), :] = q1
        for step, message in zip(ex.direct(), messages):
            upward = ex.target(index, step) > index
            message[cols, :] = jnp.where(upward, p1, q1)
            message[pl.ds(begin + ny, ct), :] = jnp.where(upward, p2, q2)
            if ex.carries(step):
                message[pl.ds(begin + 2 * ny, ct), :] = field[0, cols, :]
        return carry

    lax.fori_loop(0, tiles, body, 0)


def column(ref, j, count, ny):
    return ref[pl.ds(j, count, stride=ny), :]


def local_kernel(exy, n, ny, ct, field, xtab, pack, sums, passing, *refs):
    ytab, shares, fine, out, local, passed, full, mixed = refs
    n1, n2 = n // 2, n // 4
    where, _ = offsets(n)
    build_table(pack, sums, 1, lax.axis_index(exy.axis), ny, ytab)

    for r, name in enumerate(("v", "u")):
        nodes = [single(xtab, where[name] + i) for i in range(n1)]
        details, nodes, _, _ = one_level(
            nodes[0::2], nodes[1::2], xtab, where, "2", GA2, GB2, None, None
        )
        for i in range(n2):
            shares[r * n2 + i : r * n2 + i + 1, :] = nodes[i]
            shares[(2 + r) * n2 + i : (2 + r) * n2 + i + 1, :] = details[i]

    def body(t, carry):
        begin = pl.multiple_of(t * ct, ct)
        cols = pl.ds(begin, ct)
        details, nodes, _, _ = x_tile(xtab, where, field, n, cols, None)
        for i in range(n1):
            fine[i, cols, :] = details[i]
            full[pl.ds(i * ny + begin, ct), :] = nodes[i]
        details, nodes, _, _ = one_level(
            nodes[0::2], nodes[1::2], xtab, where, "2", GA2, GB2, None, None
        )
        for i in range(n2):
            mixed[pl.ds(i * ny + begin, ct), :] = nodes[i]
            mixed[pl.ds((n2 + i) * ny + begin, ct), :] = details[i]
        return carry

    lax.fori_loop(0, ny // ct, body, 0)

    m1, m2 = ny // 2, ny // 4
    ywhere, _ = offsets(ny)
    for j in range(m1):
        e = column(full, 2 * j + 1, n1, ny)
        e = e - single(ytab, ywhere["wl"] + j) * column(full, 2 * j, n1, ny)
        if j + 1 < m1:
            e = e - single(ytab, ywhere["wr"] + j) * column(full, 2 * j + 2, n1, ny)
        out[pl.ds(2 * j + 1, n1, stride=ny), :] = e
    even = [column(mixed, 2 * j, n1, ny) for j in range(m1)]
    odd = [column(mixed, 2 * j + 1, n1, ny) for j in range(m1)]
    _, nodes, p1, q1 = one_level(even, odd, ytab, ywhere, "", GA, GB, None, None)
    for j in range(m1):
        out[pl.ds(ny + 2 * j, n2, stride=2 * ny), :] = nodes[j][n2:]
    thin = [x[:n2] for x in nodes]
    details, nodes, p2, q2 = one_level(
        thin[0::2], thin[1::2], ytab, ywhere, "2", GA2, GB2, None, None
    )
    for j in range(m2):
        out[pl.ds(4 * j, n2, stride=2 * ny), :] = nodes[j]
        out[pl.ds(4 * j + 2, n2, stride=2 * ny), :] = details[j]
    p2, q2 = summaries(ytab, p1[:n2], q1[:n2], p2, q2)
    local[:n1, :] = p1
    local[n1 : n1 + n2, :] = p2
    local[n1 + n2 : 2 * n1 + n2, :] = q1
    local[2 * n1 + n2 : 3 * n1, :] = q2
    local[3 * n1 : 4 * n1, :] = column(full, 0, n1, ny)
    local[4 * n1 :, :] = column(mixed, 0, n2, ny)


LEFT, RIGHT, LEFT2, RIGHT2, GHOST, HALO, ARRIVED = 0, 1, 2, 3, 4, 5, 8


def arrived_y(ytab, arrived, ny):
    m1 = ny // 2
    where, _ = offsets(ny)
    even = [column(arrived, 2 * j, ARRIVED, ny) for j in range(m1)]
    odd = [column(arrived, 2 * j + 1, ARRIVED, ny) for j in range(m1)]
    details, nodes, p1, q1 = one_level(even, odd, ytab, where, "", GA, GB, None, None)
    details2, nodes2, p2, q2 = one_level(
        nodes[0::2], nodes[1::2], ytab, where, "2", GA2, GB2, None, None
    )
    return details, nodes, details2, nodes2, p1, q1, p2, q2


def second_kernel(exx, exy, n, ny, ct, *refs):
    own, xtab, shares, ytab, local = refs[:5]
    incoming = refs[5 : 5 + len(exx.steps)]
    arrived, yown = refs[5 + len(exx.steps) : 7 + len(exx.steps)]
    messages = refs[7 + len(exx.steps) :]
    index = lax.axis_index(exx.axis)
    n1, n2 = n // 2, n // 4
    where, _ = offsets(n)

    def body(t, carry):
        begin = pl.multiple_of(t * ct, ct)
        cols = pl.ds(begin, ct)
        zero = jnp.zeros((ct, LANES), F32)
        left = right = left2 = right2 = halo = zero
        for step, message in zip(exx.steps, incoming):
            source = exx.source(index, step)
            lower = source < index
            one = message[cols, :]
            two = message[pl.ds(begin + ny, ct), :]
            left = left + jnp.where(lower, one, 0.0)
            right = right + jnp.where(lower, 0.0, one)
            left2 = left2 + jnp.where(lower, two, 0.0)
            right2 = right2 + jnp.where(lower, 0.0, two)
            if exx.near(step):
                halo = jnp.where(source == index + 1, message[pl.ds(begin + 2 * ny, ct), :], halo)
        p1, q1 = own[cols, :], own[pl.ds(begin + ny, ct), :]
        left2, right2 = second_sums(xtab, left, right, left2, right2, p1, q1)
        ghost = single(xtab, HG) * halo + single(xtab, VN) * (left + p1) + single(xtab, UN) * right
        for row, value in (
            (LEFT, left),
            (RIGHT, right),
            (LEFT2, left2),
            (RIGHT2, right2),
            (GHOST, ghost),
            (HALO, halo),
            (HALO + 1, zero),
            (HALO + 2, zero),
        ):
            arrived[pl.ds(row * ny + begin, ct), :] = value
        return carry

    lax.fori_loop(0, ny // ct, body, 0)
    _, _, _, _, p1, q1, p2, q2 = arrived_y(ytab, arrived, ny)
    p2, q2 = summaries(ytab, p1, q1, p2, q2)
    first = column(arrived, 0, ARRIVED, ny)
    nodes_v, nodes_u = shares[:n2, :], shares[n2 : 2 * n2, :]
    details_v, details_u = shares[2 * n2 : 3 * n2, :], shares[3 * n2 :, :]

    def rows(name, count):
        return xtab[where[name] : where[name] + count, :]

    def coarse(x):
        return (
            nodes_v * x[LEFT : LEFT + 1]
            + nodes_u * x[RIGHT : RIGHT + 1]
            + rows("v2", n2) * x[LEFT2 : LEFT2 + 1]
            + rows("u2", n2) * x[RIGHT2 : RIGHT2 + 1]
        )

    is_last = lax.broadcasted_iota(jnp.int32, (n2, LANES), 0) == n2 - 1

    def detail(x):
        ghost = jnp.where(is_last, single(xtab, HW2) * x[GHOST : GHOST + 1], 0.0)
        return details_v * x[LEFT : LEFT + 1] + details_u * x[RIGHT : RIGHT + 1] - ghost

    p1c, p1d = local[:n2, :] + coarse(p1), local[n2:n1, :] + detail(p1)
    p2c = local[n1 : n1 + n2, :] + coarse(p2)
    q1c = local[n1 + n2 : 2 * n1, :] + coarse(q1)
    q1d = local[2 * n1 : 2 * n1 + n2, :] + detail(q1)
    q2c = local[2 * n1 + n2 : 3 * n1, :] + coarse(q2)
    yown[:n2, :] = p1c
    yown[n2:, :] = q1c
    yindex = lax.axis_index(exy.axis)
    for step, message in zip(exy.steps, messages):
        upward = exy.target(yindex, step) > yindex
        message[:n2, :] = jnp.where(upward, p1c, q1c)
        message[n2:n1, :] = jnp.where(upward, p1d, q1d)
        message[n1 : n1 + n2, :] = jnp.where(upward, p2c, q2c)
        if exy.near(step):
            message[n1 + n2 : 2 * n1 + n2, :] = (
                local[3 * n1 : 4 * n1, :]
                + rows("v", n1) * first[LEFT : LEFT + 1]
                + rows("u", n1) * first[RIGHT : RIGHT + 1]
            )
            message[2 * n1 + n2 : 2 * (n1 + n2), :] = local[4 * n1 :, :] + coarse(first)


def share_kernel(n, ny, own_part, fine, arrived, xtab, shares, ytab, result, out, *refs):
    last, one, two, blend, sems = refs
    n1, n2 = n // 2, n // 4
    m1, m2 = ny // 2, ny // 4
    where, _ = offsets(n)
    last[...] = fine[n1 - 1] - single(xtab, HW1) * arrived[HALO * ny : (HALO + 1) * ny, :]
    copies = [
        pltpu.make_async_copy(fine.at[: n1 - 1], result.at[: n1 - 1, 1], sems.at[0]),
        pltpu.make_async_copy(last, result.at[n1 - 1, 1], sems.at[1]),
    ]
    for copy in copies:
        copy.start()
    details, nodes, details2, nodes2, _, _, _, _ = arrived_y(ytab, arrived, ny)
    side = lax.broadcasted_iota(jnp.int32, (ARRIVED, LANES), 0) < LEFT2
    for j in range(m1):
        at = pl.ds(2 * j + 1, ARRIVED, stride=ny)
        one[at, :] = details[j]
        two[at, :] = jnp.where(side, details[j], 0.0)
        one[pl.ds(2 * j, ARRIVED, stride=ny), :] = nodes[j]
    for j in range(m2):
        two[pl.ds(4 * j, ARRIVED, stride=ny), :] = nodes2[j]
        two[pl.ds(4 * j + 2, ARRIVED, stride=ny), :] = details2[j]
    odd = (lax.broadcasted_iota(jnp.int32, (8, LANES), 0) & 1) == 1
    for k in range(n1):
        for r, name in enumerate(("v", "u")):
            block = (2 + r if k % 2 else r) * n2 + k // 2
            mixture = jnp.where(odd, single(xtab, where[name] + k), single(shares, block))
            blend[16 * k + 8 * r : 16 * k + 8 * r + 8, :] = mixture

    def body(t, carry):
        begin = pl.multiple_of(t * 8, 8)
        cols = pl.ds(begin, 8)

        def tile(ref, r):
            return ref[pl.ds(r * ny + begin, 8), :]

        ones = [tile(one, r) for r in (LEFT, RIGHT)]
        twos = [tile(two, r) for r in (LEFT, RIGHT, LEFT2, RIGHT2)]
        ghost = jnp.where(odd, 0.0, single(xtab, HW2) * tile(one, GHOST))
        for k in range(n1):
            x = own_part[k, cols, :]
            source = ones if k % 2 else twos
            for r in range(2):
                x = x + blend[16 * k + 8 * r : 16 * k + 8 * r + 8, :] * source[r]
            if k % 2 == 0:
                x = x + single(xtab, where["v2"] + k // 2) * twos[2]
                x = x + single(xtab, where["u2"] + k // 2) * twos[3]
            elif k == n1 - 1:
                x = x - ghost
            out[k, cols, :] = x
        return carry

    lax.fori_loop(0, ny // 8, body, 0)
    for copy in copies:
        copy.wait()


def rank_kernel(ny, tab, ranks):
    where, _ = offsets(ny)
    m1, m2 = ny // 2, ny // 4
    ranks[...] = jnp.zeros_like(ranks)

    def put(rank, j, value):
        ranks[rank, j : j + 1, :] = value

    for rank, name, end in ((0, "v", VN), (1, "u", UN)):
        nodes = [single(tab, where[name] + i) for i in range(m1)]
        for i in range(m1):
            put(rank, 2 * i, nodes[i])
        details, nodes2, _, _ = one_level(
            nodes[0::2], nodes[1::2], tab, where, "2", GA2, GB2, None, None
        )
        details[-1] = details[-1] - single(tab, HW2) * single(tab, end)
        for i in range(m2):
            put(2 + rank, 4 * i, nodes2[i])
            put(2 + rank, 4 * i + 2, details[i])
            put(4 + rank, 4 * i, single(tab, where[name + "2"] + i))
    put(6, ny - 1, -single(tab, HW1))
    put(7, ny - 2, -single(tab, HW2))


def third_kernel(ex, n, ny, *refs):
    partial, tab, ranks, own = refs[1:5]
    incoming = refs[5 : 5 + len(ex.steps)]
    result, sums, done, sems = refs[5 + len(ex.steps) :]
    n1, n2 = n // 2, n // 4
    index = lax.axis_index(ex.axis)
    zero, zero2 = jnp.zeros((n1, LANES), F32), jnp.zeros((n2, LANES), F32)
    left, right, left2, right2, halo, halo2 = zero, zero, zero2, zero2, zero, zero2
    for step, message in zip(ex.steps, incoming):
        source = ex.source(index, step)
        lower = source < index
        one, two = message[:n1, :], message[n1 : n1 + n2, :]
        left = left + jnp.where(lower, one, 0.0)
        right = right + jnp.where(lower, 0.0, one)
        left2 = left2 + jnp.where(lower, two, 0.0)
        right2 = right2 + jnp.where(lower, 0.0, two)
        if ex.near(step):
            mine = source == index + 1
            halo = jnp.where(mine, message[n1 + n2 : 2 * n1 + n2, :], halo)
            halo2 = jnp.where(mine, message[2 * n1 + n2 : 2 * (n1 + n2), :], halo2)
    p1, q1 = own[:n2, :], own[n2:, :]
    left2, right2 = second_sums(tab, left[:n2], right[:n2], left2, right2, p1, q1)
    ghost = single(tab, HG) * halo2 + single(tab, VN) * p1
    sums[0:n1, :] = left
    sums[n1 : 2 * n1, :] = right
    sums[2 * n1 : 3 * n1, :] = halo
    sums[3 * n1 : 3 * n1 + n2, :] = left2
    sums[3 * n1 + n2 : 3 * n1 + 2 * n2, :] = right2
    sums[3 * n1 + 2 * n2 : 3 * n1 + 3 * n2, :] = ghost

    def row(i):
        return sums[i : i + 1, :]

    def put(t):
        cols = pl.ds(pl.multiple_of(t * 8, 8), 8)
        return pltpu.make_async_copy(
            done.at[:, cols, :], result.at[:, 0, cols, :], sems.at[t]
        )

    def body(t, carry):
        cols = pl.ds(pl.multiple_of(t * 8, 8), 8)
        tables = [ranks[r, cols, :] for r in range(8)]
        for k in range(n1):
            x = partial[k, cols, :] + tables[6] * row(2 * n1 + k)
            if k % 2:
                i = n2 + k // 2
                x = x + tables[0] * row(i) + tables[1] * row(n1 + i)
            else:
                i = k // 2
                x = x + tables[2] * row(i) + tables[3] * row(n1 + i)
                x = x + tables[4] * row(3 * n1 + i) + tables[5] * row(3 * n1 + n2 + i)
                x = x + tables[7] * row(3 * n1 + 2 * n2 + i)
            done[k, cols, :] = x
        put(t).start()
        return carry

    lax.fori_loop(0, ny // 8, body, 0)
    for t in range(ny // 8):
        put(t).wait()


def y_rows(ex, n, step):
    if not ex.near(step):
        return 3 * n // 4
    return 3 * n // 2 + (8 if step > 1 else 0)


def shape(*dims):
    return jax.ShapeDtypeStruct(dims, F32)


def on_device(exx, exy, field, spacing_x, spacing_y):
    n, ny, _ = field.shape
    n1, n2 = n // 2, n // 4
    ct = 16
    xrows = offsets(n)[1]
    yrows = offsets(ny)[1]
    params = pltpu.CompilerParams(vmem_limit_bytes=40 * 1024 * 1024)
    anywhere = pl.BlockSpec(memory_space=pl.ANY)
    inside = pl.BlockSpec(memory_space=pltpu.VMEM)
    dma = pltpu.SemaphoreType.DMA
    operands = (spacing_x[None], spacing_y[None], field)
    lanes = max(spacing_x.shape[0], spacing_y.shape[0])
    lanes = (lanes + 2 * LANES - 1) // (2 * LANES) * LANES
    stiffness = (float(SMOOTH_X) ** 2, float(SMOOTH_Y) ** 2)
    field, pack, sums, xtab, xown, *outgoing = pl.pallas_call(
        functools.partial(first_kernel, exx, exy, n, ny, stiffness, ct),
        out_shape=[shape(n, ny, LANES), shape(24, lanes), shape(64, LANES)]
        + [shape(xrows, LANES), shape(2 * ny, LANES)]
        + [shape((3 if exx.carries(s) else 2) * ny, LANES) for s in exx.direct()],
        in_specs=[anywhere] * 3,
        scratch_shapes=[
            pltpu.VMEM((1, spacing_x.shape[0]), F32),
            pltpu.VMEM((1, spacing_y.shape[0]), F32),
            dma((ny // ct,)),
            dma((2,)),
        ],
        compiler_params=params,
        name="x_summary",
    )(*[pltpu.with_memory_space_constraint(a, pltpu.HBM) for a in operands])
    block = shape(n1, ny, LANES)
    lines = pltpu.VMEM((n1 * ny, LANES), F32)
    ytab, shares, fine, local_out, local, outgoing[0] = pl.pallas_call(
        functools.partial(local_kernel, exy, n, ny, ct),
        out_shape=[shape(yrows, LANES), shape(4 * n2, LANES), block, shape(n1 * ny, LANES)]
        + [shape(4 * n1 + n2, LANES), shape(*outgoing[0].shape)],
        in_specs=[inside] * 4 + [anywhere],
        out_specs=[inside] * 5 + [anywhere],
        input_output_aliases={4: 5},
        scratch_shapes=[lines, lines],
        compiler_params=params,
        name="local_transform",
    )(field, xtab, pack, sums, outgoing[0])
    incoming = exx.all(outgoing)
    arrived, own, *outgoing = pl.pallas_call(
        functools.partial(second_kernel, exx, exy, n, ny, ct),
        out_shape=[shape(ARRIVED * ny, LANES), shape(2 * n2, LANES)]
        + [shape(y_rows(exy, n, s), LANES) for s in exy.steps],
        compiler_params=params,
        name="x_arrived",
    )(xown, xtab, shares, ytab, local, *incoming)
    some = pltpu.VMEM((ARRIVED * ny, LANES), F32)
    result, partial = pl.pallas_call(
        functools.partial(share_kernel, n, ny),
        out_shape=[shape(n1, 2, ny, LANES), block],
        out_specs=[anywhere, inside],
        scratch_shapes=[
            pltpu.VMEM((ny, LANES), F32),
            some,
            some,
            pltpu.VMEM((16 * n1, LANES), F32),
            dma((2,)),
        ],
        compiler_params=params,
        name="x_share",
    )(local_out.reshape(n1, ny, LANES), fine, arrived, xtab, shares, ytab)
    ranks = pl.pallas_call(
        functools.partial(rank_kernel, ny),
        out_shape=shape(8, ny, LANES),
        compiler_params=params,
        name="y_ranks",
    )(ytab)
    incoming = exy.all(outgoing)
    result = pl.pallas_call(
        functools.partial(third_kernel, exy, n, ny),
        out_shape=shape(n1, 2, ny, LANES),
        in_specs=[anywhere] + [inside] * (4 + len(incoming)),
        out_specs=anywhere,
        input_output_aliases={0: 0},
        scratch_shapes=[
            pltpu.VMEM((3 * n1 + 3 * n2, LANES), F32),
            pltpu.VMEM((n1, ny, LANES), F32),
            dma((ny // 8,)),
        ],
        compiler_params=params,
        name="y_update",
    )(result, partial, ytab, ranks, own, *incoming)
    return result.reshape(n, ny, LANES)


def solution(mesh):
    exx = Exchange("gx", mesh.shape["gx"], True)
    exy = Exchange("gy", mesh.shape["gy"], False)
    placed = (P("gx", "gy", None), P(), P())
    return jax.shard_map(
        functools.partial(on_device, exx, exy),
        mesh=mesh,
        in_specs=placed,
        out_specs=P("gx", "gy", None),
        check_vma=False,
    )
```

```python
import functools

import jax
import jax.numpy as jnp
from jax import lax
from jax.experimental import pallas as pl
from jax.experimental.pallas import tpu as pltpu
from jax.sharding import PartitionSpec as P

SMOOTH_X = 48
SMOOTH_Y = 96
F32 = jnp.float32
LANES = 128

GA, GB, GA2, GB2, HW1, HW2, CA0, CA1, KAP, LAM, CB0, CB1, VN, UN, HG = range(15)
SINGLES = 16


def offsets(n):
    n1, n2 = n // 2, n // 4
    names = ["wl", "wr", "al", "be", "u", "v"]
    where, row = {}, SINGLES
    for name in names:
        where[name] = row
        row += n1
    for name in names:
        where[name + "2"] = row
        row += n2
    return where, row


def combine(left, right):
    a, b, c, d = left
    p, q, r, s = right
    return (a * p + b * r, a * q + b * s, c * p + d * r, c * q + d * s)


def gather(x, position):
    out = []
    for t in range(position.shape[1] // LANES):
        place = position[:, t * LANES : (t + 1) * LANES]
        inner, block = place & (LANES - 1), place // LANES
        picked = None
        for b in range(x.shape[1] // LANES):
            part = jnp.take_along_axis(
                x[:, b * LANES : (b + 1) * LANES], inner, axis=1, mode="promise_in_bounds"
            )
            picked = part if picked is None else jnp.where(block == b, part, picked)
        out.append(picked)
    return out[0] if len(out) == 1 else jnp.concatenate(out, axis=1)


def down(x, by):
    return pltpu.roll(x, by, 0)


def build_pack(h, counts, places, locals_, stiffness, pack, sums):
    m = h.shape[1] // 2
    lanes = lax.broadcasted_iota(jnp.int32, (8, m), 1)
    rows = lax.broadcasted_iota(jnp.int32, (8, m), 0)
    lower = rows >= 4
    is_y = (rows & 2) == 2
    second = (rows & 1) == 1

    def by_axis(pair):
        return jnp.where(is_y, pair[1], pair[0])

    count = jnp.where(second, by_axis(counts) // 4, by_axis(counts) // 2)
    real = lanes < count
    last = lanes == count - 1
    k = jnp.where(lower, count - 1 - lanes, lanes)
    k = jnp.where(real, k, 0)
    first = jnp.where(second, 4 * k, 2 * k)
    even = gather(h, first) + jnp.where(second, gather(h, first + 1), 0.0)
    odd = gather(h, jnp.where(second, first + 2, first + 1))
    odd = odd + jnp.where(second, gather(h, jnp.where(second, first + 3, first)), 0.0)
    width = even + odd
    inverse = 1.0 / width
    s = by_axis(stiffness)
    stiff = s * inverse
    across = 1.0 / (stiff - width * (1.0 / 6.0))
    same = jnp.where(real, (width * (1.0 / 3.0) + stiff) * across, 1.0)
    into = jnp.where(real, across, 0.0)
    back = jnp.where(real, (s + width * width * (1.0 / 12.0)) * across, 0.0)
    product = (same, into, back, same)
    step = 1
    while step < m:
        head = lanes < step
        shifted = [
            jnp.where(head, fill, pltpu.roll(x, step, 1))
            for x, fill in zip(product, (1.0, 0.0, 0.0, 1.0))
        ]
        product = combine(product, shifted)
        step *= 2
    w = jnp.where(lower, product[1], product[0])
    total = jnp.where(lower, product[3], product[0])[:, m - 1 : m]
    here = jnp.where(lower, count - 1 - lanes, lanes - 1)
    there = jnp.where(lower, count - 2 - lanes, lanes)
    uv = gather(w, jnp.maximum(here, 0))
    uv = jnp.where(lower, jnp.where(real, uv, 0.0), jnp.where(lanes == 0, 1.0, uv))
    uv_next = gather(w, jnp.maximum(there, 0))
    uv_next = jnp.where(lower & (lanes >= count - 1), 0.0, uv_next)
    even = jnp.where(lower, down(even, 4), even)
    odd = jnp.where(lower, down(odd, 4), odd)
    inverse = jnp.where(lower, down(inverse, 4), inverse)
    ab = jnp.where(real, (uv * even + uv_next * odd) * (0.5 / total), 0.0)
    weight = jnp.where(lower, even, odd) * inverse
    weight = jnp.where(last, jnp.where(lower, 0.0, 1.0), weight)
    weight = jnp.where(real, weight, 0.0)
    pack[0:8, :] = uv
    pack[8:16, :] = ab
    pack[16:24, :] = weight
    other = down(weight, 4)
    wl = jnp.where(lower, other, weight)
    wr = jnp.where(lower, weight, other)
    fine = down(uv, 1)
    twice = jnp.where(real & second, 2 * lanes, 0)
    halo = -wr * gather(fine, jnp.minimum(twice + 2, m - 1))
    detail = gather(fine, twice + 1) - wl * gather(fine, twice) + halo
    valid = real & second
    halo = jnp.where(valid, halo, 0.0)
    detail = jnp.where(valid, detail, 0.0)
    place = by_axis(places)
    local = jnp.where(second, by_axis(locals_) // 4, by_axis(locals_) // 2)
    begin, end = place * local, (place + 1) * local

    def lane_sum(row, x):
        value = jnp.sum(x, axis=1, keepdims=True)
        sums[8 * row : 8 * row + 8, :] = jnp.broadcast_to(value, (8, LANES))
        return value

    def below(edge, x, y):
        return jnp.where(lanes < edge, x, 0.0) - jnp.where(lanes == edge - 1, y, 0.0)

    def above(edge, x, y):
        return jnp.where(lanes >= edge, x, 0.0) + jnp.where(lanes == edge - 1, y, 0.0)

    cross, cross_halo = ab * down(detail, 4), ab * down(halo, 4)
    alike, alike_halo = ab * detail, ab * halo
    lane_sum(0, below(begin, cross, cross_halo))
    lane_sum(1, below(end, cross, cross_halo))
    lane_sum(
        2, jnp.where(lower, above(end, alike, alike_halo), below(begin, alike, alike_halo))
    )
    edge = -ab * wr
    lane_sum(3, jnp.where(lanes == begin - 1, edge, 0.0))
    edge_last = lane_sum(4, jnp.where(lanes == end - 1, edge, 0.0))
    lane_sum(5, jnp.where(lanes == end - 1, wr, 0.0))
    ghost = lane_sum(6, jnp.where(lanes == end, uv, 0.0))
    ghost, edge_last = jnp.broadcast_to(ghost, (8, LANES)), jnp.broadcast_to(edge_last, (8, LANES))
    part = down(ghost, 4) * edge_last
    sums[56:64, :] = 1.0 + part - down(part, 4)


def build_table(pack, sums, axis, index, n, tab):
    m = pack.shape[1]
    n1, n2 = n // 2, n // 4
    a = 2 * axis
    for row, (block, r) in {
        GA: (3, a),
        GB: (3, a + 4),
        GA2: (3, a + 1),
        GB2: (3, a + 5),
        HW1: (5, a),
        HW2: (5, a + 1),
        CA0: (0, a + 1),
        CA1: (1, a + 1),
        KAP: (2, a + 1),
        LAM: (2, a + 5),
        CB0: (0, a + 5),
        CB1: (1, a + 5),
        VN: (6, a + 4),
        UN: (6, a),
        HG: (7, a),
    }.items():
        source = 8 * block + r
        tab[row : row + 1, :] = sums[source : source + 1, :]
    where, _ = offsets(n)
    for lv, rows, suffix_name in ((0, n1, ""), (1, n2, "2")):
        col = lax.broadcasted_iota(jnp.int32, (rows, m), 1)
        sub = lax.broadcasted_iota(jnp.int32, (rows, m), 0)
        mine = col == index * rows + sub
        mine_inner = mine & (sub < rows - 1)
        for name, block, below, mask in (
            ("wl", 2, 0, mine),
            ("wr", 2, 4, mine_inner),
            ("al", 1, 0, mine),
            ("be", 1, 4, mine),
            ("u", 0, 0, mine),
            ("v", 0, 4, mine),
        ):
            r = 8 * block + below + a + lv
            values = jnp.sum(jnp.where(mask, pack[r : r + 1, :], 0.0), axis=1, keepdims=True)
            start = where[name + suffix_name]
            tab[start : start + rows, :] = jnp.broadcast_to(values, (rows, LANES))


def one_level(even, odd, tab, where, suffix, ga, gb, from_left, from_right):
    def c(name, i):
        row = where[name + suffix] + i
        return tab[row : row + 1, :]

    count = len(even)
    details = []
    for i in range(count):
        e = odd[i] - c("wl", i) * even[i]
        if i + 1 < count:
            e = e - c("wr", i) * even[i + 1]
        details.append(e)
    first = tab[ga : ga + 1, :] * even[0]
    acc = first if from_left is None else from_left + first
    lefts = []
    for i in range(count):
        lefts.append(acc)
        acc = acc + c("al", i) * details[i]
    left_end = acc
    acc = from_right
    rights = [None] * count
    for i in reversed(range(count)):
        term = c("be", i) * details[i]
        acc = term if acc is None else acc + term
        rights[i] = acc
    nodes = [even[i] + c("v", i) * lefts[i] + c("u", i) * rights[i] for i in range(count)]
    right_end = rights[0] + tab[gb : gb + 1, :] * even[0]
    return details, nodes, left_end, right_end


def single(tab, row):
    return tab[row : row + 1, :]


def summaries(tab, p1, q1, p2, q2):
    to_right = p2 + single(tab, KAP) * q1 - single(tab, CA1) * p1
    to_left = q2 + single(tab, LAM) * p1 + single(tab, CB0) * q1
    return to_right, to_left


def second_sums(tab, left, right, left2, right2, p1, q1):
    left_second = left2 + single(tab, CA0) * left + single(tab, KAP) * (q1 + right)
    right_second = right2 - single(tab, CB1) * right + single(tab, LAM) * (left + p1)
    return left_second, right_second


class Exchange:
    def __init__(self, axis, count, paired):
        self.axis, self.count, self.paired = axis, count, paired
        self.xor = count & (count - 1) == 0
        self.steps = list(range(1, count))

    def target(self, i, step):
        return i ^ step if self.xor else (i + step) % self.count

    def source(self, i, step):
        return i ^ step if self.xor else (i + self.count - step) % self.count

    def near(self, step):
        return any(self.target(i, step) == i - 1 for i in range(1, self.count))

    def send(self, step, x):
        pairs = [(i, self.target(i, step)) for i in range(self.count)]
        return lax.ppermute(x, self.axis, pairs)

    def direct(self):
        if not (self.xor and self.paired):
            return self.steps
        return [s for s in self.steps if s == 1 or s % 2 == 0]

    def carries(self, step):
        return self.near(step) or (step not in (1,) and self.passed(step) and self.near(step ^ 1))

    def passed(self, step):
        return step not in self.direct() or (step ^ 1) not in self.direct()

    def all(self, messages):
        direct = dict(zip(self.direct(), messages))
        got = {s: self.send(s, x) for s, x in direct.items()}
        for s in self.steps:
            if s not in got:
                got[s] = self.send(1, got[s ^ 1])
        return [got[s] for s in self.steps]


def x_tile(tab, where, field, n, cols, sums):
    even = [field[2 * i, cols, :] for i in range(n // 2)]
    odd = [field[2 * i + 1, cols, :] for i in range(n // 2)]
    left, right = sums if sums else (None, None)
    return one_level(even, odd, tab, where, "", GA, GB, left, right)


def first_kernel(exx, exy, n, ny, stiffness, ct, hx_ref, hy_ref, source, *refs):
    field, pack, sums, tab, own = refs[:5]
    messages = refs[5 : 5 + len(exx.direct())]
    hx, hy, sems, spacing_sems = refs[5 + len(exx.direct()) :]
    ex = exx
    index = lax.axis_index(exx.axis)
    tiles = ny // ct

    def fetch(t):
        part = pl.ds(t * (n // 1), n // 1)
        return pltpu.make_async_copy(source.at[part], field.at[part], sems.at[t])

    spacings = [
        pltpu.make_async_copy(a, b, spacing_sems.at[i])
        for i, (a, b) in enumerate(((hx_ref, hx), (hy_ref, hy)))
    ]
    for copy in spacings:
        copy.start()
    for t in range(1):
        fetch(t).start()
    for copy in spacings:
        copy.wait()
    lanes = 2 * pack.shape[1]
    counts = (hx.shape[1], hy.shape[1])

    def row(ref):
        x = ref[...]
        if x.shape[1] < lanes:
            x = jnp.concatenate([x, jnp.ones((1, lanes - x.shape[1]), F32)], axis=1)
        return jnp.broadcast_to(x, (8, lanes))

    is_y = (lax.broadcasted_iota(jnp.int32, (8, lanes), 0) & 2) == 2
    build_pack(
        jnp.where(is_y, row(hy), row(hx)),
        counts,
        (index, lax.axis_index(exy.axis)),
        (n, ny),
        stiffness,
        pack,
        sums,
    )
    build_table(pack, sums, 0, index, n, tab)
    for t in range(1):
        fetch(t).wait()
    where, _ = offsets(n)

    def body(t, carry):
        begin = pl.multiple_of(t * ct, ct)
        cols = pl.ds(begin, ct)
        _, nodes, p1, q1 = x_tile(tab, where, field, n, cols, None)
        _, _, p2, q2 = one_level(nodes[0::2], nodes[1::2], tab, where, "2", GA2, GB2, None, None)
        p2, q2 = summaries(tab, p1, q1, p2, q2)
        own[cols, :] = p1
        own[pl.ds(begin + ny, ct), :] = q1
        for step, message in zip(ex.direct(), messages):
            upward = ex.target(index, step) > index
            message[cols, :] = jnp.where(upward, p1, q1)
            message[pl.ds(begin + ny, ct), :] = jnp.where(upward, p2, q2)
            if ex.carries(step):
                message[pl.ds(begin + 2 * ny, ct), :] = field[0, cols, :]
        return carry

    lax.fori_loop(0, tiles, body, 0)


def column(ref, j, count, ny):
    return ref[pl.ds(j, count, stride=ny), :]


def local_kernel(exy, n, ny, ct, field, xtab, pack, sums, passing, *refs):
    ytab, shares, fine, out, local, passed, full, mixed = refs
    n1, n2 = n // 2, n // 4
    where, _ = offsets(n)
    build_table(pack, sums, 1, lax.axis_index(exy.axis), ny, ytab)

    for r, name in enumerate(("v", "u")):
        nodes = [single(xtab, where[name] + i) for i in range(n1)]
        details, nodes, _, _ = one_level(
            nodes[0::2], nodes[1::2], xtab, where, "2", GA2, GB2, None, None
        )
        for i in range(n2):
            shares[r * n2 + i : r * n2 + i + 1, :] = nodes[i]
            shares[(2 + r) * n2 + i : (2 + r) * n2 + i + 1, :] = details[i]

    def body(t, carry):
        begin = pl.multiple_of(t * ct, ct)
        cols = pl.ds(begin, ct)
        details, nodes, _, _ = x_tile(xtab, where, field, n, cols, None)
        for i in range(n1):
            fine[i, cols, :] = details[i]
            full[pl.ds(i * ny + begin, ct), :] = nodes[i]
        details, nodes, _, _ = one_level(
            nodes[0::2], nodes[1::2], xtab, where, "2", GA2, GB2, None, None
        )
        for i in range(n2):
            mixed[pl.ds(i * ny + begin, ct), :] = nodes[i]
            mixed[pl.ds((n2 + i) * ny + begin, ct), :] = details[i]
        return carry

    lax.fori_loop(0, ny // ct, body, 0)

    m1, m2 = ny // 2, ny // 4
    ywhere, _ = offsets(ny)
    for j in range(m1):
        e = column(full, 2 * j + 1, n1, ny)
        e = e - single(ytab, ywhere["wl"] + j) * column(full, 2 * j, n1, ny)
        if j + 1 < m1:
            e = e - single(ytab, ywhere["wr"] + j) * column(full, 2 * j + 2, n1, ny)
        out[pl.ds(2 * j + 1, n1, stride=ny), :] = e
    even = [column(mixed, 2 * j, n1, ny) for j in range(m1)]
    odd = [column(mixed, 2 * j + 1, n1, ny) for j in range(m1)]
    _, nodes, p1, q1 = one_level(even, odd, ytab, ywhere, "", GA, GB, None, None)
    for j in range(m1):
        out[pl.ds(ny + 2 * j, n2, stride=2 * ny), :] = nodes[j][n2:]
    thin = [x[:n2] for x in nodes]
    details, nodes, p2, q2 = one_level(
        thin[0::2], thin[1::2], ytab, ywhere, "2", GA2, GB2, None, None
    )
    for j in range(m2):
        out[pl.ds(4 * j, n2, stride=2 * ny), :] = nodes[j]
        out[pl.ds(4 * j + 2, n2, stride=2 * ny), :] = details[j]
    p2, q2 = summaries(ytab, p1[:n2], q1[:n2], p2, q2)
    local[:n1, :] = p1
    local[n1 : n1 + n2, :] = p2
    local[n1 + n2 : 2 * n1 + n2, :] = q1
    local[2 * n1 + n2 : 3 * n1, :] = q2
    local[3 * n1 : 4 * n1, :] = column(full, 0, n1, ny)
    local[4 * n1 :, :] = column(mixed, 0, n2, ny)


LEFT, RIGHT, LEFT2, RIGHT2, GHOST, HALO, ARRIVED = 0, 1, 2, 3, 4, 5, 8


def arrived_y(ytab, arrived, ny):
    m1 = ny // 2
    where, _ = offsets(ny)
    even = [column(arrived, 2 * j, ARRIVED, ny) for j in range(m1)]
    odd = [column(arrived, 2 * j + 1, ARRIVED, ny) for j in range(m1)]
    details, nodes, p1, q1 = one_level(even, odd, ytab, where, "", GA, GB, None, None)
    details2, nodes2, p2, q2 = one_level(
        nodes[0::2], nodes[1::2], ytab, where, "2", GA2, GB2, None, None
    )
    return details, nodes, details2, nodes2, p1, q1, p2, q2


def second_kernel(exx, exy, n, ny, ct, *refs):
    own, xtab, shares, ytab, local = refs[:5]
    incoming = refs[5 : 5 + len(exx.steps)]
    arrived, yown = refs[5 + len(exx.steps) : 7 + len(exx.steps)]
    messages = refs[7 + len(exx.steps) :]
    index = lax.axis_index(exx.axis)
    n1, n2 = n // 2, n // 4
    where, _ = offsets(n)

    def body(t, carry):
        begin = pl.multiple_of(t * ct, ct)
        cols = pl.ds(begin, ct)
        zero = jnp.zeros((ct, LANES), F32)
        left = right = left2 = right2 = halo = zero
        for step, message in zip(exx.steps, incoming):
            source = exx.source(index, step)
            lower = source < index
            one = message[cols, :]
            two = message[pl.ds(begin + ny, ct), :]
            left = left + jnp.where(lower, one, 0.0)
            right = right + jnp.where(lower, 0.0, one)
            left2 = left2 + jnp.where(lower, two, 0.0)
            right2 = right2 + jnp.where(lower, 0.0, two)
            if exx.near(step):
                halo = jnp.where(source == index + 1, message[pl.ds(begin + 2 * ny, ct), :], halo)
        p1, q1 = own[cols, :], own[pl.ds(begin + ny, ct), :]
        left2, right2 = second_sums(xtab, left, right, left2, right2, p1, q1)
        ghost = single(xtab, HG) * halo + single(xtab, VN) * (left + p1) + single(xtab, UN) * right
        for row, value in (
            (LEFT, left),
            (RIGHT, right),
            (LEFT2, left2),
            (RIGHT2, right2),
            (GHOST, ghost),
            (HALO, halo),
            (HALO + 1, zero),
            (HALO + 2, zero),
        ):
            arrived[pl.ds(row * ny + begin, ct), :] = value
        return carry

    lax.fori_loop(0, ny // ct, body, 0)
    _, _, _, _, p1, q1, p2, q2 = arrived_y(ytab, arrived, ny)
    p2, q2 = summaries(ytab, p1, q1, p2, q2)
    first = column(arrived, 0, ARRIVED, ny)
    nodes_v, nodes_u = shares[:n2, :], shares[n2 : 2 * n2, :]
    details_v, details_u = shares[2 * n2 : 3 * n2, :], shares[3 * n2 :, :]

    def rows(name, count):
        return xtab[where[name] : where[name] + count, :]

    def coarse(x):
        return (
            nodes_v * x[LEFT : LEFT + 1]
            + nodes_u * x[RIGHT : RIGHT + 1]
            + rows("v2", n2) * x[LEFT2 : LEFT2 + 1]
            + rows("u2", n2) * x[RIGHT2 : RIGHT2 + 1]
        )

    is_last = lax.broadcasted_iota(jnp.int32, (n2, LANES), 0) == n2 - 1

    def detail(x):
        ghost = jnp.where(is_last, single(xtab, HW2) * x[GHOST : GHOST + 1], 0.0)
        return details_v * x[LEFT : LEFT + 1] + details_u * x[RIGHT : RIGHT + 1] - ghost

    p1c, p1d = local[:n2, :] + coarse(p1), local[n2:n1, :] + detail(p1)
    p2c = local[n1 : n1 + n2, :] + coarse(p2)
    q1c = local[n1 + n2 : 2 * n1, :] + coarse(q1)
    q1d = local[2 * n1 : 2 * n1 + n2, :] + detail(q1)
    q2c = local[2 * n1 + n2 : 3 * n1, :] + coarse(q2)
    yown[:n2, :] = p1c
    yown[n2:, :] = q1c
    yindex = lax.axis_index(exy.axis)
    for step, message in zip(exy.steps, messages):
        upward = exy.target(yindex, step) > yindex
        message[:n2, :] = jnp.where(upward, p1c, q1c)
        message[n2:n1, :] = jnp.where(upward, p1d, q1d)
        message[n1 : n1 + n2, :] = jnp.where(upward, p2c, q2c)
        if exy.near(step):
            message[n1 + n2 : 2 * n1 + n2, :] = (
                local[3 * n1 : 4 * n1, :]
                + rows("v", n1) * first[LEFT : LEFT + 1]
                + rows("u", n1) * first[RIGHT : RIGHT + 1]
            )
            message[2 * n1 + n2 : 2 * (n1 + n2), :] = local[4 * n1 :, :] + coarse(first)


def share_kernel(n, ny, own_part, fine, arrived, xtab, shares, ytab, result, out, *refs):
    last, one, two, blend, sems = refs
    n1, n2 = n // 2, n // 4
    m1, m2 = ny // 2, ny // 4
    where, _ = offsets(n)
    last[...] = fine[n1 - 1] - single(xtab, HW1) * arrived[HALO * ny : (HALO + 1) * ny, :]
    copies = [
        pltpu.make_async_copy(fine.at[: n1 - 1], result.at[: n1 - 1, 1], sems.at[0]),
        pltpu.make_async_copy(last, result.at[n1 - 1, 1], sems.at[1]),
    ]
    for copy in copies:
        copy.start()
    details, nodes, details2, nodes2, _, _, _, _ = arrived_y(ytab, arrived, ny)
    side = lax.broadcasted_iota(jnp.int32, (ARRIVED, LANES), 0) < LEFT2
    for j in range(m1):
        at = pl.ds(2 * j + 1, ARRIVED, stride=ny)
        one[at, :] = details[j]
        two[at, :] = jnp.where(side, details[j], 0.0)
        one[pl.ds(2 * j, ARRIVED, stride=ny), :] = nodes[j]
    for j in range(m2):
        two[pl.ds(4 * j, ARRIVED, stride=ny), :] = nodes2[j]
        two[pl.ds(4 * j + 2, ARRIVED, stride=ny), :] = details2[j]
    odd = (lax.broadcasted_iota(jnp.int32, (8, LANES), 0) & 1) == 1
    for k in range(n1):
        for r, name in enumerate(("v", "u")):
            block = (2 + r if k % 2 else r) * n2 + k // 2
            mixture = jnp.where(odd, single(xtab, where[name] + k), single(shares, block))
            blend[16 * k + 8 * r : 16 * k + 8 * r + 8, :] = mixture

    def body(t, carry):
        begin = pl.multiple_of(t * 8, 8)
        cols = pl.ds(begin, 8)

        def tile(ref, r):
            return ref[pl.ds(r * ny + begin, 8), :]

        ones = [tile(one, r) for r in (LEFT, RIGHT)]
        twos = [tile(two, r) for r in (LEFT, RIGHT, LEFT2, RIGHT2)]
        ghost = jnp.where(odd, 0.0, single(xtab, HW2) * tile(one, GHOST))
        for k in range(n1):
            x = own_part[k, cols, :]
            source = ones if k % 2 else twos
            for r in range(2):
                x = x + blend[16 * k + 8 * r : 16 * k + 8 * r + 8, :] * source[r]
            if k % 2 == 0:
                x = x + single(xtab, where["v2"] + k // 2) * twos[2]
                x = x + single(xtab, where["u2"] + k // 2) * twos[3]
            elif k == n1 - 1:
                x = x - ghost
            out[k, cols, :] = x
        return carry

    lax.fori_loop(0, ny // 8, body, 0)
    for copy in copies:
        copy.wait()


def rank_kernel(ny, tab, ranks):
    where, _ = offsets(ny)
    m1, m2 = ny // 2, ny // 4
    ranks[...] = jnp.zeros_like(ranks)

    def put(rank, j, value):
        ranks[rank, j : j + 1, :] = value

    for rank, name, end in ((0, "v", VN), (1, "u", UN)):
        nodes = [single(tab, where[name] + i) for i in range(m1)]
        for i in range(m1):
            put(rank, 2 * i, nodes[i])
        details, nodes2, _, _ = one_level(
            nodes[0::2], nodes[1::2], tab, where, "2", GA2, GB2, None, None
        )
        details[-1] = details[-1] - single(tab, HW2) * single(tab, end)
        for i in range(m2):
            put(2 + rank, 4 * i, nodes2[i])
            put(2 + rank, 4 * i + 2, details[i])
            put(4 + rank, 4 * i, single(tab, where[name + "2"] + i))
    put(6, ny - 1, -single(tab, HW1))
    put(7, ny - 2, -single(tab, HW2))


def third_kernel(ex, n, ny, *refs):
    partial, tab, ranks, own = refs[1:5]
    incoming = refs[5 : 5 + len(ex.steps)]
    result, sums, done, sems = refs[5 + len(ex.steps) :]
    n1, n2 = n // 2, n // 4
    index = lax.axis_index(ex.axis)
    zero, zero2 = jnp.zeros((n1, LANES), F32), jnp.zeros((n2, LANES), F32)
    left, right, left2, right2, halo, halo2 = zero, zero, zero2, zero2, zero, zero2
    for step, message in zip(ex.steps, incoming):
        source = ex.source(index, step)
        lower = source < index
        one, two = message[:n1, :], message[n1 : n1 + n2, :]
        left = left + jnp.where(lower, one, 0.0)
        right = right + jnp.where(lower, 0.0, one)
        left2 = left2 + jnp.where(lower, two, 0.0)
        right2 = right2 + jnp.where(lower, 0.0, two)
        if ex.near(step):
            mine = source == index + 1
            halo = jnp.where(mine, message[n1 + n2 : 2 * n1 + n2, :], halo)
            halo2 = jnp.where(mine, message[2 * n1 + n2 : 2 * (n1 + n2), :], halo2)
    p1, q1 = own[:n2, :], own[n2:, :]
    left2, right2 = second_sums(tab, left[:n2], right[:n2], left2, right2, p1, q1)
    ghost = single(tab, HG) * halo2 + single(tab, VN) * p1
    sums[0:n1, :] = left
    sums[n1 : 2 * n1, :] = right
    sums[2 * n1 : 3 * n1, :] = halo
    sums[3 * n1 : 3 * n1 + n2, :] = left2
    sums[3 * n1 + n2 : 3 * n1 + 2 * n2, :] = right2
    sums[3 * n1 + 2 * n2 : 3 * n1 + 3 * n2, :] = ghost

    def row(i):
        return sums[i : i + 1, :]

    group = n1 // 4

    def put(g):
        part = pl.ds(g * group, group)
        return pltpu.make_async_copy(done.at[part], result.at[part, 0], sems.at[g])

    for g in range(4):
        for t in range(ny // 8):
            cols = slice(8 * t, 8 * t + 8)
            tables = [ranks[r, cols, :] for r in range(8)]
            for k in range(g * group, (g + 1) * group):
                x = partial[k, cols, :] + tables[6] * row(2 * n1 + k)
                if k % 2:
                    i = n2 + k // 2
                    x = x + tables[0] * row(i) + tables[1] * row(n1 + i)
                else:
                    i = k // 2
                    x = x + tables[2] * row(i) + tables[3] * row(n1 + i)
                    x = x + tables[4] * row(3 * n1 + i) + tables[5] * row(3 * n1 + n2 + i)
                    x = x + tables[7] * row(3 * n1 + 2 * n2 + i)
                done[k, cols, :] = x
        put(g).start()
    for g in range(4):
        put(g).wait()


def y_rows(ex, n, step):
    if not ex.near(step):
        return 3 * n // 4
    return 3 * n // 2 + (8 if step > 1 else 0)


def shape(*dims):
    return jax.ShapeDtypeStruct(dims, F32)


def on_device(exx, exy, field, spacing_x, spacing_y):
    n, ny, _ = field.shape
    n1, n2 = n // 2, n // 4
    ct = 32
    xrows = offsets(n)[1]
    yrows = offsets(ny)[1]
    params = pltpu.CompilerParams(vmem_limit_bytes=40 * 1024 * 1024)
    anywhere = pl.BlockSpec(memory_space=pl.ANY)
    inside = pl.BlockSpec(memory_space=pltpu.VMEM)
    dma = pltpu.SemaphoreType.DMA
    operands = (spacing_x[None], spacing_y[None], field)
    lanes = max(spacing_x.shape[0], spacing_y.shape[0])
    lanes = (lanes + 2 * LANES - 1) // (2 * LANES) * LANES
    stiffness = (float(SMOOTH_X) ** 2, float(SMOOTH_Y) ** 2)
    field, pack, sums, xtab, xown, *outgoing = pl.pallas_call(
        functools.partial(first_kernel, exx, exy, n, ny, stiffness, ct),
        out_shape=[shape(n, ny, LANES), shape(24, lanes), shape(64, LANES)]
        + [shape(xrows, LANES), shape(2 * ny, LANES)]
        + [shape((3 if exx.carries(s) else 2) * ny, LANES) for s in exx.direct()],
        in_specs=[anywhere] * 3,
        scratch_shapes=[
            pltpu.VMEM((1, spacing_x.shape[0]), F32),
            pltpu.VMEM((1, spacing_y.shape[0]), F32),
            dma((1,)),
            dma((2,)),
        ],
        compiler_params=params,
        name="x_summary",
    )(*[pltpu.with_memory_space_constraint(a, pltpu.HBM) for a in operands])
    block = shape(n1, ny, LANES)
    lines = pltpu.VMEM((n1 * ny, LANES), F32)
    ytab, shares, fine, local_out, local, outgoing[0] = pl.pallas_call(
        functools.partial(local_kernel, exy, n, ny, ct),
        out_shape=[shape(yrows, LANES), shape(4 * n2, LANES), block, shape(n1 * ny, LANES)]
        + [shape(4 * n1 + n2, LANES), shape(*outgoing[0].shape)],
        in_specs=[inside] * 4 + [anywhere],
        out_specs=[inside] * 5 + [anywhere],
        input_output_aliases={4: 5},
        scratch_shapes=[lines, lines],
        compiler_params=params,
        name="local_transform",
    )(field, xtab, pack, sums, outgoing[0])
    incoming = exx.all(outgoing)
    arrived, own, *outgoing = pl.pallas_call(
        functools.partial(second_kernel, exx, exy, n, ny, ct),
        out_shape=[shape(ARRIVED * ny, LANES), shape(2 * n2, LANES)]
        + [shape(y_rows(exy, n, s), LANES) for s in exy.steps],
        compiler_params=params,
        name="x_arrived",
    )(xown, xtab, shares, ytab, local, *incoming)
    some = pltpu.VMEM((ARRIVED * ny, LANES), F32)
    result, partial = pl.pallas_call(
        functools.partial(share_kernel, n, ny),
        out_shape=[shape(n1, 2, ny, LANES), block],
        out_specs=[anywhere, inside],
        scratch_shapes=[
            pltpu.VMEM((ny, LANES), F32),
            some,
            some,
            pltpu.VMEM((16 * n1, LANES), F32),
            dma((2,)),
        ],
        compiler_params=params,
        name="x_share",
    )(local_out.reshape(n1, ny, LANES), fine, arrived, xtab, shares, ytab)
    ranks = pl.pallas_call(
        functools.partial(rank_kernel, ny),
        out_shape=shape(8, ny, LANES),
        compiler_params=params,
        name="y_ranks",
    )(ytab)
    incoming = exy.all(outgoing)
    result = pl.pallas_call(
        functools.partial(third_kernel, exy, n, ny),
        out_shape=shape(n1, 2, ny, LANES),
        in_specs=[anywhere] + [inside] * (4 + len(incoming)),
        out_specs=anywhere,
        input_output_aliases={0: 0},
        scratch_shapes=[
            pltpu.VMEM((3 * n1 + 3 * n2, LANES), F32),
            pltpu.VMEM((n1, ny, LANES), F32),
            dma((4,)),
        ],
        compiler_params=params,
        name="y_update",
    )(result, partial, ytab, ranks, own, *incoming)
    return result.reshape(n, ny, LANES)


def solution(mesh):
    exx = Exchange("gx", mesh.shape["gx"], True)
    exy = Exchange("gy", mesh.shape["gy"], False)
    placed = (P("gx", "gy", None), P(), P())
    return jax.shard_map(
        functools.partial(on_device, exx, exy),
        mesh=mesh,
        in_specs=placed,
        out_specs=P("gx", "gy", None),
        check_vma=False,
    )
```

```python
import functools

import jax
import jax.numpy as jnp
from jax import lax
from jax.experimental import pallas as pl
from jax.experimental.pallas import tpu as pltpu
from jax.sharding import PartitionSpec as P

SMOOTH_X = 48
SMOOTH_Y = 96
F32 = jnp.float32
LANES = 128

GA, GB, GA2, GB2, HW1, HW2, CA0, CA1, KAP, LAM, CB0, CB1, VN, UN, HG = range(15)
SINGLES = 16


def offsets(n):
    n1, n2 = n // 2, n // 4
    names = ["wl", "wr", "al", "be", "u", "v"]
    where, row = {}, SINGLES
    for name in names:
        where[name] = row
        row += n1
    for name in names:
        where[name + "2"] = row
        row += n2
    return where, row


def combine(left, right):
    a, b, c, d = left
    p, q, r, s = right
    return (a * p + b * r, a * q + b * s, c * p + d * r, c * q + d * s)


def gather(x, position):
    out = []
    for t in range(position.shape[1] // LANES):
        place = position[:, t * LANES : (t + 1) * LANES]
        inner, block = place & (LANES - 1), place // LANES
        picked = None
        for b in range(x.shape[1] // LANES):
            part = jnp.take_along_axis(
                x[:, b * LANES : (b + 1) * LANES], inner, axis=1, mode="promise_in_bounds"
            )
            picked = part if picked is None else jnp.where(block == b, part, picked)
        out.append(picked)
    return out[0] if len(out) == 1 else jnp.concatenate(out, axis=1)


def down(x, by):
    return pltpu.roll(x, by, 0)


def build_pack(h, counts, places, locals_, stiffness, pack, sums):
    m = h.shape[1] // 2
    lanes = lax.broadcasted_iota(jnp.int32, (8, m), 1)
    rows = lax.broadcasted_iota(jnp.int32, (8, m), 0)
    lower = rows >= 4
    is_y = (rows & 2) == 2
    second = (rows & 1) == 1

    def by_axis(pair):
        return jnp.where(is_y, pair[1], pair[0])

    count = jnp.where(second, by_axis(counts) // 4, by_axis(counts) // 2)
    real = lanes < count
    last = lanes == count - 1
    k = jnp.where(lower, count - 1 - lanes, lanes)
    k = jnp.where(real, k, 0)
    first = jnp.where(second, 4 * k, 2 * k)
    even = gather(h, first) + jnp.where(second, gather(h, first + 1), 0.0)
    odd = gather(h, jnp.where(second, first + 2, first + 1))
    odd = odd + jnp.where(second, gather(h, jnp.where(second, first + 3, first)), 0.0)
    width = even + odd
    inverse = 1.0 / width
    s = by_axis(stiffness)
    stiff = s * inverse
    across = 1.0 / (stiff - width * (1.0 / 6.0))
    same = jnp.where(real, (width * (1.0 / 3.0) + stiff) * across, 1.0)
    into = jnp.where(real, across, 0.0)
    back = jnp.where(real, (s + width * width * (1.0 / 12.0)) * across, 0.0)
    product = (same, into, back, same)
    identity = (1.0, 0.0, 0.0, 1.0)

    def moved(matrix, by):
        head = lanes < by
        return [jnp.where(head, f, pltpu.roll(x, by, 1)) for x, f in zip(matrix, identity)]

    step = 1
    while step < m:
        if 2 * step < m:
            near = combine(product, moved(product, step))
            far = combine(moved(product, 2 * step), moved(product, 3 * step))
            product = combine(near, far)
            step *= 4
        else:
            product = combine(product, moved(product, step))
            step *= 2
    w = jnp.where(lower, product[1], product[0])
    total = jnp.where(lower, product[3], product[0])[:, m - 1 : m]
    here = jnp.where(lower, count - 1 - lanes, lanes - 1)
    there = jnp.where(lower, count - 2 - lanes, lanes)
    uv = gather(w, jnp.maximum(here, 0))
    uv = jnp.where(lower, jnp.where(real, uv, 0.0), jnp.where(lanes == 0, 1.0, uv))
    uv_next = gather(w, jnp.maximum(there, 0))
    uv_next = jnp.where(lower & (lanes >= count - 1), 0.0, uv_next)
    even = jnp.where(lower, down(even, 4), even)
    odd = jnp.where(lower, down(odd, 4), odd)
    inverse = jnp.where(lower, down(inverse, 4), inverse)
    ab = jnp.where(real, (uv * even + uv_next * odd) * (0.5 / total), 0.0)
    weight = jnp.where(lower, even, odd) * inverse
    weight = jnp.where(last, jnp.where(lower, 0.0, 1.0), weight)
    weight = jnp.where(real, weight, 0.0)
    pack[0:8, :] = uv
    pack[8:16, :] = ab
    pack[16:24, :] = weight
    other = down(weight, 4)
    wl = jnp.where(lower, other, weight)
    wr = jnp.where(lower, weight, other)
    fine = down(uv, 1)
    twice = jnp.where(real & second, 2 * lanes, 0)
    halo = -wr * gather(fine, jnp.minimum(twice + 2, m - 1))
    detail = gather(fine, twice + 1) - wl * gather(fine, twice) + halo
    valid = real & second
    halo = jnp.where(valid, halo, 0.0)
    detail = jnp.where(valid, detail, 0.0)
    place = by_axis(places)
    local = jnp.where(second, by_axis(locals_) // 4, by_axis(locals_) // 2)
    begin, end = place * local, (place + 1) * local

    def lane_sum(row, x):
        value = jnp.sum(x, axis=1, keepdims=True)
        sums[8 * row : 8 * row + 8, :] = jnp.broadcast_to(value, (8, LANES))
        return value

    def below(edge, x, y):
        return jnp.where(lanes < edge, x, 0.0) - jnp.where(lanes == edge - 1, y, 0.0)

    def above(edge, x, y):
        return jnp.where(lanes >= edge, x, 0.0) + jnp.where(lanes == edge - 1, y, 0.0)

    cross, cross_halo = ab * down(detail, 4), ab * down(halo, 4)
    alike, alike_halo = ab * detail, ab * halo
    lane_sum(0, below(begin, cross, cross_halo))
    lane_sum(1, below(end, cross, cross_halo))
    lane_sum(
        2, jnp.where(lower, above(end, alike, alike_halo), below(begin, alike, alike_halo))
    )
    edge = -ab * wr
    lane_sum(3, jnp.where(lanes == begin - 1, edge, 0.0))
    edge_last = lane_sum(4, jnp.where(lanes == end - 1, edge, 0.0))
    lane_sum(5, jnp.where(lanes == end - 1, wr, 0.0))
    ghost = lane_sum(6, jnp.where(lanes == end, uv, 0.0))
    ghost, edge_last = jnp.broadcast_to(ghost, (8, LANES)), jnp.broadcast_to(edge_last, (8, LANES))
    part = down(ghost, 4) * edge_last
    sums[56:64, :] = 1.0 + part - down(part, 4)


def build_table(pack, sums, axis, index, n, tab):
    m = pack.shape[1]
    n1, n2 = n // 2, n // 4
    a = 2 * axis
    for row, (block, r) in {
        GA: (3, a),
        GB: (3, a + 4),
        GA2: (3, a + 1),
        GB2: (3, a + 5),
        HW1: (5, a),
        HW2: (5, a + 1),
        CA0: (0, a + 1),
        CA1: (1, a + 1),
        KAP: (2, a + 1),
        LAM: (2, a + 5),
        CB0: (0, a + 5),
        CB1: (1, a + 5),
        VN: (6, a + 4),
        UN: (6, a),
        HG: (7, a),
    }.items():
        source = 8 * block + r
        tab[row : row + 1, :] = sums[source : source + 1, :]
    where, _ = offsets(n)
    for lv, rows, suffix_name in ((0, n1, ""), (1, n2, "2")):
        col = lax.broadcasted_iota(jnp.int32, (rows, m), 1)
        sub = lax.broadcasted_iota(jnp.int32, (rows, m), 0)
        mine = col == index * rows + sub
        mine_inner = mine & (sub < rows - 1)
        for name, block, below, mask in (
            ("wl", 2, 0, mine),
            ("wr", 2, 4, mine_inner),
            ("al", 1, 0, mine),
            ("be", 1, 4, mine),
            ("u", 0, 0, mine),
            ("v", 0, 4, mine),
        ):
            r = 8 * block + below + a + lv
            values = jnp.sum(jnp.where(mask, pack[r : r + 1, :], 0.0), axis=1, keepdims=True)
            start = where[name + suffix_name]
            tab[start : start + rows, :] = jnp.broadcast_to(values, (rows, LANES))


def one_level(even, odd, tab, where, suffix, ga, gb, from_left, from_right):
    def c(name, i):
        row = where[name + suffix] + i
        return tab[row : row + 1, :]

    count = len(even)
    details = []
    for i in range(count):
        e = odd[i] - c("wl", i) * even[i]
        if i + 1 < count:
            e = e - c("wr", i) * even[i + 1]
        details.append(e)
    first = tab[ga : ga + 1, :] * even[0]
    acc = first if from_left is None else from_left + first
    lefts = []
    for i in range(count):
        lefts.append(acc)
        acc = acc + c("al", i) * details[i]
    left_end = acc
    acc = from_right
    rights = [None] * count
    for i in reversed(range(count)):
        term = c("be", i) * details[i]
        acc = term if acc is None else acc + term
        rights[i] = acc
    nodes = [even[i] + c("v", i) * lefts[i] + c("u", i) * rights[i] for i in range(count)]
    right_end = rights[0] + tab[gb : gb + 1, :] * even[0]
    return details, nodes, left_end, right_end


def single(tab, row):
    return tab[row : row + 1, :]


def summaries(tab, p1, q1, p2, q2):
    to_right = p2 + single(tab, KAP) * q1 - single(tab, CA1) * p1
    to_left = q2 + single(tab, LAM) * p1 + single(tab, CB0) * q1
    return to_right, to_left


def second_sums(tab, left, right, left2, right2, p1, q1):
    left_second = left2 + single(tab, CA0) * left + single(tab, KAP) * (q1 + right)
    right_second = right2 - single(tab, CB1) * right + single(tab, LAM) * (left + p1)
    return left_second, right_second


class Exchange:
    def __init__(self, axis, count, paired):
        self.axis, self.count, self.paired = axis, count, paired
        self.xor = count & (count - 1) == 0
        self.steps = list(range(1, count))

    def target(self, i, step):
        return i ^ step if self.xor else (i + step) % self.count

    def source(self, i, step):
        return i ^ step if self.xor else (i + self.count - step) % self.count

    def near(self, step):
        return any(self.target(i, step) == i - 1 for i in range(1, self.count))

    def send(self, step, x):
        pairs = [(i, self.target(i, step)) for i in range(self.count)]
        return lax.ppermute(x, self.axis, pairs)

    def direct(self):
        if not (self.xor and self.paired):
            return self.steps
        return [s for s in self.steps if s == 1 or s % 2 == 0]

    def carries(self, step):
        return self.near(step) or (step not in (1,) and self.passed(step) and self.near(step ^ 1))

    def passed(self, step):
        return step not in self.direct() or (step ^ 1) not in self.direct()

    def all(self, messages):
        direct = dict(zip(self.direct(), messages))
        got = {s: self.send(s, x) for s, x in direct.items()}
        for s in self.steps:
            if s not in got:
                got[s] = self.send(1, got[s ^ 1])
        return [got[s] for s in self.steps]


def x_tile(tab, where, field, n, cols, sums):
    even = [field[2 * i, cols, :] for i in range(n // 2)]
    odd = [field[2 * i + 1, cols, :] for i in range(n // 2)]
    left, right = sums if sums else (None, None)
    return one_level(even, odd, tab, where, "", GA, GB, left, right)


def first_kernel(exx, exy, n, ny, stiffness, ct, hx_ref, hy_ref, source, *refs):
    field, pack, sums, tab, own = refs[:5]
    messages = refs[5 : 5 + len(exx.direct())]
    hx, hy, sems, spacing_sems = refs[5 + len(exx.direct()) :]
    ex = exx
    index = lax.axis_index(exx.axis)
    tiles = ny // ct

    def fetch(t):
        part = pl.ds(t * (n // 1), n // 1)
        return pltpu.make_async_copy(source.at[part], field.at[part], sems.at[t])

    spacings = [
        pltpu.make_async_copy(a, b, spacing_sems.at[i])
        for i, (a, b) in enumerate(((hx_ref, hx), (hy_ref, hy)))
    ]
    for copy in spacings:
        copy.start()
    for t in range(1):
        fetch(t).start()
    for copy in spacings:
        copy.wait()
    lanes = 2 * pack.shape[1]
    counts = (hx.shape[1], hy.shape[1])

    def row(ref):
        x = ref[...]
        if x.shape[1] < lanes:
            x = jnp.concatenate([x, jnp.ones((1, lanes - x.shape[1]), F32)], axis=1)
        return jnp.broadcast_to(x, (8, lanes))

    is_y = (lax.broadcasted_iota(jnp.int32, (8, lanes), 0) & 2) == 2
    build_pack(
        jnp.where(is_y, row(hy), row(hx)),
        counts,
        (index, lax.axis_index(exy.axis)),
        (n, ny),
        stiffness,
        pack,
        sums,
    )
    build_table(pack, sums, 0, index, n, tab)
    for t in range(1):
        fetch(t).wait()
    where, _ = offsets(n)

    def body(t, carry):
        begin = pl.multiple_of(t * ct, ct)
        cols = pl.ds(begin, ct)
        _, nodes, p1, q1 = x_tile(tab, where, field, n, cols, None)
        _, _, p2, q2 = one_level(nodes[0::2], nodes[1::2], tab, where, "2", GA2, GB2, None, None)
        p2, q2 = summaries(tab, p1, q1, p2, q2)
        own[cols, :] = p1
        own[pl.ds(begin + ny, ct), :] = q1
        for step, message in zip(ex.direct(), messages):
            upward = ex.target(index, step) > index
            message[cols, :] = jnp.where(upward, p1, q1)
            message[pl.ds(begin + ny, ct), :] = jnp.where(upward, p2, q2)
            if ex.carries(step):
                message[pl.ds(begin + 2 * ny, ct), :] = field[0, cols, :]
        return carry

    lax.fori_loop(0, tiles, body, 0)


def column(ref, j, count, ny):
    return ref[pl.ds(j, count, stride=ny), :]


def local_kernel(exy, n, ny, ct, field, xtab, pack, sums, passing, *refs):
    ytab, shares, fine, out, local, passed, full, mixed = refs
    n1, n2 = n // 2, n // 4
    where, _ = offsets(n)
    build_table(pack, sums, 1, lax.axis_index(exy.axis), ny, ytab)

    for r, name in enumerate(("v", "u")):
        nodes = [single(xtab, where[name] + i) for i in range(n1)]
        details, nodes, _, _ = one_level(
            nodes[0::2], nodes[1::2], xtab, where, "2", GA2, GB2, None, None
        )
        for i in range(n2):
            shares[r * n2 + i : r * n2 + i + 1, :] = nodes[i]
            shares[(2 + r) * n2 + i : (2 + r) * n2 + i + 1, :] = details[i]

    def body(t, carry):
        begin = pl.multiple_of(t * ct, ct)
        cols = pl.ds(begin, ct)
        details, nodes, _, _ = x_tile(xtab, where, field, n, cols, None)
        for i in range(n1):
            fine[i, cols, :] = details[i]
            full[pl.ds(i * ny + begin, ct), :] = nodes[i]
        details, nodes, _, _ = one_level(
            nodes[0::2], nodes[1::2], xtab, where, "2", GA2, GB2, None, None
        )
        for i in range(n2):
            mixed[pl.ds(i * ny + begin, ct), :] = nodes[i]
            mixed[pl.ds((n2 + i) * ny + begin, ct), :] = details[i]
        return carry

    lax.fori_loop(0, ny // ct, body, 0)

    m1, m2 = ny // 2, ny // 4
    ywhere, _ = offsets(ny)
    for j in range(m1):
        e = column(full, 2 * j + 1, n1, ny)
        e = e - single(ytab, ywhere["wl"] + j) * column(full, 2 * j, n1, ny)
        if j + 1 < m1:
            e = e - single(ytab, ywhere["wr"] + j) * column(full, 2 * j + 2, n1, ny)
        out[pl.ds(2 * j + 1, n1, stride=ny), :] = e
    even = [column(mixed, 2 * j, n1, ny) for j in range(m1)]
    odd = [column(mixed, 2 * j + 1, n1, ny) for j in range(m1)]
    _, nodes, p1, q1 = one_level(even, odd, ytab, ywhere, "", GA, GB, None, None)
    for j in range(m1):
        out[pl.ds(ny + 2 * j, n2, stride=2 * ny), :] = nodes[j][n2:]
    thin = [x[:n2] for x in nodes]
    details, nodes, p2, q2 = one_level(
        thin[0::2], thin[1::2], ytab, ywhere, "2", GA2, GB2, None, None
    )
    for j in range(m2):
        out[pl.ds(4 * j, n2, stride=2 * ny), :] = nodes[j]
        out[pl.ds(4 * j + 2, n2, stride=2 * ny), :] = details[j]
    p2, q2 = summaries(ytab, p1[:n2], q1[:n2], p2, q2)
    local[:n1, :] = p1
    local[n1 : n1 + n2, :] = p2
    local[n1 + n2 : 2 * n1 + n2, :] = q1
    local[2 * n1 + n2 : 3 * n1, :] = q2
    local[3 * n1 : 4 * n1, :] = column(full, 0, n1, ny)
    local[4 * n1 :, :] = column(mixed, 0, n2, ny)


LEFT, RIGHT, LEFT2, RIGHT2, GHOST, HALO, ARRIVED = 0, 1, 2, 3, 4, 5, 8


def arrived_y(ytab, arrived, ny):
    m1 = ny // 2
    where, _ = offsets(ny)
    even = [column(arrived, 2 * j, ARRIVED, ny) for j in range(m1)]
    odd = [column(arrived, 2 * j + 1, ARRIVED, ny) for j in range(m1)]
    details, nodes, p1, q1 = one_level(even, odd, ytab, where, "", GA, GB, None, None)
    details2, nodes2, p2, q2 = one_level(
        nodes[0::2], nodes[1::2], ytab, where, "2", GA2, GB2, None, None
    )
    return details, nodes, details2, nodes2, p1, q1, p2, q2


def second_kernel(exx, exy, n, ny, ct, *refs):
    own, xtab, shares, ytab, local = refs[:5]
    incoming = refs[5 : 5 + len(exx.steps)]
    arrived, yown = refs[5 + len(exx.steps) : 7 + len(exx.steps)]
    messages = refs[7 + len(exx.steps) :]
    index = lax.axis_index(exx.axis)
    n1, n2 = n // 2, n // 4
    where, _ = offsets(n)

    def body(t, carry):
        begin = pl.multiple_of(t * ct, ct)
        cols = pl.ds(begin, ct)
        zero = jnp.zeros((ct, LANES), F32)
        left = right = left2 = right2 = halo = zero
        for step, message in zip(exx.steps, incoming):
            source = exx.source(index, step)
            lower = source < index
            one = message[cols, :]
            two = message[pl.ds(begin + ny, ct), :]
            left = left + jnp.where(lower, one, 0.0)
            right = right + jnp.where(lower, 0.0, one)
            left2 = left2 + jnp.where(lower, two, 0.0)
            right2 = right2 + jnp.where(lower, 0.0, two)
            if exx.near(step):
                halo = jnp.where(source == index + 1, message[pl.ds(begin + 2 * ny, ct), :], halo)
        p1, q1 = own[cols, :], own[pl.ds(begin + ny, ct), :]
        left2, right2 = second_sums(xtab, left, right, left2, right2, p1, q1)
        ghost = single(xtab, HG) * halo + single(xtab, VN) * (left + p1) + single(xtab, UN) * right
        for row, value in (
            (LEFT, left),
            (RIGHT, right),
            (LEFT2, left2),
            (RIGHT2, right2),
            (GHOST, ghost),
            (HALO, halo),
            (HALO + 1, zero),
            (HALO + 2, zero),
        ):
            arrived[pl.ds(row * ny + begin, ct), :] = value
        return carry

    lax.fori_loop(0, ny // ct, body, 0)
    _, _, _, _, p1, q1, p2, q2 = arrived_y(ytab, arrived, ny)
    p2, q2 = summaries(ytab, p1, q1, p2, q2)
    first = column(arrived, 0, ARRIVED, ny)
    nodes_v, nodes_u = shares[:n2, :], shares[n2 : 2 * n2, :]
    details_v, details_u = shares[2 * n2 : 3 * n2, :], shares[3 * n2 :, :]

    def rows(name, count):
        return xtab[where[name] : where[name] + count, :]

    def coarse(x):
        return (
            nodes_v * x[LEFT : LEFT + 1]
            + nodes_u * x[RIGHT : RIGHT + 1]
            + rows("v2", n2) * x[LEFT2 : LEFT2 + 1]
            + rows("u2", n2) * x[RIGHT2 : RIGHT2 + 1]
        )

    is_last = lax.broadcasted_iota(jnp.int32, (n2, LANES), 0) == n2 - 1

    def detail(x):
        ghost = jnp.where(is_last, single(xtab, HW2) * x[GHOST : GHOST + 1], 0.0)
        return details_v * x[LEFT : LEFT + 1] + details_u * x[RIGHT : RIGHT + 1] - ghost

    p1c, p1d = local[:n2, :] + coarse(p1), local[n2:n1, :] + detail(p1)
    p2c = local[n1 : n1 + n2, :] + coarse(p2)
    q1c = local[n1 + n2 : 2 * n1, :] + coarse(q1)
    q1d = local[2 * n1 : 2 * n1 + n2, :] + detail(q1)
    q2c = local[2 * n1 + n2 : 3 * n1, :] + coarse(q2)
    yown[:n2, :] = p1c
    yown[n2:, :] = q1c
    yindex = lax.axis_index(exy.axis)
    for step, message in zip(exy.steps, messages):
        upward = exy.target(yindex, step) > yindex
        message[:n2, :] = jnp.where(upward, p1c, q1c)
        message[n2:n1, :] = jnp.where(upward, p1d, q1d)
        message[n1 : n1 + n2, :] = jnp.where(upward, p2c, q2c)
        if exy.near(step):
            message[n1 + n2 : 2 * n1 + n2, :] = (
                local[3 * n1 : 4 * n1, :]
                + rows("v", n1) * first[LEFT : LEFT + 1]
                + rows("u", n1) * first[RIGHT : RIGHT + 1]
            )
            message[2 * n1 + n2 : 2 * (n1 + n2), :] = local[4 * n1 :, :] + coarse(first)


def share_kernel(n, ny, own_part, fine, arrived, xtab, shares, ytab, result, out, *refs):
    last, one, two, blend, sems = refs
    n1, n2 = n // 2, n // 4
    m1, m2 = ny // 2, ny // 4
    where, _ = offsets(n)
    last[...] = fine[n1 - 1] - single(xtab, HW1) * arrived[HALO * ny : (HALO + 1) * ny, :]
    copies = [
        pltpu.make_async_copy(fine.at[: n1 - 1], result.at[: n1 - 1, 1], sems.at[0]),
        pltpu.make_async_copy(last, result.at[n1 - 1, 1], sems.at[1]),
    ]
    for copy in copies:
        copy.start()
    details, nodes, details2, nodes2, _, _, _, _ = arrived_y(ytab, arrived, ny)
    side = lax.broadcasted_iota(jnp.int32, (ARRIVED, LANES), 0) < LEFT2
    for j in range(m1):
        at = pl.ds(2 * j + 1, ARRIVED, stride=ny)
        one[at, :] = details[j]
        two[at, :] = jnp.where(side, details[j], 0.0)
        one[pl.ds(2 * j, ARRIVED, stride=ny), :] = nodes[j]
    for j in range(m2):
        two[pl.ds(4 * j, ARRIVED, stride=ny), :] = nodes2[j]
        two[pl.ds(4 * j + 2, ARRIVED, stride=ny), :] = details2[j]
    odd = (lax.broadcasted_iota(jnp.int32, (8, LANES), 0) & 1) == 1
    for k in range(n1):
        for r, name in enumerate(("v", "u")):
            block = (2 + r if k % 2 else r) * n2 + k // 2
            mixture = jnp.where(odd, single(xtab, where[name] + k), single(shares, block))
            blend[16 * k + 8 * r : 16 * k + 8 * r + 8, :] = mixture

    def body(t, carry):
        begin = pl.multiple_of(t * 8, 8)
        cols = pl.ds(begin, 8)

        def tile(ref, r):
            return ref[pl.ds(r * ny + begin, 8), :]

        ones = [tile(one, r) for r in (LEFT, RIGHT)]
        twos = [tile(two, r) for r in (LEFT, RIGHT, LEFT2, RIGHT2)]
        ghost = jnp.where(odd, 0.0, single(xtab, HW2) * tile(one, GHOST))
        for k in range(n1):
            x = own_part[k, cols, :]
            source = ones if k % 2 else twos
            for r in range(2):
                x = x + blend[16 * k + 8 * r : 16 * k + 8 * r + 8, :] * source[r]
            if k % 2 == 0:
                x = x + single(xtab, where["v2"] + k // 2) * twos[2]
                x = x + single(xtab, where["u2"] + k // 2) * twos[3]
            elif k == n1 - 1:
                x = x - ghost
            out[k, cols, :] = x
        return carry

    lax.fori_loop(0, ny // 8, body, 0)
    for copy in copies:
        copy.wait()


def rank_kernel(ny, tab, ranks):
    where, _ = offsets(ny)
    m1, m2 = ny // 2, ny // 4
    ranks[...] = jnp.zeros_like(ranks)

    def put(rank, j, value):
        ranks[rank, j : j + 1, :] = value

    for rank, name, end in ((0, "v", VN), (1, "u", UN)):
        nodes = [single(tab, where[name] + i) for i in range(m1)]
        for i in range(m1):
            put(rank, 2 * i, nodes[i])
        details, nodes2, _, _ = one_level(
            nodes[0::2], nodes[1::2], tab, where, "2", GA2, GB2, None, None
        )
        details[-1] = details[-1] - single(tab, HW2) * single(tab, end)
        for i in range(m2):
            put(2 + rank, 4 * i, nodes2[i])
            put(2 + rank, 4 * i + 2, details[i])
            put(4 + rank, 4 * i, single(tab, where[name + "2"] + i))
    put(6, ny - 1, -single(tab, HW1))
    put(7, ny - 2, -single(tab, HW2))


def third_kernel(ex, n, ny, *refs):
    partial, tab, ranks, own = refs[1:5]
    incoming = refs[5 : 5 + len(ex.steps)]
    result, sums, done, sems = refs[5 + len(ex.steps) :]
    n1, n2 = n // 2, n // 4
    index = lax.axis_index(ex.axis)
    zero, zero2 = jnp.zeros((n1, LANES), F32), jnp.zeros((n2, LANES), F32)
    left, right, left2, right2, halo, halo2 = zero, zero, zero2, zero2, zero, zero2
    for step, message in zip(ex.steps, incoming):
        source = ex.source(index, step)
        lower = source < index
        one, two = message[:n1, :], message[n1 : n1 + n2, :]
        left = left + jnp.where(lower, one, 0.0)
        right = right + jnp.where(lower, 0.0, one)
        left2 = left2 + jnp.where(lower, two, 0.0)
        right2 = right2 + jnp.where(lower, 0.0, two)
        if ex.near(step):
            mine = source == index + 1
            halo = jnp.where(mine, message[n1 + n2 : 2 * n1 + n2, :], halo)
            halo2 = jnp.where(mine, message[2 * n1 + n2 : 2 * (n1 + n2), :], halo2)
    p1, q1 = own[:n2, :], own[n2:, :]
    left2, right2 = second_sums(tab, left[:n2], right[:n2], left2, right2, p1, q1)
    ghost = single(tab, HG) * halo2 + single(tab, VN) * p1
    sums[0:n1, :] = left
    sums[n1 : 2 * n1, :] = right
    sums[2 * n1 : 3 * n1, :] = halo
    sums[3 * n1 : 3 * n1 + n2, :] = left2
    sums[3 * n1 + n2 : 3 * n1 + 2 * n2, :] = right2
    sums[3 * n1 + 2 * n2 : 3 * n1 + 3 * n2, :] = ghost

    def row(i):
        return sums[i : i + 1, :]

    group = n1 // 4

    def put(g):
        part = pl.ds(g * group, group)
        return pltpu.make_async_copy(done.at[part], result.at[part, 0], sems.at[g])

    for g in range(4):
        for t in range(ny // 8):
            cols = slice(8 * t, 8 * t + 8)
            tables = [ranks[r, cols, :] for r in range(8)]
            for k in range(g * group, (g + 1) * group):
                x = partial[k, cols, :] + tables[6] * row(2 * n1 + k)
                if k % 2:
                    i = n2 + k // 2
                    x = x + tables[0] * row(i) + tables[1] * row(n1 + i)
                else:
                    i = k // 2
                    x = x + tables[2] * row(i) + tables[3] * row(n1 + i)
                    x = x + tables[4] * row(3 * n1 + i) + tables[5] * row(3 * n1 + n2 + i)
                    x = x + tables[7] * row(3 * n1 + 2 * n2 + i)
                done[k, cols, :] = x
        put(g).start()
    for g in range(4):
        put(g).wait()


def y_rows(ex, n, step):
    if not ex.near(step):
        return 3 * n // 4
    return 3 * n // 2 + (8 if step > 1 else 0)


def shape(*dims):
    return jax.ShapeDtypeStruct(dims, F32)


def on_device(exx, exy, field, spacing_x, spacing_y):
    n, ny, _ = field.shape
    n1, n2 = n // 2, n // 4
    ct = 32
    xrows = offsets(n)[1]
    yrows = offsets(ny)[1]
    params = pltpu.CompilerParams(vmem_limit_bytes=40 * 1024 * 1024)
    anywhere = pl.BlockSpec(memory_space=pl.ANY)
    inside = pl.BlockSpec(memory_space=pltpu.VMEM)
    dma = pltpu.SemaphoreType.DMA
    operands = (spacing_x[None], spacing_y[None], field)
    lanes = max(spacing_x.shape[0], spacing_y.shape[0])
    lanes = (lanes + 2 * LANES - 1) // (2 * LANES) * LANES
    stiffness = (float(SMOOTH_X) ** 2, float(SMOOTH_Y) ** 2)
    field, pack, sums, xtab, xown, *outgoing = pl.pallas_call(
        functools.partial(first_kernel, exx, exy, n, ny, stiffness, ct),
        out_shape=[shape(n, ny, LANES), shape(24, lanes), shape(64, LANES)]
        + [shape(xrows, LANES), shape(2 * ny, LANES)]
        + [shape((3 if exx.carries(s) else 2) * ny, LANES) for s in exx.direct()],
        in_specs=[anywhere] * 3,
        scratch_shapes=[
            pltpu.VMEM((1, spacing_x.shape[0]), F32),
            pltpu.VMEM((1, spacing_y.shape[0]), F32),
            dma((1,)),
            dma((2,)),
        ],
        compiler_params=params,
        name="x_summary",
    )(*[pltpu.with_memory_space_constraint(a, pltpu.HBM) for a in operands])
    block = shape(n1, ny, LANES)
    lines = pltpu.VMEM((n1 * ny, LANES), F32)
    ytab, shares, fine, local_out, local, outgoing[0] = pl.pallas_call(
        functools.partial(local_kernel, exy, n, ny, ct),
        out_shape=[shape(yrows, LANES), shape(4 * n2, LANES), block, shape(n1 * ny, LANES)]
        + [shape(4 * n1 + n2, LANES), shape(*outgoing[0].shape)],
        in_specs=[inside] * 4 + [anywhere],
        out_specs=[inside] * 5 + [anywhere],
        input_output_aliases={4: 5},
        scratch_shapes=[lines, lines],
        compiler_params=params,
        name="local_transform",
    )(field, xtab, pack, sums, outgoing[0])
    incoming = exx.all(outgoing)
    arrived, own, *outgoing = pl.pallas_call(
        functools.partial(second_kernel, exx, exy, n, ny, ct),
        out_shape=[shape(ARRIVED * ny, LANES), shape(2 * n2, LANES)]
        + [shape(y_rows(exy, n, s), LANES) for s in exy.steps],
        compiler_params=params,
        name="x_arrived",
    )(xown, xtab, shares, ytab, local, *incoming)
    some = pltpu.VMEM((ARRIVED * ny, LANES), F32)
    result, partial = pl.pallas_call(
        functools.partial(share_kernel, n, ny),
        out_shape=[shape(n1, 2, ny, LANES), block],
        out_specs=[anywhere, inside],
        scratch_shapes=[
            pltpu.VMEM((ny, LANES), F32),
            some,
            some,
            pltpu.VMEM((16 * n1, LANES), F32),
            dma((2,)),
        ],
        compiler_params=params,
        name="x_share",
    )(local_out.reshape(n1, ny, LANES), fine, arrived, xtab, shares, ytab)
    ranks = pl.pallas_call(
        functools.partial(rank_kernel, ny),
        out_shape=shape(8, ny, LANES),
        compiler_params=params,
        name="y_ranks",
    )(ytab)
    incoming = exy.all(outgoing)
    result = pl.pallas_call(
        functools.partial(third_kernel, exy, n, ny),
        out_shape=shape(n1, 2, ny, LANES),
        in_specs=[anywhere] + [inside] * (4 + len(incoming)),
        out_specs=anywhere,
        input_output_aliases={0: 0},
        scratch_shapes=[
            pltpu.VMEM((3 * n1 + 3 * n2, LANES), F32),
            pltpu.VMEM((n1, ny, LANES), F32),
            dma((4,)),
        ],
        compiler_params=params,
        name="y_update",
    )(result, partial, ytab, ranks, own, *incoming)
    return result.reshape(n, ny, LANES)


def solution(mesh):
    exx = Exchange("gx", mesh.shape["gx"], True)
    exy = Exchange("gy", mesh.shape["gy"], False)
    placed = (P("gx", "gy", None), P(), P())
    return jax.shard_map(
        functools.partial(on_device, exx, exy),
        mesh=mesh,
        in_specs=placed,
        out_specs=P("gx", "gy", None),
        check_vma=False,
    )
```

```python
import functools

import jax
import jax.numpy as jnp
from jax import lax
from jax.experimental import pallas as pl
from jax.experimental.pallas import tpu as pltpu
from jax.sharding import PartitionSpec as P

SMOOTH_X = 48
SMOOTH_Y = 96
F32 = jnp.float32
LANES = 128

GA, GB, GA2, GB2, HW1, HW2, CA0, CA1, KAP, LAM, CB0, CB1, VN, UN, HG = range(15)
SINGLES = 16


def offsets(n):
    n1, n2 = n // 2, n // 4
    names = ["wl", "wr", "al", "be", "u", "v"]
    where, row = {}, SINGLES
    for name in names:
        where[name] = row
        row += n1
    for name in names:
        where[name + "2"] = row
        row += n2
    return where, row


def combine(left, right):
    a, b, c, d = left
    p, q, r, s = right
    return (a * p + b * r, a * q + b * s, c * p + d * r, c * q + d * s)


def gather(x, position):
    out = []
    for t in range(position.shape[1] // LANES):
        place = position[:, t * LANES : (t + 1) * LANES]
        inner, block = place & (LANES - 1), place // LANES
        picked = None
        for b in range(x.shape[1] // LANES):
            part = jnp.take_along_axis(
                x[:, b * LANES : (b + 1) * LANES], inner, axis=1, mode="promise_in_bounds"
            )
            picked = part if picked is None else jnp.where(block == b, part, picked)
        out.append(picked)
    return out[0] if len(out) == 1 else jnp.concatenate(out, axis=1)


def down(x, by):
    return pltpu.roll(x, by, 0)


def build_pack(h, counts, places, locals_, stiffness, pack, sums):
    m = h.shape[1] // 2
    lanes = lax.broadcasted_iota(jnp.int32, (8, m), 1)
    rows = lax.broadcasted_iota(jnp.int32, (8, m), 0)
    lower = rows >= 4
    is_y = (rows & 2) == 2
    second = (rows & 1) == 1

    def by_axis(pair):
        return jnp.where(is_y, pair[1], pair[0])

    count = jnp.where(second, by_axis(counts) // 4, by_axis(counts) // 2)
    real = lanes < count
    last = lanes == count - 1
    k = jnp.where(lower, count - 1 - lanes, lanes)
    k = jnp.where(real, k, 0)
    first = jnp.where(second, 4 * k, 2 * k)
    even = gather(h, first) + jnp.where(second, gather(h, first + 1), 0.0)
    odd = gather(h, jnp.where(second, first + 2, first + 1))
    odd = odd + jnp.where(second, gather(h, jnp.where(second, first + 3, first)), 0.0)
    width = even + odd
    inverse = 1.0 / width
    s = by_axis(stiffness)
    stiff = s * inverse
    across = 1.0 / (stiff - width * (1.0 / 6.0))
    same = jnp.where(real, (width * (1.0 / 3.0) + stiff) * across, 1.0)
    into = jnp.where(real, across, 0.0)
    back = jnp.where(real, (s + width * width * (1.0 / 12.0)) * across, 0.0)
    product = (same, into, back, same)
    identity = (1.0, 0.0, 0.0, 1.0)

    def moved(matrix, by):
        head = lanes < by
        return [jnp.where(head, f, pltpu.roll(x, by, 1)) for x, f in zip(matrix, identity)]

    step = 1
    while step < m:
        if 2 * step < m:
            near = combine(product, moved(product, step))
            far = combine(moved(product, 2 * step), moved(product, 3 * step))
            product = combine(near, far)
            step *= 4
        else:
            product = combine(product, moved(product, step))
            step *= 2
    w = jnp.where(lower, product[1], product[0])
    total = jnp.where(lower, product[3], product[0])[:, m - 1 : m]
    here = jnp.where(lower, count - 1 - lanes, lanes - 1)
    there = jnp.where(lower, count - 2 - lanes, lanes)
    uv = gather(w, jnp.maximum(here, 0))
    uv = jnp.where(lower, jnp.where(real, uv, 0.0), jnp.where(lanes == 0, 1.0, uv))
    uv_next = gather(w, jnp.maximum(there, 0))
    uv_next = jnp.where(lower & (lanes >= count - 1), 0.0, uv_next)
    even = jnp.where(lower, down(even, 4), even)
    odd = jnp.where(lower, down(odd, 4), odd)
    inverse = jnp.where(lower, down(inverse, 4), inverse)
    ab = jnp.where(real, (uv * even + uv_next * odd) * (0.5 / total), 0.0)
    weight = jnp.where(lower, even, odd) * inverse
    weight = jnp.where(last, jnp.where(lower, 0.0, 1.0), weight)
    weight = jnp.where(real, weight, 0.0)
    pack[0:8, :] = uv
    pack[8:16, :] = ab
    pack[16:24, :] = weight
    other = down(weight, 4)
    wl = jnp.where(lower, other, weight)
    wr = jnp.where(lower, weight, other)
    fine = down(uv, 1)
    twice = jnp.where(real & second, 2 * lanes, 0)
    halo = -wr * gather(fine, jnp.minimum(twice + 2, m - 1))
    detail = gather(fine, twice + 1) - wl * gather(fine, twice) + halo
    valid = real & second
    halo = jnp.where(valid, halo, 0.0)
    detail = jnp.where(valid, detail, 0.0)
    place = by_axis(places)
    local = jnp.where(second, by_axis(locals_) // 4, by_axis(locals_) // 2)
    begin, end = place * local, (place + 1) * local

    def lane_sum(row, x):
        value = jnp.sum(x, axis=1, keepdims=True)
        sums[8 * row : 8 * row + 8, :] = jnp.broadcast_to(value, (8, LANES))
        return value

    def below(edge, x, y):
        return jnp.where(lanes < edge, x, 0.0) - jnp.where(lanes == edge - 1, y, 0.0)

    def above(edge, x, y):
        return jnp.where(lanes >= edge, x, 0.0) + jnp.where(lanes == edge - 1, y, 0.0)

    cross, cross_halo = ab * down(detail, 4), ab * down(halo, 4)
    alike, alike_halo = ab * detail, ab * halo
    lane_sum(0, below(begin, cross, cross_halo))
    lane_sum(1, below(end, cross, cross_halo))
    lane_sum(
        2, jnp.where(lower, above(end, alike, alike_halo), below(begin, alike, alike_halo))
    )
    edge = -ab * wr
    lane_sum(3, jnp.where(lanes == begin - 1, edge, 0.0))
    edge_last = lane_sum(4, jnp.where(lanes == end - 1, edge, 0.0))
    lane_sum(5, jnp.where(lanes == end - 1, wr, 0.0))
    ghost = lane_sum(6, jnp.where(lanes == end, uv, 0.0))
    ghost, edge_last = jnp.broadcast_to(ghost, (8, LANES)), jnp.broadcast_to(edge_last, (8, LANES))
    part = down(ghost, 4) * edge_last
    sums[56:64, :] = 1.0 + part - down(part, 4)


def build_table(pack, sums, axis, index, n, tab):
    m = pack.shape[1]
    n1, n2 = n // 2, n // 4
    a = 2 * axis
    for row, (block, r) in {
        GA: (3, a),
        GB: (3, a + 4),
        GA2: (3, a + 1),
        GB2: (3, a + 5),
        HW1: (5, a),
        HW2: (5, a + 1),
        CA0: (0, a + 1),
        CA1: (1, a + 1),
        KAP: (2, a + 1),
        LAM: (2, a + 5),
        CB0: (0, a + 5),
        CB1: (1, a + 5),
        VN: (6, a + 4),
        UN: (6, a),
        HG: (7, a),
    }.items():
        source = 8 * block + r
        tab[row : row + 1, :] = sums[source : source + 1, :]
    where, _ = offsets(n)
    for lv, rows, suffix_name in ((0, n1, ""), (1, n2, "2")):
        col = lax.broadcasted_iota(jnp.int32, (rows, m), 1)
        sub = lax.broadcasted_iota(jnp.int32, (rows, m), 0)
        mine = col == index * rows + sub
        mine_inner = mine & (sub < rows - 1)
        for name, block, below, mask in (
            ("wl", 2, 0, mine),
            ("wr", 2, 4, mine_inner),
            ("al", 1, 0, mine),
            ("be", 1, 4, mine),
            ("u", 0, 0, mine),
            ("v", 0, 4, mine),
        ):
            r = 8 * block + below + a + lv
            values = jnp.sum(jnp.where(mask, pack[r : r + 1, :], 0.0), axis=1, keepdims=True)
            start = where[name + suffix_name]
            tab[start : start + rows, :] = jnp.broadcast_to(values, (rows, LANES))


def one_level(even, odd, tab, where, suffix, ga, gb, from_left, from_right):
    def c(name, i):
        row = where[name + suffix] + i
        return tab[row : row + 1, :]

    count = len(even)
    details = []
    for i in range(count):
        e = odd[i] - c("wl", i) * even[i]
        if i + 1 < count:
            e = e - c("wr", i) * even[i + 1]
        details.append(e)
    first = tab[ga : ga + 1, :] * even[0]
    acc = first if from_left is None else from_left + first
    lefts = []
    for i in range(count):
        lefts.append(acc)
        acc = acc + c("al", i) * details[i]
    left_end = acc
    acc = from_right
    rights = [None] * count
    for i in reversed(range(count)):
        term = c("be", i) * details[i]
        acc = term if acc is None else acc + term
        rights[i] = acc
    nodes = [even[i] + c("v", i) * lefts[i] + c("u", i) * rights[i] for i in range(count)]
    right_end = rights[0] + tab[gb : gb + 1, :] * even[0]
    return details, nodes, left_end, right_end


def single(tab, row):
    return tab[row : row + 1, :]


def summaries(tab, p1, q1, p2, q2):
    to_right = p2 + single(tab, KAP) * q1 - single(tab, CA1) * p1
    to_left = q2 + single(tab, LAM) * p1 + single(tab, CB0) * q1
    return to_right, to_left


def second_sums(tab, left, right, left2, right2, p1, q1):
    left_second = left2 + single(tab, CA0) * left + single(tab, KAP) * (q1 + right)
    right_second = right2 - single(tab, CB1) * right + single(tab, LAM) * (left + p1)
    return left_second, right_second


class Exchange:
    def __init__(self, axis, count, paired):
        self.axis, self.count = axis, count
        if paired and count % 2 == 0:
            shifts = range(2, count, 2)
            self.direct = [(0, 1)] + [(s, 0) for s in shifts]
            self.passed = [(s, 1) for s in shifts]
        else:
            self.direct = [(s, 0) for s in range(1, count)]
            self.passed = []
        self.steps = self.direct + self.passed

    def target(self, i, step):
        return ((i + step[0]) % self.count) ^ step[1]

    def source(self, i, step):
        return ((i ^ step[1]) + self.count - step[0]) % self.count

    def near(self, step):
        return any(self.source(i, step) == i + 1 for i in range(self.count - 1))

    def carries(self, step):
        return self.near(step) or ((step[0], 1) in self.passed and self.near((step[0], 1)))

    def send(self, step, x):
        pairs = [(i, self.target(i, step)) for i in range(self.count)]
        return lax.ppermute(x, self.axis, pairs)

    def all(self, messages):
        got = [self.send(s, x) for s, x in zip(self.direct, messages)]
        return got + [self.send((0, 1), x) for x in got[1 : 1 + len(self.passed)]]


def x_tile(tab, where, field, n, cols, sums):
    even = [field[2 * i, cols, :] for i in range(n // 2)]
    odd = [field[2 * i + 1, cols, :] for i in range(n // 2)]
    left, right = sums if sums else (None, None)
    return one_level(even, odd, tab, where, "", GA, GB, left, right)


def first_kernel(exx, exy, n, ny, stiffness, ct, hx_ref, hy_ref, source, *refs):
    field, pack, sums, tab, own = refs[:5]
    messages = refs[5 : 5 + len(exx.direct)]
    hx, hy, sems, spacing_sems = refs[5 + len(exx.direct) :]
    ex = exx
    index = lax.axis_index(exx.axis)
    tiles = ny // ct

    def fetch(t):
        part = pl.ds(t * (n // 1), n // 1)
        return pltpu.make_async_copy(source.at[part], field.at[part], sems.at[t])

    spacings = [
        pltpu.make_async_copy(a, b, spacing_sems.at[i])
        for i, (a, b) in enumerate(((hx_ref, hx), (hy_ref, hy)))
    ]
    for copy in spacings:
        copy.start()
    for t in range(1):
        fetch(t).start()
    for copy in spacings:
        copy.wait()
    lanes = 2 * pack.shape[1]
    counts = (hx.shape[1], hy.shape[1])

    def row(ref):
        x = ref[...]
        if x.shape[1] < lanes:
            x = jnp.concatenate([x, jnp.ones((1, lanes - x.shape[1]), F32)], axis=1)
        return jnp.broadcast_to(x, (8, lanes))

    is_y = (lax.broadcasted_iota(jnp.int32, (8, lanes), 0) & 2) == 2
    build_pack(
        jnp.where(is_y, row(hy), row(hx)),
        counts,
        (index, lax.axis_index(exy.axis)),
        (n, ny),
        stiffness,
        pack,
        sums,
    )
    build_table(pack, sums, 0, index, n, tab)
    for t in range(1):
        fetch(t).wait()
    where, _ = offsets(n)

    def body(t, carry):
        begin = pl.multiple_of(t * ct, ct)
        cols = pl.ds(begin, ct)
        _, nodes, p1, q1 = x_tile(tab, where, field, n, cols, None)
        _, _, p2, q2 = one_level(nodes[0::2], nodes[1::2], tab, where, "2", GA2, GB2, None, None)
        p2, q2 = summaries(tab, p1, q1, p2, q2)
        own[cols, :] = p1
        own[pl.ds(begin + ny, ct), :] = q1
        for step, message in zip(ex.direct, messages):
            upward = ex.target(index, step) > index
            message[cols, :] = jnp.where(upward, p1, q1)
            message[pl.ds(begin + ny, ct), :] = jnp.where(upward, p2, q2)
            if ex.carries(step):
                message[pl.ds(begin + 2 * ny, ct), :] = field[0, cols, :]
        return carry

    lax.fori_loop(0, tiles, body, 0)


def column(ref, j, count, ny):
    return ref[pl.ds(j, count, stride=ny), :]


def local_kernel(exy, n, ny, ct, field, xtab, pack, sums, passing, *refs):
    ytab, shares, fine, out, local, passed, full, mixed = refs
    n1, n2 = n // 2, n // 4
    where, _ = offsets(n)
    build_table(pack, sums, 1, lax.axis_index(exy.axis), ny, ytab)

    for r, name in enumerate(("v", "u")):
        nodes = [single(xtab, where[name] + i) for i in range(n1)]
        details, nodes, _, _ = one_level(
            nodes[0::2], nodes[1::2], xtab, where, "2", GA2, GB2, None, None
        )
        for i in range(n2):
            shares[r * n2 + i : r * n2 + i + 1, :] = nodes[i]
            shares[(2 + r) * n2 + i : (2 + r) * n2 + i + 1, :] = details[i]

    def body(t, carry):
        begin = pl.multiple_of(t * ct, ct)
        cols = pl.ds(begin, ct)
        details, nodes, _, _ = x_tile(xtab, where, field, n, cols, None)
        for i in range(n1):
            fine[i, cols, :] = details[i]
            full[pl.ds(i * ny + begin, ct), :] = nodes[i]
        details, nodes, _, _ = one_level(
            nodes[0::2], nodes[1::2], xtab, where, "2", GA2, GB2, None, None
        )
        for i in range(n2):
            mixed[pl.ds(i * ny + begin, ct), :] = nodes[i]
            mixed[pl.ds((n2 + i) * ny + begin, ct), :] = details[i]
        return carry

    lax.fori_loop(0, ny // ct, body, 0)

    m1, m2 = ny // 2, ny // 4
    ywhere, _ = offsets(ny)
    for j in range(m1):
        e = column(full, 2 * j + 1, n1, ny)
        e = e - single(ytab, ywhere["wl"] + j) * column(full, 2 * j, n1, ny)
        if j + 1 < m1:
            e = e - single(ytab, ywhere["wr"] + j) * column(full, 2 * j + 2, n1, ny)
        out[pl.ds(2 * j + 1, n1, stride=ny), :] = e
    even = [column(mixed, 2 * j, n1, ny) for j in range(m1)]
    odd = [column(mixed, 2 * j + 1, n1, ny) for j in range(m1)]
    _, nodes, p1, q1 = one_level(even, odd, ytab, ywhere, "", GA, GB, None, None)
    for j in range(m1):
        out[pl.ds(ny + 2 * j, n2, stride=2 * ny), :] = nodes[j][n2:]
    thin = [x[:n2] for x in nodes]
    details, nodes, p2, q2 = one_level(
        thin[0::2], thin[1::2], ytab, ywhere, "2", GA2, GB2, None, None
    )
    for j in range(m2):
        out[pl.ds(4 * j, n2, stride=2 * ny), :] = nodes[j]
        out[pl.ds(4 * j + 2, n2, stride=2 * ny), :] = details[j]
    p2, q2 = summaries(ytab, p1[:n2], q1[:n2], p2, q2)
    local[:n1, :] = p1
    local[n1 : n1 + n2, :] = p2
    local[n1 + n2 : 2 * n1 + n2, :] = q1
    local[2 * n1 + n2 : 3 * n1, :] = q2
    local[3 * n1 : 4 * n1, :] = column(full, 0, n1, ny)
    local[4 * n1 :, :] = column(mixed, 0, n2, ny)


LEFT, RIGHT, LEFT2, RIGHT2, GHOST, HALO, ARRIVED = 0, 1, 2, 3, 4, 5, 8


def arrived_y(ytab, arrived, ny):
    m1 = ny // 2
    where, _ = offsets(ny)
    even = [column(arrived, 2 * j, ARRIVED, ny) for j in range(m1)]
    odd = [column(arrived, 2 * j + 1, ARRIVED, ny) for j in range(m1)]
    details, nodes, p1, q1 = one_level(even, odd, ytab, where, "", GA, GB, None, None)
    details2, nodes2, p2, q2 = one_level(
        nodes[0::2], nodes[1::2], ytab, where, "2", GA2, GB2, None, None
    )
    return details, nodes, details2, nodes2, p1, q1, p2, q2


def second_kernel(exx, exy, n, ny, ct, *refs):
    own, xtab, shares, ytab, local = refs[:5]
    incoming = refs[5 : 5 + len(exx.steps)]
    arrived, yown = refs[5 + len(exx.steps) : 7 + len(exx.steps)]
    messages = refs[7 + len(exx.steps) :]
    index = lax.axis_index(exx.axis)
    n1, n2 = n // 2, n // 4
    where, _ = offsets(n)

    def body(t, carry):
        begin = pl.multiple_of(t * ct, ct)
        cols = pl.ds(begin, ct)
        zero = jnp.zeros((ct, LANES), F32)
        left = right = left2 = right2 = halo = zero
        for step, message in zip(exx.steps, incoming):
            source = exx.source(index, step)
            lower = source < index
            one = message[cols, :]
            two = message[pl.ds(begin + ny, ct), :]
            left = left + jnp.where(lower, one, 0.0)
            right = right + jnp.where(lower, 0.0, one)
            left2 = left2 + jnp.where(lower, two, 0.0)
            right2 = right2 + jnp.where(lower, 0.0, two)
            if exx.near(step):
                halo = jnp.where(source == index + 1, message[pl.ds(begin + 2 * ny, ct), :], halo)
        p1, q1 = own[cols, :], own[pl.ds(begin + ny, ct), :]
        left2, right2 = second_sums(xtab, left, right, left2, right2, p1, q1)
        ghost = single(xtab, HG) * halo + single(xtab, VN) * (left + p1) + single(xtab, UN) * right
        for row, value in (
            (LEFT, left),
            (RIGHT, right),
            (LEFT2, left2),
            (RIGHT2, right2),
            (GHOST, ghost),
            (HALO, halo),
            (HALO + 1, zero),
            (HALO + 2, zero),
        ):
            arrived[pl.ds(row * ny + begin, ct), :] = value
        return carry

    lax.fori_loop(0, ny // ct, body, 0)
    _, _, _, _, p1, q1, p2, q2 = arrived_y(ytab, arrived, ny)
    p2, q2 = summaries(ytab, p1, q1, p2, q2)
    first = column(arrived, 0, ARRIVED, ny)
    nodes_v, nodes_u = shares[:n2, :], shares[n2 : 2 * n2, :]
    details_v, details_u = shares[2 * n2 : 3 * n2, :], shares[3 * n2 :, :]

    def rows(name, count):
        return xtab[where[name] : where[name] + count, :]

    def coarse(x):
        return (
            nodes_v * x[LEFT : LEFT + 1]
            + nodes_u * x[RIGHT : RIGHT + 1]
            + rows("v2", n2) * x[LEFT2 : LEFT2 + 1]
            + rows("u2", n2) * x[RIGHT2 : RIGHT2 + 1]
        )

    is_last = lax.broadcasted_iota(jnp.int32, (n2, LANES), 0) == n2 - 1

    def detail(x):
        ghost = jnp.where(is_last, single(xtab, HW2) * x[GHOST : GHOST + 1], 0.0)
        return details_v * x[LEFT : LEFT + 1] + details_u * x[RIGHT : RIGHT + 1] - ghost

    p1c, p1d = local[:n2, :] + coarse(p1), local[n2:n1, :] + detail(p1)
    p2c = local[n1 : n1 + n2, :] + coarse(p2)
    q1c = local[n1 + n2 : 2 * n1, :] + coarse(q1)
    q1d = local[2 * n1 : 2 * n1 + n2, :] + detail(q1)
    q2c = local[2 * n1 + n2 : 3 * n1, :] + coarse(q2)
    yown[:n2, :] = p1c
    yown[n2:, :] = q1c
    yindex = lax.axis_index(exy.axis)
    for step, message in zip(exy.steps, messages):
        upward = exy.target(yindex, step) > yindex
        message[:n2, :] = jnp.where(upward, p1c, q1c)
        message[n2:n1, :] = jnp.where(upward, p1d, q1d)
        message[n1 : n1 + n2, :] = jnp.where(upward, p2c, q2c)
        if exy.near(step):
            message[n1 + n2 : 2 * n1 + n2, :] = (
                local[3 * n1 : 4 * n1, :]
                + rows("v", n1) * first[LEFT : LEFT + 1]
                + rows("u", n1) * first[RIGHT : RIGHT + 1]
            )
            message[2 * n1 + n2 : 2 * (n1 + n2), :] = local[4 * n1 :, :] + coarse(first)


def share_kernel(n, ny, own_part, fine, arrived, xtab, shares, ytab, result, out, *refs):
    last, one, two, blend, sems = refs
    n1, n2 = n // 2, n // 4
    m1, m2 = ny // 2, ny // 4
    where, _ = offsets(n)
    last[...] = fine[n1 - 1] - single(xtab, HW1) * arrived[HALO * ny : (HALO + 1) * ny, :]
    copies = [
        pltpu.make_async_copy(fine.at[: n1 - 1], result.at[: n1 - 1, 1], sems.at[0]),
        pltpu.make_async_copy(last, result.at[n1 - 1, 1], sems.at[1]),
    ]
    for copy in copies:
        copy.start()
    details, nodes, details2, nodes2, _, _, _, _ = arrived_y(ytab, arrived, ny)
    side = lax.broadcasted_iota(jnp.int32, (ARRIVED, LANES), 0) < LEFT2
    for j in range(m1):
        at = pl.ds(2 * j + 1, ARRIVED, stride=ny)
        one[at, :] = details[j]
        two[at, :] = jnp.where(side, details[j], 0.0)
        one[pl.ds(2 * j, ARRIVED, stride=ny), :] = nodes[j]
    for j in range(m2):
        two[pl.ds(4 * j, ARRIVED, stride=ny), :] = nodes2[j]
        two[pl.ds(4 * j + 2, ARRIVED, stride=ny), :] = details2[j]
    odd = (lax.broadcasted_iota(jnp.int32, (8, LANES), 0) & 1) == 1
    for k in range(n1):
        for r, name in enumerate(("v", "u")):
            block = (2 + r if k % 2 else r) * n2 + k // 2
            mixture = jnp.where(odd, single(xtab, where[name] + k), single(shares, block))
            blend[16 * k + 8 * r : 16 * k + 8 * r + 8, :] = mixture

    def body(t, carry):
        begin = pl.multiple_of(t * 8, 8)
        cols = pl.ds(begin, 8)

        def tile(ref, r):
            return ref[pl.ds(r * ny + begin, 8), :]

        ones = [tile(one, r) for r in (LEFT, RIGHT)]
        twos = [tile(two, r) for r in (LEFT, RIGHT, LEFT2, RIGHT2)]
        ghost = jnp.where(odd, 0.0, single(xtab, HW2) * tile(one, GHOST))
        for k in range(n1):
            x = own_part[k, cols, :]
            source = ones if k % 2 else twos
            for r in range(2):
                x = x + blend[16 * k + 8 * r : 16 * k + 8 * r + 8, :] * source[r]
            if k % 2 == 0:
                x = x + single(xtab, where["v2"] + k // 2) * twos[2]
                x = x + single(xtab, where["u2"] + k // 2) * twos[3]
            elif k == n1 - 1:
                x = x - ghost
            out[k, cols, :] = x
        return carry

    lax.fori_loop(0, ny // 8, body, 0)
    for copy in copies:
        copy.wait()


def rank_kernel(ny, tab, ranks):
    where, _ = offsets(ny)
    m1, m2 = ny // 2, ny // 4
    ranks[...] = jnp.zeros_like(ranks)

    def put(rank, j, value):
        ranks[rank, j : j + 1, :] = value

    for rank, name, end in ((0, "v", VN), (1, "u", UN)):
        nodes = [single(tab, where[name] + i) for i in range(m1)]
        for i in range(m1):
            put(rank, 2 * i, nodes[i])
        details, nodes2, _, _ = one_level(
            nodes[0::2], nodes[1::2], tab, where, "2", GA2, GB2, None, None
        )
        details[-1] = details[-1] - single(tab, HW2) * single(tab, end)
        for i in range(m2):
            put(2 + rank, 4 * i, nodes2[i])
            put(2 + rank, 4 * i + 2, details[i])
            put(4 + rank, 4 * i, single(tab, where[name + "2"] + i))
    put(6, ny - 1, -single(tab, HW1))
    put(7, ny - 2, -single(tab, HW2))


def third_kernel(ex, n, ny, *refs):
    partial, tab, ranks, own = refs[1:5]
    incoming = refs[5 : 5 + len(ex.steps)]
    result, sums, done, sems = refs[5 + len(ex.steps) :]
    n1, n2 = n // 2, n // 4
    index = lax.axis_index(ex.axis)
    zero, zero2 = jnp.zeros((n1, LANES), F32), jnp.zeros((n2, LANES), F32)
    left, right, left2, right2, halo, halo2 = zero, zero, zero2, zero2, zero, zero2
    for step, message in zip(ex.steps, incoming):
        source = ex.source(index, step)
        lower = source < index
        one, two = message[:n1, :], message[n1 : n1 + n2, :]
        left = left + jnp.where(lower, one, 0.0)
        right = right + jnp.where(lower, 0.0, one)
        left2 = left2 + jnp.where(lower, two, 0.0)
        right2 = right2 + jnp.where(lower, 0.0, two)
        if ex.near(step):
            mine = source == index + 1
            halo = jnp.where(mine, message[n1 + n2 : 2 * n1 + n2, :], halo)
            halo2 = jnp.where(mine, message[2 * n1 + n2 : 2 * (n1 + n2), :], halo2)
    p1, q1 = own[:n2, :], own[n2:, :]
    left2, right2 = second_sums(tab, left[:n2], right[:n2], left2, right2, p1, q1)
    ghost = single(tab, HG) * halo2 + single(tab, VN) * p1
    sums[0:n1, :] = left
    sums[n1 : 2 * n1, :] = right
    sums[2 * n1 : 3 * n1, :] = halo
    sums[3 * n1 : 3 * n1 + n2, :] = left2
    sums[3 * n1 + n2 : 3 * n1 + 2 * n2, :] = right2
    sums[3 * n1 + 2 * n2 : 3 * n1 + 3 * n2, :] = ghost

    def row(i):
        return sums[i : i + 1, :]

    group = n1 // 4

    def put(g):
        part = pl.ds(g * group, group)
        return pltpu.make_async_copy(done.at[part], result.at[part, 0], sems.at[g])

    for g in range(4):
        for t in range(ny // 8):
            cols = slice(8 * t, 8 * t + 8)
            tables = [ranks[r, cols, :] for r in range(8)]
            for k in range(g * group, (g + 1) * group):
                x = partial[k, cols, :] + tables[6] * row(2 * n1 + k)
                if k % 2:
                    i = n2 + k // 2
                    x = x + tables[0] * row(i) + tables[1] * row(n1 + i)
                else:
                    i = k // 2
                    x = x + tables[2] * row(i) + tables[3] * row(n1 + i)
                    x = x + tables[4] * row(3 * n1 + i) + tables[5] * row(3 * n1 + n2 + i)
                    x = x + tables[7] * row(3 * n1 + 2 * n2 + i)
                done[k, cols, :] = x
        put(g).start()
    for g in range(4):
        put(g).wait()


def y_rows(ex, n, step):
    return 3 * n // 4 * (2 if ex.near(ex.direct[-1]) else 1) + 8 * (ex.count - 1 - step[0])


def x_rows(ex, ny, step):
    return (3 if ex.carries(step) else 2) * ny


def shape(*dims):
    return jax.ShapeDtypeStruct(dims, F32)


def on_device(exx, exy, field, spacing_x, spacing_y):
    n, ny, _ = field.shape
    n1, n2 = n // 2, n // 4
    ct = 32
    xrows = offsets(n)[1]
    yrows = offsets(ny)[1]
    params = pltpu.CompilerParams(vmem_limit_bytes=40 * 1024 * 1024)
    anywhere = pl.BlockSpec(memory_space=pl.ANY)
    inside = pl.BlockSpec(memory_space=pltpu.VMEM)
    dma = pltpu.SemaphoreType.DMA
    operands = (spacing_x[None], spacing_y[None], field)
    lanes = max(spacing_x.shape[0], spacing_y.shape[0])
    lanes = (lanes + 2 * LANES - 1) // (2 * LANES) * LANES
    stiffness = (float(SMOOTH_X) ** 2, float(SMOOTH_Y) ** 2)
    field, pack, sums, xtab, xown, *outgoing = pl.pallas_call(
        functools.partial(first_kernel, exx, exy, n, ny, stiffness, ct),
        out_shape=[shape(n, ny, LANES), shape(24, lanes), shape(64, LANES)]
        + [shape(xrows, LANES), shape(2 * ny, LANES)]
        + [shape(x_rows(exx, ny, s), LANES) for s in exx.direct],
        in_specs=[anywhere] * 3,
        scratch_shapes=[
            pltpu.VMEM((1, spacing_x.shape[0]), F32),
            pltpu.VMEM((1, spacing_y.shape[0]), F32),
            dma((1,)),
            dma((2,)),
        ],
        compiler_params=params,
        name="x_summary",
    )(*[pltpu.with_memory_space_constraint(a, pltpu.HBM) for a in operands])
    block = shape(n1, ny, LANES)
    lines = pltpu.VMEM((n1 * ny, LANES), F32)
    ytab, shares, fine, local_out, local, outgoing[0] = pl.pallas_call(
        functools.partial(local_kernel, exy, n, ny, ct),
        out_shape=[shape(yrows, LANES), shape(4 * n2, LANES), block, shape(n1 * ny, LANES)]
        + [shape(4 * n1 + n2, LANES), shape(*outgoing[0].shape)],
        in_specs=[inside] * 4 + [anywhere],
        out_specs=[inside] * 5 + [anywhere],
        input_output_aliases={4: 5},
        scratch_shapes=[lines, lines],
        compiler_params=params,
        name="local_transform",
    )(field, xtab, pack, sums, outgoing[0])
    incoming = exx.all(outgoing)
    arrived, own, *outgoing = pl.pallas_call(
        functools.partial(second_kernel, exx, exy, n, ny, ct),
        out_shape=[shape(ARRIVED * ny, LANES), shape(2 * n2, LANES)]
        + [shape(y_rows(exy, n, s), LANES) for s in exy.steps],
        compiler_params=params,
        name="x_arrived",
    )(xown, xtab, shares, ytab, local, *incoming)
    some = pltpu.VMEM((ARRIVED * ny, LANES), F32)
    result, partial = pl.pallas_call(
        functools.partial(share_kernel, n, ny),
        out_shape=[shape(n1, 2, ny, LANES), block],
        out_specs=[anywhere, inside],
        scratch_shapes=[
            pltpu.VMEM((ny, LANES), F32),
            some,
            some,
            pltpu.VMEM((16 * n1, LANES), F32),
            dma((2,)),
        ],
        compiler_params=params,
        name="x_share",
    )(local_out.reshape(n1, ny, LANES), fine, arrived, xtab, shares, ytab)
    ranks = pl.pallas_call(
        functools.partial(rank_kernel, ny),
        out_shape=shape(8, ny, LANES),
        compiler_params=params,
        name="y_ranks",
    )(ytab)
    incoming = exy.all(outgoing)
    result = pl.pallas_call(
        functools.partial(third_kernel, exy, n, ny),
        out_shape=shape(n1, 2, ny, LANES),
        in_specs=[anywhere] + [inside] * (4 + len(incoming)),
        out_specs=anywhere,
        input_output_aliases={0: 0},
        scratch_shapes=[
            pltpu.VMEM((3 * n1 + 3 * n2, LANES), F32),
            pltpu.VMEM((n1, ny, LANES), F32),
            dma((4,)),
        ],
        compiler_params=params,
        name="y_update",
    )(result, partial, ytab, ranks, own, *incoming)
    return result.reshape(n, ny, LANES)


def solution(mesh):
    exx = Exchange("gx", mesh.shape["gx"], True)
    exy = Exchange("gy", mesh.shape["gy"], False)
    placed = (P("gx", "gy", None), P(), P())
    return jax.shard_map(
        functools.partial(on_device, exx, exy),
        mesh=mesh,
        in_specs=placed,
        out_specs=P("gx", "gy", None),
        check_vma=False,
    )
```

```python
import functools

import jax
import jax.numpy as jnp
from jax import lax
from jax.experimental import pallas as pl
from jax.experimental.pallas import tpu as pltpu
from jax.sharding import PartitionSpec as P

SMOOTH_X = 48
SMOOTH_Y = 96
F32 = jnp.float32
LANES = 128

GA, GB, GA2, GB2, HW1, HW2, CA0, CA1, KAP, LAM, CB0, CB1, VN, UN, HG = range(15)
SINGLES = 16


def offsets(n):
    n1, n2 = n // 2, n // 4
    names = ["wl", "wr", "al", "be", "u", "v"]
    where, row = {}, SINGLES
    for name in names:
        where[name] = row
        row += n1
    for name in names:
        where[name + "2"] = row
        row += n2
    return where, row


def combine(left, right):
    a, b, c, d = left
    p, q, r, s = right
    return (a * p + b * r, a * q + b * s, c * p + d * r, c * q + d * s)


def gather(x, position):
    out = []
    for t in range(position.shape[1] // LANES):
        place = position[:, t * LANES : (t + 1) * LANES]
        inner, block = place & (LANES - 1), place // LANES
        picked = None
        for b in range(x.shape[1] // LANES):
            part = jnp.take_along_axis(
                x[:, b * LANES : (b + 1) * LANES], inner, axis=1, mode="promise_in_bounds"
            )
            picked = part if picked is None else jnp.where(block == b, part, picked)
        out.append(picked)
    return out[0] if len(out) == 1 else jnp.concatenate(out, axis=1)


def down(x, by):
    return pltpu.roll(x, by, 0)


def build_pack(h, counts, places, locals_, stiffness, pack, sums):
    m = h.shape[1] // 2
    lanes = lax.broadcasted_iota(jnp.int32, (8, m), 1)
    rows = lax.broadcasted_iota(jnp.int32, (8, m), 0)
    lower = rows >= 4
    is_y = (rows & 2) == 2
    second = (rows & 1) == 1

    def by_axis(pair):
        return jnp.where(is_y, pair[1], pair[0])

    count = jnp.where(second, by_axis(counts) // 4, by_axis(counts) // 2)
    real = lanes < count
    last = lanes == count - 1
    k = jnp.where(lower, count - 1 - lanes, lanes)
    k = jnp.where(real, k, 0)
    first = jnp.where(second, 4 * k, 2 * k)
    even = gather(h, first) + jnp.where(second, gather(h, first + 1), 0.0)
    odd = gather(h, jnp.where(second, first + 2, first + 1))
    odd = odd + jnp.where(second, gather(h, jnp.where(second, first + 3, first)), 0.0)
    width = even + odd
    inverse = 1.0 / width
    s = by_axis(stiffness)
    stiff = s * inverse
    across = 1.0 / (stiff - width * (1.0 / 6.0))
    same = jnp.where(real, (width * (1.0 / 3.0) + stiff) * across, 1.0)
    into = jnp.where(real, across, 0.0)
    back = jnp.where(real, (s + width * width * (1.0 / 12.0)) * across, 0.0)
    product = (same, into, back, same)
    identity = (1.0, 0.0, 0.0, 1.0)

    def moved(matrix, by):
        head = lanes < by
        return [jnp.where(head, f, pltpu.roll(x, by, 1)) for x, f in zip(matrix, identity)]

    step = 1
    while step < m:
        if 2 * step < m:
            near = combine(product, moved(product, step))
            far = combine(moved(product, 2 * step), moved(product, 3 * step))
            product = combine(near, far)
            step *= 4
        else:
            product = combine(product, moved(product, step))
            step *= 2
    w = jnp.where(lower, product[1], product[0])
    total = jnp.where(lower, product[3], product[0])[:, m - 1 : m]
    here = jnp.where(lower, count - 1 - lanes, lanes - 1)
    there = jnp.where(lower, count - 2 - lanes, lanes)
    uv = gather(w, jnp.maximum(here, 0))
    uv = jnp.where(lower, jnp.where(real, uv, 0.0), jnp.where(lanes == 0, 1.0, uv))
    uv_next = gather(w, jnp.maximum(there, 0))
    uv_next = jnp.where(lower & (lanes >= count - 1), 0.0, uv_next)
    even = jnp.where(lower, down(even, 4), even)
    odd = jnp.where(lower, down(odd, 4), odd)
    inverse = jnp.where(lower, down(inverse, 4), inverse)
    ab = jnp.where(real, (uv * even + uv_next * odd) * (0.5 / total), 0.0)
    weight = jnp.where(lower, even, odd) * inverse
    weight = jnp.where(last, jnp.where(lower, 0.0, 1.0), weight)
    weight = jnp.where(real, weight, 0.0)
    pack[0:8, :] = uv
    pack[8:16, :] = ab
    pack[16:24, :] = weight
    other = down(weight, 4)
    wl = jnp.where(lower, other, weight)
    wr = jnp.where(lower, weight, other)
    fine = down(uv, 1)
    twice = jnp.where(real & second, 2 * lanes, 0)
    halo = -wr * gather(fine, jnp.minimum(twice + 2, m - 1))
    detail = gather(fine, twice + 1) - wl * gather(fine, twice) + halo
    valid = real & second
    halo = jnp.where(valid, halo, 0.0)
    detail = jnp.where(valid, detail, 0.0)
    place = by_axis(places)
    local = jnp.where(second, by_axis(locals_) // 4, by_axis(locals_) // 2)
    begin, end = place * local, (place + 1) * local

    def lane_sum(row, x):
        value = jnp.sum(x, axis=1, keepdims=True)
        sums[8 * row : 8 * row + 8, :] = jnp.broadcast_to(value, (8, LANES))
        return value

    def below(edge, x, y):
        return jnp.where(lanes < edge, x, 0.0) - jnp.where(lanes == edge - 1, y, 0.0)

    def above(edge, x, y):
        return jnp.where(lanes >= edge, x, 0.0) + jnp.where(lanes == edge - 1, y, 0.0)

    cross, cross_halo = ab * down(detail, 4), ab * down(halo, 4)
    alike, alike_halo = ab * detail, ab * halo
    lane_sum(0, below(begin, cross, cross_halo))
    lane_sum(1, below(end, cross, cross_halo))
    lane_sum(
        2, jnp.where(lower, above(end, alike, alike_halo), below(begin, alike, alike_halo))
    )
    edge = -ab * wr
    lane_sum(3, jnp.where(lanes == begin - 1, edge, 0.0))
    edge_last = lane_sum(4, jnp.where(lanes == end - 1, edge, 0.0))
    lane_sum(5, jnp.where(lanes == end - 1, wr, 0.0))
    ghost = lane_sum(6, jnp.where(lanes == end, uv, 0.0))
    ghost, edge_last = jnp.broadcast_to(ghost, (8, LANES)), jnp.broadcast_to(edge_last, (8, LANES))
    part = down(ghost, 4) * edge_last
    sums[56:64, :] = 1.0 + part - down(part, 4)


def build_table(pack, sums, axis, index, n, tab):
    m = pack.shape[1]
    n1, n2 = n // 2, n // 4
    a = 2 * axis
    for row, (block, r) in {
        GA: (3, a),
        GB: (3, a + 4),
        GA2: (3, a + 1),
        GB2: (3, a + 5),
        HW1: (5, a),
        HW2: (5, a + 1),
        CA0: (0, a + 1),
        CA1: (1, a + 1),
        KAP: (2, a + 1),
        LAM: (2, a + 5),
        CB0: (0, a + 5),
        CB1: (1, a + 5),
        VN: (6, a + 4),
        UN: (6, a),
        HG: (7, a),
    }.items():
        source = 8 * block + r
        tab[row : row + 1, :] = sums[source : source + 1, :]
    where, _ = offsets(n)
    for lv, rows, suffix_name in ((0, n1, ""), (1, n2, "2")):
        col = lax.broadcasted_iota(jnp.int32, (rows, m), 1)
        sub = lax.broadcasted_iota(jnp.int32, (rows, m), 0)
        mine = col == index * rows + sub
        mine_inner = mine & (sub < rows - 1)
        for name, block, below, mask in (
            ("wl", 2, 0, mine),
            ("wr", 2, 4, mine_inner),
            ("al", 1, 0, mine),
            ("be", 1, 4, mine),
            ("u", 0, 0, mine),
            ("v", 0, 4, mine),
        ):
            r = 8 * block + below + a + lv
            values = jnp.sum(jnp.where(mask, pack[r : r + 1, :], 0.0), axis=1, keepdims=True)
            start = where[name + suffix_name]
            tab[start : start + rows, :] = jnp.broadcast_to(values, (rows, LANES))


def one_level(even, odd, tab, where, suffix, ga, gb, from_left, from_right):
    def c(name, i):
        row = where[name + suffix] + i
        return tab[row : row + 1, :]

    count = len(even)
    details = []
    for i in range(count):
        e = odd[i] - c("wl", i) * even[i]
        if i + 1 < count:
            e = e - c("wr", i) * even[i + 1]
        details.append(e)
    first = tab[ga : ga + 1, :] * even[0]
    acc = first if from_left is None else from_left + first
    lefts = []
    for i in range(count):
        lefts.append(acc)
        acc = acc + c("al", i) * details[i]
    left_end = acc
    acc = from_right
    rights = [None] * count
    for i in reversed(range(count)):
        term = c("be", i) * details[i]
        acc = term if acc is None else acc + term
        rights[i] = acc
    nodes = [even[i] + c("v", i) * lefts[i] + c("u", i) * rights[i] for i in range(count)]
    right_end = rights[0] + tab[gb : gb + 1, :] * even[0]
    return details, nodes, left_end, right_end


def single(tab, row):
    return tab[row : row + 1, :]


def summaries(tab, p1, q1, p2, q2):
    to_right = p2 + single(tab, KAP) * q1 - single(tab, CA1) * p1
    to_left = q2 + single(tab, LAM) * p1 + single(tab, CB0) * q1
    return to_right, to_left


def second_sums(tab, left, right, left2, right2, p1, q1):
    left_second = left2 + single(tab, CA0) * left + single(tab, KAP) * (q1 + right)
    right_second = right2 - single(tab, CB1) * right + single(tab, LAM) * (left + p1)
    return left_second, right_second


class Exchange:
    def __init__(self, axis, count, paired):
        self.axis, self.count = axis, count
        self.folded = not paired and count & (count - 1) == 0
        if paired and count % 2 == 0:
            shifts = range(2, count, 2)
            self.direct = [(0, 1)] + [(s, 0) for s in shifts]
            self.passed = [(s, 1) for s in shifts]
        else:
            self.direct = [(s, 0) for s in range(1, count)]
            self.passed = []
        self.steps = self.direct + self.passed

    def position(self, i):
        if not self.folded:
            return i
        shift = 1
        while shift < self.count:
            i = i ^ (i >> shift)
            shift *= 2
        return i

    def device(self, position):
        return position ^ (position >> 1) if self.folded else position

    def target(self, i, step):
        return self.device((self.position(i) + step[0]) % self.count) ^ step[1]

    def source(self, i, step):
        return self.device((self.position(i ^ step[1]) + self.count - step[0]) % self.count)

    def near(self, step):
        return any(self.source(i, step) == i + 1 for i in range(self.count - 1))

    def carries(self, step):
        return self.near(step) or ((step[0], 1) in self.passed and self.near((step[0], 1)))

    def send(self, step, x):
        pairs = [(i, self.target(i, step)) for i in range(self.count)]
        return lax.ppermute(x, self.axis, pairs)

    def all(self, messages):
        got = [self.send(s, x) for s, x in zip(self.direct, messages)]
        return got + [self.send((0, 1), x) for x in got[1 : 1 + len(self.passed)]]


def x_tile(tab, where, field, n, cols, sums):
    even = [field[2 * i, cols, :] for i in range(n // 2)]
    odd = [field[2 * i + 1, cols, :] for i in range(n // 2)]
    left, right = sums if sums else (None, None)
    return one_level(even, odd, tab, where, "", GA, GB, left, right)


def first_kernel(exx, exy, n, ny, stiffness, ct, hx_ref, hy_ref, source, *refs):
    field, pack, sums, tab, own = refs[:5]
    messages = refs[5 : 5 + len(exx.direct)]
    hx, hy, sems, spacing_sems = refs[5 + len(exx.direct) :]
    ex = exx
    index = lax.axis_index(exx.axis)
    tiles = ny // ct

    def fetch(t):
        part = pl.ds(t * (n // 1), n // 1)
        return pltpu.make_async_copy(source.at[part], field.at[part], sems.at[t])

    spacings = [
        pltpu.make_async_copy(a, b, spacing_sems.at[i])
        for i, (a, b) in enumerate(((hx_ref, hx), (hy_ref, hy)))
    ]
    for copy in spacings:
        copy.start()
    for t in range(1):
        fetch(t).start()
    for copy in spacings:
        copy.wait()
    lanes = 2 * pack.shape[1]
    counts = (hx.shape[1], hy.shape[1])

    def row(ref):
        x = ref[...]
        if x.shape[1] < lanes:
            x = jnp.concatenate([x, jnp.ones((1, lanes - x.shape[1]), F32)], axis=1)
        return jnp.broadcast_to(x, (8, lanes))

    is_y = (lax.broadcasted_iota(jnp.int32, (8, lanes), 0) & 2) == 2
    build_pack(
        jnp.where(is_y, row(hy), row(hx)),
        counts,
        (index, lax.axis_index(exy.axis)),
        (n, ny),
        stiffness,
        pack,
        sums,
    )
    build_table(pack, sums, 0, index, n, tab)
    for t in range(1):
        fetch(t).wait()
    where, _ = offsets(n)

    def body(t, carry):
        begin = pl.multiple_of(t * ct, ct)
        cols = pl.ds(begin, ct)
        _, nodes, p1, q1 = x_tile(tab, where, field, n, cols, None)
        _, _, p2, q2 = one_level(nodes[0::2], nodes[1::2], tab, where, "2", GA2, GB2, None, None)
        p2, q2 = summaries(tab, p1, q1, p2, q2)
        own[cols, :] = p1
        own[pl.ds(begin + ny, ct), :] = q1
        for step, message in zip(ex.direct, messages):
            upward = ex.target(index, step) > index
            message[cols, :] = jnp.where(upward, p1, q1)
            message[pl.ds(begin + ny, ct), :] = jnp.where(upward, p2, q2)
            if ex.carries(step):
                message[pl.ds(begin + 2 * ny, ct), :] = field[0, cols, :]
        return carry

    lax.fori_loop(0, tiles, body, 0)


def column(ref, j, count, ny):
    return ref[pl.ds(j, count, stride=ny), :]


def local_kernel(exy, n, ny, ct, field, xtab, pack, sums, passing, *refs):
    ytab, shares, fine, out, local, passed, full, mixed = refs
    n1, n2 = n // 2, n // 4
    where, _ = offsets(n)
    build_table(pack, sums, 1, lax.axis_index(exy.axis), ny, ytab)

    for r, name in enumerate(("v", "u")):
        nodes = [single(xtab, where[name] + i) for i in range(n1)]
        details, nodes, _, _ = one_level(
            nodes[0::2], nodes[1::2], xtab, where, "2", GA2, GB2, None, None
        )
        for i in range(n2):
            shares[r * n2 + i : r * n2 + i + 1, :] = nodes[i]
            shares[(2 + r) * n2 + i : (2 + r) * n2 + i + 1, :] = details[i]

    def body(t, carry):
        begin = pl.multiple_of(t * ct, ct)
        cols = pl.ds(begin, ct)
        details, nodes, _, _ = x_tile(xtab, where, field, n, cols, None)
        for i in range(n1):
            fine[i, cols, :] = details[i]
            full[pl.ds(i * ny + begin, ct), :] = nodes[i]
        details, nodes, _, _ = one_level(
            nodes[0::2], nodes[1::2], xtab, where, "2", GA2, GB2, None, None
        )
        for i in range(n2):
            mixed[pl.ds(i * ny + begin, ct), :] = nodes[i]
            mixed[pl.ds((n2 + i) * ny + begin, ct), :] = details[i]
        return carry

    lax.fori_loop(0, ny // ct, body, 0)

    m1, m2 = ny // 2, ny // 4
    ywhere, _ = offsets(ny)
    for j in range(m1):
        e = column(full, 2 * j + 1, n1, ny)
        e = e - single(ytab, ywhere["wl"] + j) * column(full, 2 * j, n1, ny)
        if j + 1 < m1:
            e = e - single(ytab, ywhere["wr"] + j) * column(full, 2 * j + 2, n1, ny)
        out[pl.ds(2 * j + 1, n1, stride=ny), :] = e
    even = [column(mixed, 2 * j, n1, ny) for j in range(m1)]
    odd = [column(mixed, 2 * j + 1, n1, ny) for j in range(m1)]
    _, nodes, p1, q1 = one_level(even, odd, ytab, ywhere, "", GA, GB, None, None)
    for j in range(m1):
        out[pl.ds(ny + 2 * j, n2, stride=2 * ny), :] = nodes[j][n2:]
    thin = [x[:n2] for x in nodes]
    details, nodes, p2, q2 = one_level(
        thin[0::2], thin[1::2], ytab, ywhere, "2", GA2, GB2, None, None
    )
    for j in range(m2):
        out[pl.ds(4 * j, n2, stride=2 * ny), :] = nodes[j]
        out[pl.ds(4 * j + 2, n2, stride=2 * ny), :] = details[j]
    p2, q2 = summaries(ytab, p1[:n2], q1[:n2], p2, q2)
    local[:n1, :] = p1
    local[n1 : n1 + n2, :] = p2
    local[n1 + n2 : 2 * n1 + n2, :] = q1
    local[2 * n1 + n2 : 3 * n1, :] = q2
    local[3 * n1 : 4 * n1, :] = column(full, 0, n1, ny)
    local[4 * n1 :, :] = column(mixed, 0, n2, ny)


LEFT, RIGHT, LEFT2, RIGHT2, GHOST, HALO, ARRIVED = 0, 1, 2, 3, 4, 5, 8


def arrived_y(ytab, arrived, ny):
    m1 = ny // 2
    where, _ = offsets(ny)
    even = [column(arrived, 2 * j, ARRIVED, ny) for j in range(m1)]
    odd = [column(arrived, 2 * j + 1, ARRIVED, ny) for j in range(m1)]
    details, nodes, p1, q1 = one_level(even, odd, ytab, where, "", GA, GB, None, None)
    details2, nodes2, p2, q2 = one_level(
        nodes[0::2], nodes[1::2], ytab, where, "2", GA2, GB2, None, None
    )
    return details, nodes, details2, nodes2, p1, q1, p2, q2


def second_kernel(exx, exy, n, ny, ct, *refs):
    own, xtab, shares, ytab, local = refs[:5]
    incoming = refs[5 : 5 + len(exx.steps)]
    arrived, yown = refs[5 + len(exx.steps) : 7 + len(exx.steps)]
    messages = refs[7 + len(exx.steps) :]
    index = lax.axis_index(exx.axis)
    n1, n2 = n // 2, n // 4
    where, _ = offsets(n)

    def body(t, carry):
        begin = pl.multiple_of(t * ct, ct)
        cols = pl.ds(begin, ct)
        zero = jnp.zeros((ct, LANES), F32)
        left = right = left2 = right2 = halo = zero
        for step, message in zip(exx.steps, incoming):
            source = exx.source(index, step)
            lower = source < index
            one = message[cols, :]
            two = message[pl.ds(begin + ny, ct), :]
            left = left + jnp.where(lower, one, 0.0)
            right = right + jnp.where(lower, 0.0, one)
            left2 = left2 + jnp.where(lower, two, 0.0)
            right2 = right2 + jnp.where(lower, 0.0, two)
            if exx.near(step):
                halo = jnp.where(source == index + 1, message[pl.ds(begin + 2 * ny, ct), :], halo)
        p1, q1 = own[cols, :], own[pl.ds(begin + ny, ct), :]
        left2, right2 = second_sums(xtab, left, right, left2, right2, p1, q1)
        ghost = single(xtab, HG) * halo + single(xtab, VN) * (left + p1) + single(xtab, UN) * right
        for row, value in (
            (LEFT, left),
            (RIGHT, right),
            (LEFT2, left2),
            (RIGHT2, right2),
            (GHOST, ghost),
            (HALO, halo),
            (HALO + 1, zero),
            (HALO + 2, zero),
        ):
            arrived[pl.ds(row * ny + begin, ct), :] = value
        return carry

    lax.fori_loop(0, ny // ct, body, 0)
    _, _, _, _, p1, q1, p2, q2 = arrived_y(ytab, arrived, ny)
    p2, q2 = summaries(ytab, p1, q1, p2, q2)
    first = column(arrived, 0, ARRIVED, ny)
    nodes_v, nodes_u = shares[:n2, :], shares[n2 : 2 * n2, :]
    details_v, details_u = shares[2 * n2 : 3 * n2, :], shares[3 * n2 :, :]

    def rows(name, count):
        return xtab[where[name] : where[name] + count, :]

    def coarse(x):
        return (
            nodes_v * x[LEFT : LEFT + 1]
            + nodes_u * x[RIGHT : RIGHT + 1]
            + rows("v2", n2) * x[LEFT2 : LEFT2 + 1]
            + rows("u2", n2) * x[RIGHT2 : RIGHT2 + 1]
        )

    is_last = lax.broadcasted_iota(jnp.int32, (n2, LANES), 0) == n2 - 1

    def detail(x):
        ghost = jnp.where(is_last, single(xtab, HW2) * x[GHOST : GHOST + 1], 0.0)
        return details_v * x[LEFT : LEFT + 1] + details_u * x[RIGHT : RIGHT + 1] - ghost

    p1c, p1d = local[:n2, :] + coarse(p1), local[n2:n1, :] + detail(p1)
    p2c = local[n1 : n1 + n2, :] + coarse(p2)
    q1c = local[n1 + n2 : 2 * n1, :] + coarse(q1)
    q1d = local[2 * n1 : 2 * n1 + n2, :] + detail(q1)
    q2c = local[2 * n1 + n2 : 3 * n1, :] + coarse(q2)
    yown[:n2, :] = p1c
    yown[n2:, :] = q1c
    yindex = lax.axis_index(exy.axis)
    for step, message in zip(exy.steps, messages):
        upward = exy.target(yindex, step) > yindex
        message[:n2, :] = jnp.where(upward, p1c, q1c)
        message[n2:n1, :] = jnp.where(upward, p1d, q1d)
        message[n1 : n1 + n2, :] = jnp.where(upward, p2c, q2c)
        if exy.near(step):
            message[n1 + n2 : 2 * n1 + n2, :] = (
                local[3 * n1 : 4 * n1, :]
                + rows("v", n1) * first[LEFT : LEFT + 1]
                + rows("u", n1) * first[RIGHT : RIGHT + 1]
            )
            message[2 * n1 + n2 : 2 * (n1 + n2), :] = local[4 * n1 :, :] + coarse(first)


def share_kernel(n, ny, own_part, fine, arrived, xtab, shares, ytab, result, out, *refs):
    last, one, two, blend, sems = refs
    n1, n2 = n // 2, n // 4
    m1, m2 = ny // 2, ny // 4
    where, _ = offsets(n)
    last[...] = fine[n1 - 1] - single(xtab, HW1) * arrived[HALO * ny : (HALO + 1) * ny, :]
    copies = [
        pltpu.make_async_copy(fine.at[: n1 - 1], result.at[: n1 - 1, 1], sems.at[0]),
        pltpu.make_async_copy(last, result.at[n1 - 1, 1], sems.at[1]),
    ]
    for copy in copies:
        copy.start()
    details, nodes, details2, nodes2, _, _, _, _ = arrived_y(ytab, arrived, ny)
    side = lax.broadcasted_iota(jnp.int32, (ARRIVED, LANES), 0) < LEFT2
    for j in range(m1):
        at = pl.ds(2 * j + 1, ARRIVED, stride=ny)
        one[at, :] = details[j]
        two[at, :] = jnp.where(side, details[j], 0.0)
        one[pl.ds(2 * j, ARRIVED, stride=ny), :] = nodes[j]
    for j in range(m2):
        two[pl.ds(4 * j, ARRIVED, stride=ny), :] = nodes2[j]
        two[pl.ds(4 * j + 2, ARRIVED, stride=ny), :] = details2[j]
    odd = (lax.broadcasted_iota(jnp.int32, (8, LANES), 0) & 1) == 1
    for k in range(n1):
        for r, name in enumerate(("v", "u")):
            block = (2 + r if k % 2 else r) * n2 + k // 2
            mixture = jnp.where(odd, single(xtab, where[name] + k), single(shares, block))
            blend[16 * k + 8 * r : 16 * k + 8 * r + 8, :] = mixture

    def body(t, carry):
        begin = pl.multiple_of(t * 8, 8)
        cols = pl.ds(begin, 8)

        def tile(ref, r):
            return ref[pl.ds(r * ny + begin, 8), :]

        ones = [tile(one, r) for r in (LEFT, RIGHT)]
        twos = [tile(two, r) for r in (LEFT, RIGHT, LEFT2, RIGHT2)]
        ghost = jnp.where(odd, 0.0, single(xtab, HW2) * tile(one, GHOST))
        for k in range(n1):
            x = own_part[k, cols, :]
            source = ones if k % 2 else twos
            for r in range(2):
                x = x + blend[16 * k + 8 * r : 16 * k + 8 * r + 8, :] * source[r]
            if k % 2 == 0:
                x = x + single(xtab, where["v2"] + k // 2) * twos[2]
                x = x + single(xtab, where["u2"] + k // 2) * twos[3]
            elif k == n1 - 1:
                x = x - ghost
            out[k, cols, :] = x
        return carry

    lax.fori_loop(0, ny // 8, body, 0)
    for copy in copies:
        copy.wait()


def rank_kernel(ny, tab, ranks):
    where, _ = offsets(ny)
    m1, m2 = ny // 2, ny // 4
    ranks[...] = jnp.zeros_like(ranks)

    def put(rank, j, value):
        ranks[rank, j : j + 1, :] = value

    for rank, name, end in ((0, "v", VN), (1, "u", UN)):
        nodes = [single(tab, where[name] + i) for i in range(m1)]
        for i in range(m1):
            put(rank, 2 * i, nodes[i])
        details, nodes2, _, _ = one_level(
            nodes[0::2], nodes[1::2], tab, where, "2", GA2, GB2, None, None
        )
        details[-1] = details[-1] - single(tab, HW2) * single(tab, end)
        for i in range(m2):
            put(2 + rank, 4 * i, nodes2[i])
            put(2 + rank, 4 * i + 2, details[i])
            put(4 + rank, 4 * i, single(tab, where[name + "2"] + i))
    put(6, ny - 1, -single(tab, HW1))
    put(7, ny - 2, -single(tab, HW2))


def third_kernel(ex, n, ny, *refs):
    partial, tab, ranks, own = refs[1:5]
    incoming = refs[5 : 5 + len(ex.steps)]
    result, sums, done, sems = refs[5 + len(ex.steps) :]
    n1, n2 = n // 2, n // 4
    index = lax.axis_index(ex.axis)
    zero, zero2 = jnp.zeros((n1, LANES), F32), jnp.zeros((n2, LANES), F32)
    left, right, left2, right2, halo, halo2 = zero, zero, zero2, zero2, zero, zero2
    for step, message in zip(ex.steps, incoming):
        source = ex.source(index, step)
        lower = source < index
        one, two = message[:n1, :], message[n1 : n1 + n2, :]
        left = left + jnp.where(lower, one, 0.0)
        right = right + jnp.where(lower, 0.0, one)
        left2 = left2 + jnp.where(lower, two, 0.0)
        right2 = right2 + jnp.where(lower, 0.0, two)
        if ex.near(step):
            mine = source == index + 1
            halo = jnp.where(mine, message[n1 + n2 : 2 * n1 + n2, :], halo)
            halo2 = jnp.where(mine, message[2 * n1 + n2 : 2 * (n1 + n2), :], halo2)
    p1, q1 = own[:n2, :], own[n2:, :]
    left2, right2 = second_sums(tab, left[:n2], right[:n2], left2, right2, p1, q1)
    ghost = single(tab, HG) * halo2 + single(tab, VN) * p1
    sums[0:n1, :] = left
    sums[n1 : 2 * n1, :] = right
    sums[2 * n1 : 3 * n1, :] = halo
    sums[3 * n1 : 3 * n1 + n2, :] = left2
    sums[3 * n1 + n2 : 3 * n1 + 2 * n2, :] = right2
    sums[3 * n1 + 2 * n2 : 3 * n1 + 3 * n2, :] = ghost

    def row(i):
        return sums[i : i + 1, :]

    group = n1 // 4

    def put(g):
        part = pl.ds(g * group, group)
        return pltpu.make_async_copy(done.at[part], result.at[part, 0], sems.at[g])

    for g in range(4):
        for t in range(ny // 8):
            cols = slice(8 * t, 8 * t + 8)
            tables = [ranks[r, cols, :] for r in range(8)]
            for k in range(g * group, (g + 1) * group):
                x = partial[k, cols, :] + tables[6] * row(2 * n1 + k)
                if k % 2:
                    i = n2 + k // 2
                    x = x + tables[0] * row(i) + tables[1] * row(n1 + i)
                else:
                    i = k // 2
                    x = x + tables[2] * row(i) + tables[3] * row(n1 + i)
                    x = x + tables[4] * row(3 * n1 + i) + tables[5] * row(3 * n1 + n2 + i)
                    x = x + tables[7] * row(3 * n1 + 2 * n2 + i)
                done[k, cols, :] = x
        put(g).start(priority=g % 2)
    for g in range(4):
        put(g).wait()


def y_rows(ex, n, step):
    return 3 * n // 4 * (2 if any(map(ex.near, ex.direct)) else 1) + 8 * (ex.count - 1 - step[0])


def x_rows(ex, ny, step):
    return (3 if ex.carries(step) else 2) * ny


def shape(*dims):
    return jax.ShapeDtypeStruct(dims, F32)


def on_device(exx, exy, field, spacing_x, spacing_y):
    n, ny, _ = field.shape
    n1, n2 = n // 2, n // 4
    ct = min(ny, 64)
    xrows = offsets(n)[1]
    yrows = offsets(ny)[1]
    params = pltpu.CompilerParams(vmem_limit_bytes=40 * 1024 * 1024)
    anywhere = pl.BlockSpec(memory_space=pl.ANY)
    inside = pl.BlockSpec(memory_space=pltpu.VMEM)
    dma = pltpu.SemaphoreType.DMA
    operands = (spacing_x[None], spacing_y[None], field)
    lanes = max(spacing_x.shape[0], spacing_y.shape[0])
    lanes = (lanes + 2 * LANES - 1) // (2 * LANES) * LANES
    stiffness = (float(SMOOTH_X) ** 2, float(SMOOTH_Y) ** 2)
    field, pack, sums, xtab, xown, *outgoing = pl.pallas_call(
        functools.partial(first_kernel, exx, exy, n, ny, stiffness, ct),
        out_shape=[shape(n, ny, LANES), shape(24, lanes), shape(64, LANES)]
        + [shape(xrows, LANES), shape(2 * ny, LANES)]
        + [shape(x_rows(exx, ny, s), LANES) for s in exx.direct],
        in_specs=[anywhere] * 3,
        scratch_shapes=[
            pltpu.VMEM((1, spacing_x.shape[0]), F32),
            pltpu.VMEM((1, spacing_y.shape[0]), F32),
            dma((1,)),
            dma((2,)),
        ],
        compiler_params=params,
        name="x_summary",
    )(*[pltpu.with_memory_space_constraint(a, pltpu.HBM) for a in operands])
    block = shape(n1, ny, LANES)
    lines = pltpu.VMEM((n1 * ny, LANES), F32)
    ytab, shares, fine, local_out, local, outgoing[0] = pl.pallas_call(
        functools.partial(local_kernel, exy, n, ny, ct),
        out_shape=[shape(yrows, LANES), shape(4 * n2, LANES), block, shape(n1 * ny, LANES)]
        + [shape(4 * n1 + n2, LANES), shape(*outgoing[0].shape)],
        in_specs=[inside] * 4 + [anywhere],
        out_specs=[inside] * 5 + [anywhere],
        input_output_aliases={4: 5},
        scratch_shapes=[lines, lines],
        compiler_params=params,
        name="local_transform",
    )(field, xtab, pack, sums, outgoing[0])
    incoming = exx.all(outgoing)
    arrived, own, *outgoing = pl.pallas_call(
        functools.partial(second_kernel, exx, exy, n, ny, ct),
        out_shape=[shape(ARRIVED * ny, LANES), shape(2 * n2, LANES)]
        + [shape(y_rows(exy, n, s), LANES) for s in exy.steps],
        compiler_params=params,
        name="x_arrived",
    )(xown, xtab, shares, ytab, local, *incoming)
    some = pltpu.VMEM((ARRIVED * ny, LANES), F32)
    result, partial = pl.pallas_call(
        functools.partial(share_kernel, n, ny),
        out_shape=[shape(n1, 2, ny, LANES), block],
        out_specs=[anywhere, inside],
        scratch_shapes=[
            pltpu.VMEM((ny, LANES), F32),
            some,
            some,
            pltpu.VMEM((16 * n1, LANES), F32),
            dma((2,)),
        ],
        compiler_params=params,
        name="x_share",
    )(local_out.reshape(n1, ny, LANES), fine, arrived, xtab, shares, ytab)
    ranks = pl.pallas_call(
        functools.partial(rank_kernel, ny),
        out_shape=shape(8, ny, LANES),
        compiler_params=params,
        name="y_ranks",
    )(ytab)
    incoming = exy.all(outgoing)
    result = pl.pallas_call(
        functools.partial(third_kernel, exy, n, ny),
        out_shape=shape(n1, 2, ny, LANES),
        in_specs=[anywhere] + [inside] * (4 + len(incoming)),
        out_specs=anywhere,
        input_output_aliases={0: 0},
        scratch_shapes=[
            pltpu.VMEM((3 * n1 + 3 * n2, LANES), F32),
            pltpu.VMEM((n1, ny, LANES), F32),
            dma((4,)),
        ],
        compiler_params=params,
        name="y_update",
    )(result, partial, ytab, ranks, own, *incoming)
    return result.reshape(n, ny, LANES)


def solution(mesh):
    exx = Exchange("gx", mesh.shape["gx"], True)
    exy = Exchange("gy", mesh.shape["gy"], False)
    placed = (P("gx", "gy", None), P(), P())
    return jax.shard_map(
        functools.partial(on_device, exx, exy),
        mesh=mesh,
        in_specs=placed,
        out_specs=P("gx", "gy", None),
        check_vma=False,
    )
```

```python
import functools

import jax
import jax.numpy as jnp
from jax import lax
from jax.experimental import pallas as pl
from jax.experimental.pallas import tpu as pltpu
from jax.sharding import PartitionSpec as P

SMOOTH_X = 48
SMOOTH_Y = 96
F32 = jnp.float32
LANES = 128

GA, GB, GA2, GB2, HW1, HW2, CA0, CA1, KAP, LAM, CB0, CB1, VN, UN, HG = range(15)
SINGLES = 16


def offsets(n):
    n1, n2 = n // 2, n // 4
    names = ["wl", "wr", "al", "be", "u", "v"]
    where, row = {}, SINGLES
    for name in names:
        where[name] = row
        row += n1
    for name in names:
        where[name + "2"] = row
        row += n2
    return where, row


def combine(left, right):
    a, b, c, d = left
    p, q, r, s = right
    return (a * p + b * r, a * q + b * s, c * p + d * r, c * q + d * s)


def gather(x, position):
    out = []
    for t in range(position.shape[1] // LANES):
        place = position[:, t * LANES : (t + 1) * LANES]
        inner, block = place & (LANES - 1), place // LANES
        picked = None
        for b in range(x.shape[1] // LANES):
            part = jnp.take_along_axis(
                x[:, b * LANES : (b + 1) * LANES], inner, axis=1, mode="promise_in_bounds"
            )
            picked = part if picked is None else jnp.where(block == b, part, picked)
        out.append(picked)
    return out[0] if len(out) == 1 else jnp.concatenate(out, axis=1)


def down(x, by):
    return pltpu.roll(x, by, 0)


def build_pack(h, counts, places, locals_, stiffness, pack, sums):
    m = h.shape[1] // 2
    lanes = lax.broadcasted_iota(jnp.int32, (8, m), 1)
    rows = lax.broadcasted_iota(jnp.int32, (8, m), 0)
    lower = rows >= 4
    is_y = (rows & 2) == 2
    second = (rows & 1) == 1

    def by_axis(pair):
        return jnp.where(is_y, pair[1], pair[0])

    count = jnp.where(second, by_axis(counts) // 4, by_axis(counts) // 2)
    real = lanes < count
    last = lanes == count - 1
    k = jnp.where(lower, count - 1 - lanes, lanes)
    k = jnp.where(real, k, 0)
    first = jnp.where(second, 4 * k, 2 * k)
    even = gather(h, first) + jnp.where(second, gather(h, first + 1), 0.0)
    odd = gather(h, jnp.where(second, first + 2, first + 1))
    odd = odd + jnp.where(second, gather(h, jnp.where(second, first + 3, first)), 0.0)
    width = even + odd
    inverse = 1.0 / width
    s = by_axis(stiffness)
    stiff = s * inverse
    across = 1.0 / (stiff - width * (1.0 / 6.0))
    same = jnp.where(real, (width * (1.0 / 3.0) + stiff) * across, 1.0)
    into = jnp.where(real, across, 0.0)
    back = jnp.where(real, (s + width * width * (1.0 / 12.0)) * across, 0.0)
    product = (same, into, back, same)
    identity = (1.0, 0.0, 0.0, 1.0)

    def moved(matrix, by):
        head = lanes < by
        return [jnp.where(head, f, pltpu.roll(x, by, 1)) for x, f in zip(matrix, identity)]

    step = 1
    while step < m:
        if 2 * step < m:
            near = combine(product, moved(product, step))
            far = combine(moved(product, 2 * step), moved(product, 3 * step))
            product = combine(near, far)
            step *= 4
        else:
            product = combine(product, moved(product, step))
            step *= 2
    w = jnp.where(lower, product[1], product[0])
    total = jnp.where(lower, product[3], product[0])[:, m - 1 : m]
    here = jnp.where(lower, count - 1 - lanes, lanes - 1)
    there = jnp.where(lower, count - 2 - lanes, lanes)
    uv = gather(w, jnp.maximum(here, 0))
    uv = jnp.where(lower, jnp.where(real, uv, 0.0), jnp.where(lanes == 0, 1.0, uv))
    uv_next = gather(w, jnp.maximum(there, 0))
    uv_next = jnp.where(lower & (lanes >= count - 1), 0.0, uv_next)
    even = jnp.where(lower, down(even, 4), even)
    odd = jnp.where(lower, down(odd, 4), odd)
    inverse = jnp.where(lower, down(inverse, 4), inverse)
    ab = jnp.where(real, (uv * even + uv_next * odd) * (0.5 / total), 0.0)
    weight = jnp.where(lower, even, odd) * inverse
    weight = jnp.where(last, jnp.where(lower, 0.0, 1.0), weight)
    weight = jnp.where(real, weight, 0.0)
    pack[0:8, :] = uv
    pack[8:16, :] = ab
    pack[16:24, :] = weight
    other = down(weight, 4)
    wl = jnp.where(lower, other, weight)
    wr = jnp.where(lower, weight, other)
    fine = down(uv, 1)
    twice = jnp.where(real & second, 2 * lanes, 0)
    halo = -wr * gather(fine, jnp.minimum(twice + 2, m - 1))
    detail = gather(fine, twice + 1) - wl * gather(fine, twice) + halo
    valid = real & second
    halo = jnp.where(valid, halo, 0.0)
    detail = jnp.where(valid, detail, 0.0)
    place = by_axis(places)
    local = jnp.where(second, by_axis(locals_) // 4, by_axis(locals_) // 2)
    begin, end = place * local, (place + 1) * local

    def lane_sum(row, x):
        value = jnp.sum(x, axis=1, keepdims=True)
        sums[8 * row : 8 * row + 8, :] = jnp.broadcast_to(value, (8, LANES))
        return value

    def below(edge, x, y):
        return jnp.where(lanes < edge, x, 0.0) - jnp.where(lanes == edge - 1, y, 0.0)

    def above(edge, x, y):
        return jnp.where(lanes >= edge, x, 0.0) + jnp.where(lanes == edge - 1, y, 0.0)

    cross, cross_halo = ab * down(detail, 4), ab * down(halo, 4)
    alike, alike_halo = ab * detail, ab * halo
    lane_sum(0, below(begin, cross, cross_halo))
    lane_sum(1, below(end, cross, cross_halo))
    lane_sum(
        2, jnp.where(lower, above(end, alike, alike_halo), below(begin, alike, alike_halo))
    )
    edge = -ab * wr
    lane_sum(3, jnp.where(lanes == begin - 1, edge, 0.0))
    edge_last = lane_sum(4, jnp.where(lanes == end - 1, edge, 0.0))
    lane_sum(5, jnp.where(lanes == end - 1, wr, 0.0))
    ghost = lane_sum(6, jnp.where(lanes == end, uv, 0.0))
    ghost, edge_last = jnp.broadcast_to(ghost, (8, LANES)), jnp.broadcast_to(edge_last, (8, LANES))
    part = down(ghost, 4) * edge_last
    sums[56:64, :] = 1.0 + part - down(part, 4)


def build_table(pack, sums, axis, index, n, tab):
    m = pack.shape[1]
    n1, n2 = n // 2, n // 4
    a = 2 * axis
    for row, (block, r) in {
        GA: (3, a),
        GB: (3, a + 4),
        GA2: (3, a + 1),
        GB2: (3, a + 5),
        HW1: (5, a),
        HW2: (5, a + 1),
        CA0: (0, a + 1),
        CA1: (1, a + 1),
        KAP: (2, a + 1),
        LAM: (2, a + 5),
        CB0: (0, a + 5),
        CB1: (1, a + 5),
        VN: (6, a + 4),
        UN: (6, a),
        HG: (7, a),
    }.items():
        source = 8 * block + r
        tab[row : row + 1, :] = sums[source : source + 1, :]
    where, _ = offsets(n)
    for lv, rows, suffix_name in ((0, n1, ""), (1, n2, "2")):
        col = lax.broadcasted_iota(jnp.int32, (rows, m), 1)
        sub = lax.broadcasted_iota(jnp.int32, (rows, m), 0)
        mine = col == index * rows + sub
        mine_inner = mine & (sub < rows - 1)
        for name, block, below, mask in (
            ("wl", 2, 0, mine),
            ("wr", 2, 4, mine_inner),
            ("al", 1, 0, mine),
            ("be", 1, 4, mine),
            ("u", 0, 0, mine),
            ("v", 0, 4, mine),
        ):
            r = 8 * block + below + a + lv
            values = jnp.sum(jnp.where(mask, pack[r : r + 1, :], 0.0), axis=1, keepdims=True)
            start = where[name + suffix_name]
            tab[start : start + rows, :] = jnp.broadcast_to(values, (rows, LANES))


def one_level(even, odd, tab, where, suffix, ga, gb, from_left, from_right):
    def c(name, i):
        row = where[name + suffix] + i
        return tab[row : row + 1, :]

    count = len(even)
    details = []
    for i in range(count):
        e = odd[i] - c("wl", i) * even[i]
        if i + 1 < count:
            e = e - c("wr", i) * even[i + 1]
        details.append(e)
    first = tab[ga : ga + 1, :] * even[0]
    acc = first if from_left is None else from_left + first
    lefts = []
    for i in range(count):
        lefts.append(acc)
        acc = acc + c("al", i) * details[i]
    left_end = acc
    acc = from_right
    rights = [None] * count
    for i in reversed(range(count)):
        term = c("be", i) * details[i]
        acc = term if acc is None else acc + term
        rights[i] = acc
    nodes = [even[i] + c("v", i) * lefts[i] + c("u", i) * rights[i] for i in range(count)]
    right_end = rights[0] + tab[gb : gb + 1, :] * even[0]
    return details, nodes, left_end, right_end


def single(tab, row):
    return tab[row : row + 1, :]


def summaries(tab, p1, q1, p2, q2):
    to_right = p2 + single(tab, KAP) * q1 - single(tab, CA1) * p1
    to_left = q2 + single(tab, LAM) * p1 + single(tab, CB0) * q1
    return to_right, to_left


def second_sums(tab, left, right, left2, right2, p1, q1):
    left_second = left2 + single(tab, CA0) * left + single(tab, KAP) * (q1 + right)
    right_second = right2 - single(tab, CB1) * right + single(tab, LAM) * (left + p1)
    return left_second, right_second


class Exchange:
    def __init__(self, axis, count, paired):
        self.axis, self.count = axis, count
        self.folded = not paired and count & (count - 1) == 0
        if paired and count % 2 == 0:
            shifts = range(2, count, 2)
            self.direct = [(0, 1)] + [(s, 0) for s in shifts]
            self.passed = [(s, 1) for s in shifts]
        else:
            self.direct = [(s, 0) for s in range(1, count)]
            self.passed = []
        self.steps = self.direct + self.passed

    def position(self, i):
        if not self.folded:
            return i
        shift = 1
        while shift < self.count:
            i = i ^ (i >> shift)
            shift *= 2
        return i

    def device(self, position):
        return position ^ (position >> 1) if self.folded else position

    def target(self, i, step):
        return self.device((self.position(i) + step[0]) % self.count) ^ step[1]

    def source(self, i, step):
        return self.device((self.position(i ^ step[1]) + self.count - step[0]) % self.count)

    def near(self, step):
        return any(self.source(i, step) == i + 1 for i in range(self.count - 1))

    def carries(self, step):
        return self.near(step) or ((step[0], 1) in self.passed and self.near((step[0], 1)))

    def send(self, step, x):
        pairs = [(i, self.target(i, step)) for i in range(self.count)]
        return lax.ppermute(x, self.axis, pairs)

    def all(self, messages):
        got = [self.send(s, x) for s, x in zip(self.direct, messages)]
        return got + [self.send((0, 1), x) for x in got[1 : 1 + len(self.passed)]]


def x_tile(tab, where, field, n, cols, sums):
    even = [field[2 * i, cols, :] for i in range(n // 2)]
    odd = [field[2 * i + 1, cols, :] for i in range(n // 2)]
    left, right = sums if sums else (None, None)
    return one_level(even, odd, tab, where, "", GA, GB, left, right)


def first_kernel(exx, exy, n, ny, stiffness, ct, hx_ref, hy_ref, source, *refs):
    field, pack, sums, tab, own = refs[:5]
    messages = refs[5 : 5 + len(exx.direct)]
    hx, hy, sems, spacing_sems = refs[5 + len(exx.direct) :]
    ex = exx
    index = lax.axis_index(exx.axis)
    tiles = ny // ct

    def fetch(t):
        part = pl.ds(t * (n // 1), n // 1)
        return pltpu.make_async_copy(source.at[part], field.at[part], sems.at[t])

    spacings = [
        pltpu.make_async_copy(a, b, spacing_sems.at[i])
        for i, (a, b) in enumerate(((hx_ref, hx), (hy_ref, hy)))
    ]
    for copy in spacings:
        copy.start(priority=1)
    for t in range(1):
        fetch(t).start()
    for copy in spacings:
        copy.wait()
    lanes = 2 * pack.shape[1]
    counts = (hx.shape[1], hy.shape[1])

    def row(ref):
        x = ref[...]
        if x.shape[1] < lanes:
            x = jnp.concatenate([x, jnp.ones((1, lanes - x.shape[1]), F32)], axis=1)
        return jnp.broadcast_to(x, (8, lanes))

    is_y = (lax.broadcasted_iota(jnp.int32, (8, lanes), 0) & 2) == 2
    build_pack(
        jnp.where(is_y, row(hy), row(hx)),
        counts,
        (index, lax.axis_index(exy.axis)),
        (n, ny),
        stiffness,
        pack,
        sums,
    )
    build_table(pack, sums, 0, index, n, tab)
    for t in range(1):
        fetch(t).wait()
    where, _ = offsets(n)

    def body(t, carry):
        begin = pl.multiple_of(t * ct, ct)
        cols = pl.ds(begin, ct)
        _, nodes, p1, q1 = x_tile(tab, where, field, n, cols, None)
        _, _, p2, q2 = one_level(nodes[0::2], nodes[1::2], tab, where, "2", GA2, GB2, None, None)
        p2, q2 = summaries(tab, p1, q1, p2, q2)
        own[cols, :] = p1
        own[pl.ds(begin + ny, ct), :] = q1
        for step, message in zip(ex.direct, messages):
            upward = ex.target(index, step) > index
            message[cols, :] = jnp.where(upward, p1, q1)
            message[pl.ds(begin + ny, ct), :] = jnp.where(upward, p2, q2)
            if ex.carries(step):
                message[pl.ds(begin + 2 * ny, ct), :] = field[0, cols, :]
        return carry

    lax.fori_loop(0, tiles, body, 0)


def column(ref, j, count, ny):
    return ref[pl.ds(j, count, stride=ny), :]


def local_kernel(exy, n, ny, ct, field, xtab, pack, sums, passing, *refs):
    ytab, shares, fine, out, local, passed, full, mixed = refs
    n1, n2 = n // 2, n // 4
    where, _ = offsets(n)
    build_table(pack, sums, 1, lax.axis_index(exy.axis), ny, ytab)

    for r, name in enumerate(("v", "u")):
        nodes = [single(xtab, where[name] + i) for i in range(n1)]
        details, nodes, _, _ = one_level(
            nodes[0::2], nodes[1::2], xtab, where, "2", GA2, GB2, None, None
        )
        for i in range(n2):
            shares[r * n2 + i : r * n2 + i + 1, :] = nodes[i]
            shares[(2 + r) * n2 + i : (2 + r) * n2 + i + 1, :] = details[i]

    def body(t, carry):
        begin = pl.multiple_of(t * ct, ct)
        cols = pl.ds(begin, ct)
        details, nodes, _, _ = x_tile(xtab, where, field, n, cols, None)
        for i in range(n1):
            fine[i, cols, :] = details[i]
            full[pl.ds(i * ny + begin, ct), :] = nodes[i]
        details, nodes, _, _ = one_level(
            nodes[0::2], nodes[1::2], xtab, where, "2", GA2, GB2, None, None
        )
        for i in range(n2):
            mixed[pl.ds(i * ny + begin, ct), :] = nodes[i]
            mixed[pl.ds((n2 + i) * ny + begin, ct), :] = details[i]
        return carry

    lax.fori_loop(0, ny // ct, body, 0)

    m1, m2 = ny // 2, ny // 4
    ywhere, _ = offsets(ny)
    for j in range(m1):
        e = column(full, 2 * j + 1, n1, ny)
        e = e - single(ytab, ywhere["wl"] + j) * column(full, 2 * j, n1, ny)
        if j + 1 < m1:
            e = e - single(ytab, ywhere["wr"] + j) * column(full, 2 * j + 2, n1, ny)
        out[pl.ds(2 * j + 1, n1, stride=ny), :] = e
    even = [column(mixed, 2 * j, n1, ny) for j in range(m1)]
    odd = [column(mixed, 2 * j + 1, n1, ny) for j in range(m1)]
    _, nodes, p1, q1 = one_level(even, odd, ytab, ywhere, "", GA, GB, None, None)
    for j in range(m1):
        out[pl.ds(ny + 2 * j, n2, stride=2 * ny), :] = nodes[j][n2:]
    thin = [x[:n2] for x in nodes]
    details, nodes, p2, q2 = one_level(
        thin[0::2], thin[1::2], ytab, ywhere, "2", GA2, GB2, None, None
    )
    for j in range(m2):
        out[pl.ds(4 * j, n2, stride=2 * ny), :] = nodes[j]
        out[pl.ds(4 * j + 2, n2, stride=2 * ny), :] = details[j]
    p2, q2 = summaries(ytab, p1[:n2], q1[:n2], p2, q2)
    local[:n1, :] = p1
    local[n1 : n1 + n2, :] = p2
    local[n1 + n2 : 2 * n1 + n2, :] = q1
    local[2 * n1 + n2 : 3 * n1, :] = q2
    local[3 * n1 : 4 * n1, :] = column(full, 0, n1, ny)
    local[4 * n1 :, :] = column(mixed, 0, n2, ny)


LEFT, RIGHT, LEFT2, RIGHT2, GHOST, HALO, ARRIVED = 0, 1, 2, 3, 4, 5, 8


def arrived_y(ytab, arrived, ny):
    m1 = ny // 2
    where, _ = offsets(ny)
    even = [column(arrived, 2 * j, ARRIVED, ny) for j in range(m1)]
    odd = [column(arrived, 2 * j + 1, ARRIVED, ny) for j in range(m1)]
    details, nodes, p1, q1 = one_level(even, odd, ytab, where, "", GA, GB, None, None)
    details2, nodes2, p2, q2 = one_level(
        nodes[0::2], nodes[1::2], ytab, where, "2", GA2, GB2, None, None
    )
    return details, nodes, details2, nodes2, p1, q1, p2, q2


def second_kernel(exx, exy, n, ny, ct, *refs):
    own, xtab, shares, ytab, local = refs[:5]
    incoming = refs[5 : 5 + len(exx.steps)]
    arrived, yown = refs[5 + len(exx.steps) : 7 + len(exx.steps)]
    messages = refs[7 + len(exx.steps) :]
    index = lax.axis_index(exx.axis)
    n1, n2 = n // 2, n // 4
    where, _ = offsets(n)

    def body(t, carry):
        begin = pl.multiple_of(t * ct, ct)
        cols = pl.ds(begin, ct)
        zero = jnp.zeros((ct, LANES), F32)
        left = right = left2 = right2 = halo = zero
        for step, message in zip(exx.steps, incoming):
            source = exx.source(index, step)
            lower = source < index
            one = message[cols, :]
            two = message[pl.ds(begin + ny, ct), :]
            left = left + jnp.where(lower, one, 0.0)
            right = right + jnp.where(lower, 0.0, one)
            left2 = left2 + jnp.where(lower, two, 0.0)
            right2 = right2 + jnp.where(lower, 0.0, two)
            if exx.near(step):
                halo = jnp.where(source == index + 1, message[pl.ds(begin + 2 * ny, ct), :], halo)
        p1, q1 = own[cols, :], own[pl.ds(begin + ny, ct), :]
        left2, right2 = second_sums(xtab, left, right, left2, right2, p1, q1)
        ghost = single(xtab, HG) * halo + single(xtab, VN) * (left + p1) + single(xtab, UN) * right
        for row, value in (
            (LEFT, left),
            (RIGHT, right),
            (LEFT2, left2),
            (RIGHT2, right2),
            (GHOST, ghost),
            (HALO, halo),
            (HALO + 1, zero),
            (HALO + 2, zero),
        ):
            arrived[pl.ds(row * ny + begin, ct), :] = value
        return carry

    lax.fori_loop(0, ny // ct, body, 0)
    _, _, _, _, p1, q1, p2, q2 = arrived_y(ytab, arrived, ny)
    p2, q2 = summaries(ytab, p1, q1, p2, q2)
    first = column(arrived, 0, ARRIVED, ny)
    nodes_v, nodes_u = shares[:n2, :], shares[n2 : 2 * n2, :]
    details_v, details_u = shares[2 * n2 : 3 * n2, :], shares[3 * n2 :, :]

    def rows(name, count):
        return xtab[where[name] : where[name] + count, :]

    def coarse(x):
        return (
            nodes_v * x[LEFT : LEFT + 1]
            + nodes_u * x[RIGHT : RIGHT + 1]
            + rows("v2", n2) * x[LEFT2 : LEFT2 + 1]
            + rows("u2", n2) * x[RIGHT2 : RIGHT2 + 1]
        )

    is_last = lax.broadcasted_iota(jnp.int32, (n2, LANES), 0) == n2 - 1

    def detail(x):
        ghost = jnp.where(is_last, single(xtab, HW2) * x[GHOST : GHOST + 1], 0.0)
        return details_v * x[LEFT : LEFT + 1] + details_u * x[RIGHT : RIGHT + 1] - ghost

    p1c, p1d = local[:n2, :] + coarse(p1), local[n2:n1, :] + detail(p1)
    p2c = local[n1 : n1 + n2, :] + coarse(p2)
    q1c = local[n1 + n2 : 2 * n1, :] + coarse(q1)
    q1d = local[2 * n1 : 2 * n1 + n2, :] + detail(q1)
    q2c = local[2 * n1 + n2 : 3 * n1, :] + coarse(q2)
    yown[:n2, :] = p1c
    yown[n2:, :] = q1c
    yindex = lax.axis_index(exy.axis)
    for step, message in zip(exy.steps, messages):
        upward = exy.target(yindex, step) > yindex
        message[:n2, :] = jnp.where(upward, p1c, q1c)
        message[n2:n1, :] = jnp.where(upward, p1d, q1d)
        message[n1 : n1 + n2, :] = jnp.where(upward, p2c, q2c)
        if exy.near(step):
            message[n1 + n2 : 2 * n1 + n2, :] = (
                local[3 * n1 : 4 * n1, :]
                + rows("v", n1) * first[LEFT : LEFT + 1]
                + rows("u", n1) * first[RIGHT : RIGHT + 1]
            )
            message[2 * n1 + n2 : 2 * (n1 + n2), :] = local[4 * n1 :, :] + coarse(first)


def share_kernel(n, ny, own_part, fine, arrived, xtab, shares, ytab, result, out, *refs):
    last, one, two, blend, sems = refs
    n1, n2 = n // 2, n // 4
    m1, m2 = ny // 2, ny // 4
    where, _ = offsets(n)
    last[...] = fine[n1 - 1] - single(xtab, HW1) * arrived[HALO * ny : (HALO + 1) * ny, :]
    copies = [
        pltpu.make_async_copy(fine.at[: n1 - 1], result.at[: n1 - 1, 1], sems.at[0]),
        pltpu.make_async_copy(last, result.at[n1 - 1, 1], sems.at[1]),
    ]
    for copy in copies:
        copy.start()
    details, nodes, details2, nodes2, _, _, _, _ = arrived_y(ytab, arrived, ny)
    side = lax.broadcasted_iota(jnp.int32, (ARRIVED, LANES), 0) < LEFT2
    for j in range(m1):
        at = pl.ds(2 * j + 1, ARRIVED, stride=ny)
        one[at, :] = details[j]
        two[at, :] = jnp.where(side, details[j], 0.0)
        one[pl.ds(2 * j, ARRIVED, stride=ny), :] = nodes[j]
    for j in range(m2):
        two[pl.ds(4 * j, ARRIVED, stride=ny), :] = nodes2[j]
        two[pl.ds(4 * j + 2, ARRIVED, stride=ny), :] = details2[j]
    odd = (lax.broadcasted_iota(jnp.int32, (8, LANES), 0) & 1) == 1
    for k in range(n1):
        for r, name in enumerate(("v", "u")):
            block = (2 + r if k % 2 else r) * n2 + k // 2
            mixture = jnp.where(odd, single(xtab, where[name] + k), single(shares, block))
            blend[16 * k + 8 * r : 16 * k + 8 * r + 8, :] = mixture

    def body(t, carry):
        begin = pl.multiple_of(t * 8, 8)
        cols = pl.ds(begin, 8)

        def tile(ref, r):
            return ref[pl.ds(r * ny + begin, 8), :]

        ones = [tile(one, r) for r in (LEFT, RIGHT)]
        twos = [tile(two, r) for r in (LEFT, RIGHT, LEFT2, RIGHT2)]
        ghost = jnp.where(odd, 0.0, single(xtab, HW2) * tile(one, GHOST))
        for k in range(n1):
            x = own_part[k, cols, :]
            source = ones if k % 2 else twos
            for r in range(2):
                x = x + blend[16 * k + 8 * r : 16 * k + 8 * r + 8, :] * source[r]
            if k % 2 == 0:
                x = x + single(xtab, where["v2"] + k // 2) * twos[2]
                x = x + single(xtab, where["u2"] + k // 2) * twos[3]
            elif k == n1 - 1:
                x = x - ghost
            out[k, cols, :] = x
        return carry

    lax.fori_loop(0, ny // 8, body, 0)
    for copy in copies:
        copy.wait()


def rank_kernel(ny, tab, ranks):
    where, _ = offsets(ny)
    m1, m2 = ny // 2, ny // 4
    ranks[...] = jnp.zeros_like(ranks)

    def put(rank, j, value):
        ranks[rank, j : j + 1, :] = value

    for rank, name, end in ((0, "v", VN), (1, "u", UN)):
        nodes = [single(tab, where[name] + i) for i in range(m1)]
        for i in range(m1):
            put(rank, 2 * i, nodes[i])
        details, nodes2, _, _ = one_level(
            nodes[0::2], nodes[1::2], tab, where, "2", GA2, GB2, None, None
        )
        details[-1] = details[-1] - single(tab, HW2) * single(tab, end)
        for i in range(m2):
            put(2 + rank, 4 * i, nodes2[i])
            put(2 + rank, 4 * i + 2, details[i])
            put(4 + rank, 4 * i, single(tab, where[name + "2"] + i))
    put(6, ny - 1, -single(tab, HW1))
    put(7, ny - 2, -single(tab, HW2))


def third_kernel(ex, n, ny, *refs):
    partial, tab, ranks, own = refs[1:5]
    incoming = refs[5 : 5 + len(ex.steps)]
    result, sums, done, sems = refs[5 + len(ex.steps) :]
    n1, n2 = n // 2, n // 4
    index = lax.axis_index(ex.axis)
    zero, zero2 = jnp.zeros((n1, LANES), F32), jnp.zeros((n2, LANES), F32)
    left, right, left2, right2, halo, halo2 = zero, zero, zero2, zero2, zero, zero2
    for step, message in zip(ex.steps, incoming):
        source = ex.source(index, step)
        lower = source < index
        one, two = message[:n1, :], message[n1 : n1 + n2, :]
        left = left + jnp.where(lower, one, 0.0)
        right = right + jnp.where(lower, 0.0, one)
        left2 = left2 + jnp.where(lower, two, 0.0)
        right2 = right2 + jnp.where(lower, 0.0, two)
        if ex.near(step):
            mine = source == index + 1
            halo = jnp.where(mine, message[n1 + n2 : 2 * n1 + n2, :], halo)
            halo2 = jnp.where(mine, message[2 * n1 + n2 : 2 * (n1 + n2), :], halo2)
    p1, q1 = own[:n2, :], own[n2:, :]
    left2, right2 = second_sums(tab, left[:n2], right[:n2], left2, right2, p1, q1)
    ghost = single(tab, HG) * halo2 + single(tab, VN) * p1
    sums[0:n1, :] = left
    sums[n1 : 2 * n1, :] = right
    sums[2 * n1 : 3 * n1, :] = halo
    sums[3 * n1 : 3 * n1 + n2, :] = left2
    sums[3 * n1 + n2 : 3 * n1 + 2 * n2, :] = right2
    sums[3 * n1 + 2 * n2 : 3 * n1 + 3 * n2, :] = ghost

    def row(i):
        return sums[i : i + 1, :]

    group = n1 // 4

    def put(g):
        part = pl.ds(g * group, group)
        return pltpu.make_async_copy(done.at[part], result.at[part, 0], sems.at[g])

    for g in range(4):
        for t in range(ny // 8):
            cols = slice(8 * t, 8 * t + 8)
            tables = [ranks[r, cols, :] for r in range(8)]
            for k in range(g * group, (g + 1) * group):
                x = partial[k, cols, :] + tables[6] * row(2 * n1 + k)
                if k % 2:
                    i = n2 + k // 2
                    x = x + tables[0] * row(i) + tables[1] * row(n1 + i)
                else:
                    i = k // 2
                    x = x + tables[2] * row(i) + tables[3] * row(n1 + i)
                    x = x + tables[4] * row(3 * n1 + i) + tables[5] * row(3 * n1 + n2 + i)
                    x = x + tables[7] * row(3 * n1 + 2 * n2 + i)
                done[k, cols, :] = x
        put(g).start(priority=g % 2)
    for g in range(4):
        put(g).wait()


def y_rows(ex, n, step):
    return 3 * n // 4 * (2 if any(map(ex.near, ex.direct)) else 1) + 8 * (ex.count - 1 - step[0])


def x_rows(ex, ny, step):
    return (3 if ex.carries(step) else 2) * ny


def shape(*dims):
    return jax.ShapeDtypeStruct(dims, F32)


def on_device(exx, exy, field, spacing_x, spacing_y):
    n, ny, _ = field.shape
    n1, n2 = n // 2, n // 4
    ct = min(ny, 64)
    xrows = offsets(n)[1]
    yrows = offsets(ny)[1]
    params = pltpu.CompilerParams(vmem_limit_bytes=40 * 1024 * 1024)
    anywhere = pl.BlockSpec(memory_space=pl.ANY)
    inside = pl.BlockSpec(memory_space=pltpu.VMEM)
    dma = pltpu.SemaphoreType.DMA
    operands = (spacing_x[None], spacing_y[None], field)
    lanes = max(spacing_x.shape[0], spacing_y.shape[0])
    lanes = (lanes + 2 * LANES - 1) // (2 * LANES) * LANES
    stiffness = (float(SMOOTH_X) ** 2, float(SMOOTH_Y) ** 2)
    field, pack, sums, xtab, xown, *outgoing = pl.pallas_call(
        functools.partial(first_kernel, exx, exy, n, ny, stiffness, ct),
        out_shape=[shape(n, ny, LANES), shape(24, lanes), shape(64, LANES)]
        + [shape(xrows, LANES), shape(2 * ny, LANES)]
        + [shape(x_rows(exx, ny, s), LANES) for s in exx.direct],
        in_specs=[anywhere] * 3,
        scratch_shapes=[
            pltpu.VMEM((1, spacing_x.shape[0]), F32),
            pltpu.VMEM((1, spacing_y.shape[0]), F32),
            dma((1,)),
            dma((2,)),
        ],
        compiler_params=params,
        name="x_summary",
    )(*[pltpu.with_memory_space_constraint(a, pltpu.HBM) for a in operands])
    block = shape(n1, ny, LANES)
    lines = pltpu.VMEM((n1 * ny, LANES), F32)
    ytab, shares, fine, local_out, local, outgoing[0] = pl.pallas_call(
        functools.partial(local_kernel, exy, n, ny, ct),
        out_shape=[shape(yrows, LANES), shape(4 * n2, LANES), block, shape(n1 * ny, LANES)]
        + [shape(4 * n1 + n2, LANES), shape(*outgoing[0].shape)],
        in_specs=[inside] * 4 + [anywhere],
        out_specs=[inside] * 5 + [anywhere],
        input_output_aliases={4: 5},
        scratch_shapes=[lines, lines],
        compiler_params=params,
        name="local_transform",
    )(field, xtab, pack, sums, outgoing[0])
    incoming = exx.all(outgoing)
    arrived, own, *outgoing = pl.pallas_call(
        functools.partial(second_kernel, exx, exy, n, ny, ct),
        out_shape=[shape(ARRIVED * ny, LANES), shape(2 * n2, LANES)]
        + [shape(y_rows(exy, n, s), LANES) for s in exy.steps],
        compiler_params=params,
        name="x_arrived",
    )(xown, xtab, shares, ytab, local, *incoming)
    some = pltpu.VMEM((ARRIVED * ny, LANES), F32)
    result, partial = pl.pallas_call(
        functools.partial(share_kernel, n, ny),
        out_shape=[shape(n1, 2, ny, LANES), block],
        out_specs=[anywhere, inside],
        scratch_shapes=[
            pltpu.VMEM((ny, LANES), F32),
            some,
            some,
            pltpu.VMEM((16 * n1, LANES), F32),
            dma((2,)),
        ],
        compiler_params=params,
        name="x_share",
    )(local_out.reshape(n1, ny, LANES), fine, arrived, xtab, shares, ytab)
    ranks = pl.pallas_call(
        functools.partial(rank_kernel, ny),
        out_shape=shape(8, ny, LANES),
        compiler_params=params,
        name="y_ranks",
    )(ytab)
    incoming = exy.all(outgoing)
    result = pl.pallas_call(
        functools.partial(third_kernel, exy, n, ny),
        out_shape=shape(n1, 2, ny, LANES),
        in_specs=[anywhere] + [inside] * (4 + len(incoming)),
        out_specs=anywhere,
        input_output_aliases={0: 0},
        scratch_shapes=[
            pltpu.VMEM((3 * n1 + 3 * n2, LANES), F32),
            pltpu.VMEM((n1, ny, LANES), F32),
            dma((4,)),
        ],
        compiler_params=params,
        name="y_update",
    )(result, partial, ytab, ranks, own, *incoming)
    return result.reshape(n, ny, LANES)


def solution(mesh):
    exx = Exchange("gx", mesh.shape["gx"], True)
    exy = Exchange("gy", mesh.shape["gy"], False)
    placed = (P("gx", "gy", None), P(), P())
    return jax.shard_map(
        functools.partial(on_device, exx, exy),
        mesh=mesh,
        in_specs=placed,
        out_specs=P("gx", "gy", None),
        check_vma=False,
    )
```
